32 devices in a mesh: slab: 8 (over z, x), tile: 4 (over y, core).
Axes of the slice: x: 2, y: 2, z: 4, core: 2. Of those that a mesh axis runs over, the one named last changes fastest.
Arguments:
- solution: float32 [128, 128, 256], P('tile', 'slab'), may hold values from -6 to 6
- source: float32 [128, 128, 256], P('tile', 'slab'), may hold values from 0 to 2
- phase_label: int32 [128, 128, 256], P('tile', 'slab'), may hold values from 0 to 2
- phase_diffusivity: float32 [3], replicated, may hold values from 0.1 to 2
- phase_uptake: float32 [3], replicated, may hold values from 0.2 to 1
- send_tiles: int32 [8, 4, 8, 8], P('slab', 'tile'), may hold values from 0 to 31
- support_slot: int32 [8, 4, 64], P('slab', 'tile'), may hold values from 0 to 63, each once within a row
- support_len: int32 [8, 4, 8], P('slab', 'tile'), may hold values from 1 to 8, 40 in all within a row
- coarse_ids: int32 [256], P(('slab', 'tile')), may hold values from 0 to 255, each once
- basis_values: bfloat16 [256, 8, 4096], P(('slab', 'tile')), may hold values from 0 to 0.25
- coarse_diag: float32 [256], P(('slab', 'tile')), may hold values from 320 to 480
- coarse_off: float32 [256, 26], P(('slab', 'tile')), may hold values from -12 to -4
- coarse_cols: int32 [256, 26], P(('slab', 'tile')), may hold values from 0 to 255
Outputs:
- new_solution: float32 [128, 128, 256], P('tile', 'slab')
- coarse_correction: float32 [256], P(('slab', 'tile'))
The draws below stay inside these ranges and needn't reach their ends.
Inputs may be any that keep to these rules, and one draw needn't show every extreme that they name: `support_slot`: on each device the 64 entries are the numbers 0 to 63, each once. `support_len`: on each device the lengths sum to 40, and some cell has 8. `coarse_ids`: every coarse cell appears once.
All inputs are finite; a program needn't handle non-finite values.
Results may differ from the reference program's by a relative error of at most 0.00062.
Values may be sent and summed in bfloat16 or wider, within the bound.
No kernel may reach another device: no remote copies, remote signals or barrier semaphores. Data moves between devices by JAX's collectives and lax.ppermute only.
A program may use at most 64 MiB of HBM per device.

```python
import math
import jax
import jax.numpy as jnp
import numpy as np
from jax import lax

CY = 32
NX = 256
SUPPORT = 8
NPHASE = 3
NNZ = 26
COARSE_SWEEPS = 4
SMOOTH_SWEEPS = 2
TV = 4096
CELLS = 8
CAP = 8
LIVE = 40
NY = 128
NZ = 128
NC = 256
N_SLAB = 8
N_TILE = 4


def set_ends(result, rng, low, top_value):
    dims = result.shape
    index_at = [jax.random.randint(jax.random.fold_in(rng, axis), (), 0, dims[axis]) for axis in range(len(dims))]
    result = result.at[tuple(index_at)].set(low)
    longest = dims.index(max(dims))
    index_at[longest] = (index_at[longest] + 1) % dims[longest]
    return result.at[tuple(index_at)].set(top_value)


def block_scale(stream_key, shape, split, low, top_value):
    def one(axis_at, parts):
        draws = jax.random.uniform(jax.random.fold_in(jax.random.fold_in(stream_key, 6), axis_at), (parts,), jnp.float32, low / len(split), top_value / len(split))
        return jnp.repeat(jnp.exp(draws), shape[axis_at] // parts).reshape((-1,) + (1,) * (len(shape) - axis_at - 1))

    loudness = one(*split[0])
    for cut in split[1:]:
        loudness = loudness * one(*cut)
    return loudness


def length_profile(count, total, bound, lean):
    portions = [(1 << 20) // math.isqrt(standing ** lean) + 1 for standing in range(2, count + 1)]
    surplus, holding = total - bound - (count - 1), [1] * (count - 1)
    while surplus > 0:
        free = [i for i in range(count - 1) if holding[i] < bound]
        whole, remaining = sum([portions[i] for i in free]), surplus
        for i in free:
            extra = min(bound - holding[i], max(1, remaining * portions[i] // whole), surplus)
            holding[i] = holding[i] + extra
            surplus = surplus - extra
    return np.array([bound] + holding)


def uneven(key, count, total, limit, slope):
    if count == 2:
        one = jax.random.randint(key, (), max(1, total - limit), min(limit, total - 1) + 1)
        return jnp.stack([one, total - one])
    sizes = jnp.asarray(length_profile(count, total, limit, slope), jnp.int32)
    pairs = (count - 1) // 2
    giver, receiver = sizes[1:1 + 2 * pairs:2], sizes[2:2 + 2 * pairs:2]
    room = jnp.minimum(giver - 1, limit - receiver)
    moved = jax.random.randint(jax.random.fold_in(key, 1), (pairs,), 0, 1 << 20) % (room + 1)
    sizes = sizes.at[1:1 + 2 * pairs:2].set(giver - moved).at[2:2 + 2 * pairs:2].set(receiver + moved)
    return sizes[jax.random.permutation(jax.random.fold_in(key, 2), count)]


def centred(key, dims, spread, limit, cuts=(), kind=jnp.bfloat16):
    drawn = spread * jax.random.normal(key, dims, jnp.float32)
    if cuts:
        drawn = drawn * block_scale(key, dims, cuts, -0.22, 0.18)
    return jnp.clip(drawn, -limit, limit).astype(kind)


def setup_inputs(seed: int = 0) -> dict:
    key_of = jax.random.split(jax.random.key(seed), 14)
    solution = centred(key_of[0], (NY, NZ, NX), 1.0, 6.0, ((0, 4), (1, 8)), jnp.float32)
    source = jnp.clip(2.0 * jax.random.uniform(key_of[1], (NY, NZ, NX), jnp.float32) ** block_scale(key_of[1], (NY, NZ, NX), ((0, 4), (1, 8)), -0.2, 0.2), 0.0, 2.0)
    phase_label = set_ends(jax.random.randint(key_of[2], (NY, NZ, NX), 0, NPHASE), jax.random.fold_in(key_of[2], 1), 0, NPHASE - 1).astype(jnp.int32)
    phase_diffusivity = jnp.clip(jnp.exp(jax.random.uniform(key_of[3], (NPHASE,), jnp.float32, math.log(0.1), math.log(2.0))), 0.1, 2.0)
    phase_uptake = jnp.clip(jnp.exp(jax.random.uniform(key_of[4], (NPHASE,), jnp.float32, math.log(0.2), math.log(1.0))), 0.2, 1.0)
    send_tiles = set_ends(jax.random.randint(key_of[5], (N_SLAB, N_TILE, N_SLAB, CAP), 0, CY), jax.random.fold_in(key_of[5], 1), 0, CY - 1).astype(jnp.int32)
    support_slot = jax.vmap(lambda own: jax.random.permutation(own, CELLS * SUPPORT))(jax.random.split(key_of[6], N_SLAB * N_TILE)).reshape((N_SLAB, N_TILE, CELLS * SUPPORT)).astype(jnp.int32)
    support_len = jax.vmap(lambda own: uneven(own, CELLS, LIVE, SUPPORT, 1))(jax.random.split(key_of[7], N_SLAB * N_TILE)).reshape((N_SLAB, N_TILE, CELLS)).astype(jnp.int32)
    coarse_ids = jax.random.permutation(key_of[8], NC).astype(jnp.int32)
    basis_values = jnp.clip(0.25 * jax.random.uniform(key_of[9], (NC, SUPPORT, TV), jnp.float32) ** block_scale(key_of[9], (NC, SUPPORT, TV), ((0, 32),), -0.2, 0.2), 0.0, 0.25).astype(jnp.bfloat16)
    coarse_diag = jnp.clip(jnp.exp(math.log(480.0) - 0.4054651 * jax.random.uniform(key_of[10], (NC,), jnp.float32) ** block_scale(key_of[10], (NC,), ((0, 32),), -0.2, 0.2)), 320.0, 480.0)
    coarse_off = jnp.clip(-12.0 + 8.0 * jax.random.uniform(key_of[11], (NC, NNZ), jnp.float32) ** block_scale(key_of[11], (NC, NNZ), ((0, 32),), -0.2, 0.2), -12.0, -4.0)
    coarse_cols = set_ends(jax.random.randint(key_of[12], (NC, NNZ), 0, NC), jax.random.fold_in(key_of[12], 1), 0, NC - 1).astype(jnp.int32)
    return dict(solution=solution, source=source, phase_label=phase_label, phase_diffusivity=phase_diffusivity, phase_uptake=phase_uptake, send_tiles=send_tiles, support_slot=support_slot, support_len=support_len, coarse_ids=coarse_ids, basis_values=basis_values, coarse_diag=coarse_diag, coarse_off=coarse_off, coarse_cols=coarse_cols)


OMEGA = 0.8


def neighbours(padded):
    return (padded[2:, 1:-1, 1:-1], padded[:-2, 1:-1, 1:-1], padded[1:-1, 2:, 1:-1],
            padded[1:-1, :-2, 1:-1], padded[1:-1, 1:-1, 2:], padded[1:-1, 1:-1, :-2])


def face_weights(center, padded):
    return tuple(0.5 * (center + other) for other in neighbours(padded))


def operate(values, weights, diagonal):
    beside_all = neighbours(jnp.pad(values, 1))
    coupled = weights[0] * beside_all[0]
    for number in range(1, 6):
        coupled = coupled + weights[number] * beside_all[number]
    return diagonal * values - coupled


def reference(solution, source, phase_label, phase_diffusivity, phase_uptake, send_tiles, support_slot, support_len, coarse_ids, basis_values, coarse_diag, coarse_off, coarse_cols):
    conduct = phase_diffusivity[phase_label]
    uptake = phase_uptake[phase_label]
    weights = face_weights(conduct, jnp.pad(conduct, 1))
    diagonal = uptake + weights[0] + weights[1] + weights[2] + weights[3] + weights[4] + weights[5]
    residual = source - operate(solution, weights, diagonal)
    tile_stack = residual.astype(jnp.bfloat16).reshape(NY, N_SLAB, TV)
    owners = N_SLAB * N_TILE
    slot_all = support_slot.reshape(owners, CELLS * SUPPORT)
    live_all = jnp.arange(SUPPORT)[None, None, :] < support_len.reshape(owners, CELLS)[:, :, None]
    basis_all = basis_values.reshape(owners, CELLS * SUPPORT, TV)

    def locate(owner):
        owner_slab = owner // N_TILE
        owner_tile = owner % N_TILE
        slot_list = slot_all[owner]
        source_slab = (slot_list // CAP).astype(jnp.int32)
        position = (slot_list % CAP).astype(jnp.int32)
        tile_row = (owner_tile * CY + send_tiles[source_slab, owner_tile, owner_slab, position]).astype(jnp.int32)
        return tile_row, source_slab

    def restrict(owner):
        tile_row, source_slab = locate(owner)
        pieces = tile_stack[tile_row, source_slab].astype(jnp.float32)
        products = jnp.sum(pieces * basis_all[owner].astype(jnp.float32), axis=1).reshape(CELLS, SUPPORT)
        return jnp.sum(jnp.where(live_all[owner], products, 0.0), axis=1)

    restricted = lax.map(restrict, jnp.arange(owners, dtype=jnp.int32)).reshape(NC)
    coarse_rhs = jnp.zeros((NC,), jnp.float32).at[coarse_ids].set(restricted)
    coarse_state = coarse_rhs / coarse_diag
    for repeat in range(COARSE_SWEEPS - 1):
        coarse_state = (coarse_rhs - jnp.sum(coarse_off * coarse_state[coarse_cols], axis=1)) / coarse_diag
    coarse_correction = coarse_state[coarse_ids]
    correction_all = coarse_correction.reshape(owners, CELLS)

    def deposit(accumulated, owner):
        tile_row, source_slab = locate(owner)
        scaled = correction_all[owner][:, None, None] * basis_all[owner].reshape(CELLS, SUPPORT, TV).astype(jnp.float32)
        rounded = jnp.where(live_all[owner][:, :, None], scaled, 0.0).astype(jnp.bfloat16)
        rounded = lax.optimization_barrier(rounded).astype(jnp.float32)
        accumulated = accumulated.at[tile_row, source_slab].add(rounded.reshape(CELLS * SUPPORT, TV))
        return accumulated, None

    prolonged, unused = lax.scan(deposit, jnp.zeros((NY, N_SLAB, TV), jnp.float32), jnp.arange(owners, dtype=jnp.int32))
    corrected = solution + prolonged.reshape(NY, NZ, NX)
    for repeat in range(SMOOTH_SWEEPS):
        corrected = corrected + OMEGA * (source - operate(corrected, weights, diagonal)) / diagonal
    return corrected, coarse_correction
```

```python
import functools

import jax
import jax.numpy as jnp
from jax import lax
from jax.experimental import pallas as pl
from jax.experimental.pallas import tpu as pltpu
from jax.sharding import PartitionSpec as P

COARSE_SWEEPS = 4
SMOOTH_SWEEPS = 2
OMEGA = 0.8

VMEM = pl.BlockSpec(memory_space=pltpu.VMEM)
SMEM = pl.BlockSpec(memory_space=pltpu.SMEM)
PARAMS = pltpu.CompilerParams(vmem_limit_bytes=48 * 1024 * 1024)
HALF = 64
DIAG_LANE = 60


def wheel(count, step):
    return [(i, (i + step) % count) for i in range(count)]


def extend(stack, fills):
    fill = jnp.asarray(fills, jnp.float32).reshape(-1, 1, 1, 1)
    slabs, tiles = lax.axis_size("slab"), lax.axis_size("tile")
    slab, tile = lax.axis_index("slab"), lax.axis_index("tile")
    low = lax.ppermute(stack[:, -2:], "slab", wheel(slabs, 1))
    high = lax.ppermute(stack[:, :2], "slab", wheel(slabs, -1))
    low = jnp.where(slab == 0, fill, low)
    high = jnp.where(slab == slabs - 1, fill, high)
    stack = jnp.concatenate([stack, high, low], axis=1)
    low = lax.ppermute(stack[:, :, -2:], "tile", wheel(tiles, 1))
    high = lax.ppermute(stack[:, :, :2], "tile", wheel(tiles, -1))
    low = jnp.where(tile == 0, fill, low)
    high = jnp.where(tile == tiles - 1, fill, high)
    unused = jnp.zeros(high.shape[:2] + (4,) + high.shape[3:], jnp.float32)
    return jnp.concatenate([stack, high, unused, low], axis=2)


def in_plane(plane):
    rows, width = plane.shape
    lane = lax.broadcasted_iota(jnp.int32, plane.shape, 1)
    left = jnp.where(lane == 0, 0.0, pltpu.roll(plane, 1, 1))
    right = jnp.where(lane == width - 1, 0.0, pltpu.roll(plane, width - 1, 1))
    return left + right + pltpu.roll(plane, 1, 0) + pltpu.roll(plane, rows - 1, 0)


def around(z, planes):
    above = jnp.where(z == planes - 1, 0, z + 1)
    below = jnp.where(z == 0, planes - 1, z - 1)
    return above, below


def sort_kernel(slot_ref, len_ref, ids_ref, basis_ref, out_ref):
    entries, voxels = basis_ref.shape
    cells = len_ref.shape[0]
    support = entries // cells
    lane = lax.broadcasted_iota(jnp.int32, (1, entries), 1)
    length = jnp.zeros((1, entries), jnp.int32)
    ident = jnp.zeros((1, entries), jnp.int32)
    for cell in range(cells):
        here = lane // support == cell
        length = jnp.where(here, len_ref[cell], length)
        ident = jnp.where(here, ids_ref[cell], ident)
    live = lane % support < length
    slot = jnp.where(live, slot_ref[...], -1)
    hit = slot == lax.broadcasted_iota(jnp.int32, (entries, entries), 0)
    pick = jnp.where(hit, 1.0, 0.0).astype(jnp.bfloat16)
    step = 512
    for start in range(0, voxels, step):
        out_ref[:, start : start + step] = jnp.dot(
            pick, basis_ref[:, start : start + step], preferred_element_type=jnp.float32
        ).astype(jnp.bfloat16)
    low = jnp.sum(jnp.where(hit, ident % 256, 0).astype(jnp.float32), axis=1, keepdims=True)
    high = jnp.sum(jnp.where(hit, ident // 256, 0).astype(jnp.float32), axis=1, keepdims=True)
    extra = lax.broadcasted_iota(jnp.int32, (entries, out_ref.shape[1] - voxels), 1)
    out_ref[:, voxels:] = jnp.where(extra == 0, low, jnp.where(extra == 1, high, 0.0)).astype(
        jnp.bfloat16
    )


def residual_kernel(diff_ref, upt_ref, ext_ref, res_ref, conduct_ref, scale_ref):
    unused, planes, rows, width = ext_ref.shape
    depth, own, unused = res_ref.shape
    phases = diff_ref.shape[0]

    def fill(z, carry):
        label = ext_ref[1, z]
        conduct = jnp.zeros(label.shape, jnp.float32)
        for phase in range(phases):
            conduct = jnp.where(label == float(phase), diff_ref[phase], conduct)
        conduct_ref[z] = conduct
        return carry

    lax.fori_loop(0, planes, fill, 0)

    def step(z, carry):
        above, below = around(z, planes)
        label, conduct = ext_ref[1, z], conduct_ref[z]
        uptake = jnp.zeros(label.shape, jnp.float32)
        for phase in range(phases):
            uptake = jnp.where(label == float(phase), upt_ref[phase], uptake)
        c_up, c_down = conduct_ref[above], conduct_ref[below]
        diagonal = uptake + 0.5 * (6.0 * conduct + (in_plane(conduct) + c_up + c_down))
        inside = conduct > 0.0
        scale_ref[z] = jnp.where(inside, OMEGA / jnp.where(inside, diagonal, 1.0), 0.0)

        @pl.when(z < depth)
        def _():
            v, v_up, v_down = ext_ref[0, z], ext_ref[0, above], ext_ref[0, below]
            near = in_plane(v) + v_up + v_down
            flow = in_plane(conduct * v) + c_up * v_up + c_down * v_down
            residual = ext_ref[2, z] - (diagonal * v - 0.5 * (conduct * near + flow))
            res_ref[z] = residual[:own].astype(jnp.bfloat16)

        return carry

    lax.fori_loop(0, planes, step, 0)


def owner_of(basis_ref, voxels):
    tail = basis_ref[:, voxels:].astype(jnp.float32)
    return (tail[:, 0:1] + 256.0 * tail[:, 1:2]).astype(jnp.int32)


def restrict_kernel(row_ref, record_ref, res_ref, basis_ref, out_ref):
    depth, own, width = res_ref.shape
    entries = basis_ref.shape[0]
    pick = jnp.where(
        row_ref[...] == lax.broadcasted_iota(jnp.int32, (entries, own), 1), 1.0, 0.0
    ).astype(jnp.bfloat16)
    total = jnp.zeros((entries, width), jnp.float32)
    for z in range(depth):
        piece = jnp.dot(pick, res_ref[z], preferred_element_type=jnp.float32)
        total = total + piece * basis_ref[:, z * width : (z + 1) * width].astype(jnp.float32)
    product = jnp.sum(total, axis=1, keepdims=True)
    ident = owner_of(basis_ref, depth * width)
    copies, lines, lanes = out_ref.shape
    lane = lax.broadcasted_iota(jnp.int32, (entries, lanes), 1)
    line = lax.broadcasted_iota(jnp.int32, (8, lanes), 0)
    for base in range(0, lines, 8):
        block = record_ref[...] if base == 0 else jnp.zeros((8, lanes), jnp.float32)
        for row in range(8):
            share = jnp.where(ident == (base + row) * HALF + lane - HALF, product, 0.0)
            share = jnp.sum(jnp.where(lane >= HALF, share, 0.0), axis=0, keepdims=True)
            block = jnp.where((line == row) & (lane[:8] >= HALF), share, block)

        def put(copy, carry):
            out_ref[copy, base : base + 8, :] = block
            return carry

        lax.fori_loop(0, copies, put, 0, unroll=8)


def solve(got_ref, matrix_ref, count, nnz):
    devices, lines, lanes = got_ref.shape
    column_id = lax.broadcasted_iota(jnp.int32, (8, count), 1)

    def build(device, carry):
        record = got_ref[device, 0:8, :]
        where_to = record.astype(jnp.int32)
        row = jnp.zeros((8, count), jnp.float32)
        for entry in range(nnz):
            hit = where_to[:, 32 + entry : 33 + entry] == column_id
            row = row + jnp.where(hit, record[:, entry : entry + 1], 0.0)
        matrix_ref[pl.ds(device * 8, 8), :] = row
        return carry

    lax.fori_loop(0, devices, build, 0, unroll=2)
    summed = lax.fori_loop(
        1, devices, lambda device, total: total + got_ref[device], got_ref[0], unroll=4
    )
    rhs = jnp.concatenate([summed[line : line + 1, HALF:] for line in range(count // HALF)], axis=1)
    rhs_column, diag_column = [], []
    for device in range(devices):
        eye = column_id == device * 8 + lax.broadcasted_iota(jnp.int32, (8, count), 0)
        rhs_column.append(jnp.sum(jnp.where(eye, rhs, 0.0), axis=1, keepdims=True))
        diag_column.append(got_ref[device, 0:8, DIAG_LANE : DIAG_LANE + 1])

    def to_row(columns):
        total = jnp.zeros((8, count), jnp.float32)
        for device in range(devices):
            eye = column_id == device * 8 + lax.broadcasted_iota(jnp.int32, (8, count), 0)
            total = total + jnp.where(eye, columns[device], 0.0)
        return jnp.sum(total, axis=0, keepdims=True)

    state = to_row([rhs_column[d] / diag_column[d] for d in range(devices)])
    for repeat in range(COARSE_SWEEPS - 1):
        columns = []
        for d in range(devices):
            product = jnp.sum(matrix_ref[d * 8 : d * 8 + 8, :] * state, axis=1, keepdims=True)
            columns.append((rhs_column[d] - product) / diag_column[d])
        state = to_row(columns)
    return state


def prolong_kernel(nnz, ids_ref, row_ref, got_ref, basis_ref, sol_ref, cor_ref, out_ref, matrix_ref):
    depth, own, width = cor_ref.shape
    entries = basis_ref.shape[0]
    count = matrix_ref.shape[0]
    state = solve(got_ref, matrix_ref, count, nnz)
    cells = ids_ref.shape[0]
    line = lax.broadcasted_iota(jnp.int32, (cells, count), 0)
    mine = jnp.zeros((cells, count), jnp.int32)
    for cell in range(cells):
        mine = jnp.where(line == cell, ids_ref[cell], mine)
    hit = mine == lax.broadcasted_iota(jnp.int32, (cells, count), 1)
    out_ref[...] = jnp.sum(jnp.where(hit, state, 0.0), axis=1, keepdims=True)
    ident = owner_of(basis_ref, depth * width)
    hit = ident == lax.broadcasted_iota(jnp.int32, (entries, count), 1)
    factor = jnp.sum(jnp.where(hit, state, 0.0), axis=1, keepdims=True)
    pick = jnp.where(
        row_ref[...] == lax.broadcasted_iota(jnp.int32, (own, entries), 0), 1.0, 0.0
    ).astype(jnp.bfloat16)
    for z in range(depth):
        part = basis_ref[:, z * width : (z + 1) * width].astype(jnp.float32) * factor
        added = jnp.dot(pick, part.astype(jnp.bfloat16), preferred_element_type=jnp.float32)
        cor_ref[z] = sol_ref[z] + added


def smooth_kernel(ext_ref, conduct_ref, scale_ref, src_ref, out_ref, mid_ref):
    planes, rows, width = ext_ref.shape
    depth, own, unused = out_ref.shape

    def sweep(v_ref, z):
        above, below = around(z, planes)
        conduct = conduct_ref[z]
        v, v_up, v_down = v_ref[z], v_ref[above], v_ref[below]
        near = in_plane(v) + v_up + v_down
        flow = in_plane(conduct * v) + conduct_ref[above] * v_up + conduct_ref[below] * v_down
        return (1.0 - OMEGA) * v + scale_ref[z] * (src_ref[0, z] + 0.5 * (conduct * near + flow))

    def first(step, carry):
        z = jnp.where(step == depth + 1, planes - 1, step)
        mid_ref[z] = sweep(ext_ref, z)
        return carry

    def second(z, carry):
        out_ref[z] = sweep(mid_ref, z)[:own]
        return carry

    lax.fori_loop(0, depth + 2, first, 0)
    lax.fori_loop(0, depth, second, 0)


def shards(
    solution,
    source,
    phase_label,
    phase_diffusivity,
    phase_uptake,
    send_tiles,
    support_slot,
    support_len,
    coarse_ids,
    basis_values,
    coarse_diag,
    coarse_off,
    coarse_cols,
):
    f32, bf16 = jnp.float32, jnp.bfloat16
    rows, depth, width = solution.shape
    voxels = depth * width
    slabs, tiles = lax.axis_size("slab"), lax.axis_size("tile")
    devices = slabs * tiles
    capacity = send_tiles.shape[3]
    cells, support, unused = basis_values.shape
    entries = cells * support
    count = cells * devices
    nnz = coarse_off.shape[1]
    shape = jax.ShapeDtypeStruct

    wide = voxels + 128
    outgoing = pl.pallas_call(
        sort_kernel,
        out_shape=shape((entries, wide), bf16),
        in_specs=[VMEM, SMEM, SMEM, VMEM],
        out_specs=VMEM,
        compiler_params=PARAMS,
        name="sort_basis",
    )(
        support_slot.reshape(1, entries),
        support_len.reshape(cells),
        coarse_ids,
        basis_values.reshape(entries, voxels),
    )
    basis = lax.all_to_all(
        outgoing.reshape(slabs, capacity, wide), "slab", split_axis=0, concat_axis=0, tiled=True
    ).reshape(entries, wide)

    stack = jnp.stack([solution, phase_label.astype(f32), source]).transpose(0, 2, 1, 3)
    ext = extend(stack, (0.0, -1.0, 0.0))
    planes, tall = ext.shape[1:3]
    residual, conduct, scale = pl.pallas_call(
        residual_kernel,
        out_shape=(
            shape((depth, rows, width), bf16),
            shape((planes, tall, width), f32),
            shape((planes, tall, width), f32),
        ),
        in_specs=[SMEM, SMEM, VMEM],
        out_specs=(VMEM, VMEM, VMEM),
        compiler_params=PARAMS,
        name="residual",
    )(phase_diffusivity, phase_uptake, ext)

    record = jnp.concatenate(
        [
            coarse_off,
            jnp.zeros((cells, 32 - nnz), f32),
            coarse_cols.astype(f32),
            jnp.zeros((cells, DIAG_LANE - 32 - nnz), f32),
            coarse_diag[:, None],
            jnp.zeros((cells, 128 - DIAG_LANE - 1), f32),
        ],
        axis=1,
    )
    lines = max(8, count // HALF)
    row_of = send_tiles.reshape(entries)
    payload = pl.pallas_call(
        restrict_kernel,
        out_shape=shape((devices, lines, 128), f32),
        in_specs=[VMEM, VMEM, VMEM, VMEM],
        out_specs=VMEM,
        compiler_params=PARAMS,
        name="restrict",
    )(row_of[:, None], record, residual, basis)
    got = lax.all_to_all(payload, ("slab", "tile"), split_axis=0, concat_axis=0, tiled=True)

    corrected, coarse_correction = pl.pallas_call(
        functools.partial(prolong_kernel, nnz),
        out_shape=(shape((depth, rows, width), f32), shape((cells, 1), f32)),
        in_specs=[SMEM, VMEM, VMEM, VMEM, VMEM],
        out_specs=(VMEM, VMEM),
        scratch_shapes=[pltpu.VMEM((count, count), f32)],
        compiler_params=PARAMS,
        name="solve_prolong",
    )(coarse_ids, row_of[None, :], got, basis, stack[0])

    cor_ext = extend(corrected[None], (0.0,))[0]
    smooth = pl.pallas_call(
        smooth_kernel,
        out_shape=shape((depth, rows, width), f32),
        in_specs=[VMEM, VMEM, VMEM, VMEM],
        out_specs=VMEM,
        scratch_shapes=[pltpu.VMEM((planes, tall, width), f32)],
        compiler_params=PARAMS,
        name="smooth",
    )(cor_ext, conduct, scale, ext[2:3])
    return smooth.transpose(1, 0, 2), coarse_correction.reshape(cells)


def solution(mesh):
    placed = (
        P("tile", "slab", None),
        P("tile", "slab", None),
        P("tile", "slab", None),
        P(),
        P(),
        P("slab", "tile", None, None),
        P("slab", "tile", None),
        P("slab", "tile", None),
        P(("slab", "tile")),
        P(("slab", "tile"), None, None),
        P(("slab", "tile")),
        P(("slab", "tile"), None),
        P(("slab", "tile"), None),
    )
    return jax.shard_map(
        shards,
        mesh=mesh,
        in_specs=placed,
        out_specs=(P("tile", "slab", None), P(("slab", "tile"))),
        check_vma=False,
    )
```

```python
import functools

import jax
import jax.numpy as jnp
from jax import lax
from jax.experimental import pallas as pl
from jax.experimental.pallas import tpu as pltpu
from jax.sharding import PartitionSpec as P

COARSE_SWEEPS = 4
SMOOTH_SWEEPS = 2
OMEGA = 0.8

VMEM = pl.BlockSpec(memory_space=pltpu.VMEM)
SMEM = pl.BlockSpec(memory_space=pltpu.SMEM)
HBM = pl.BlockSpec(memory_space=pltpu.HBM)
MIB = 1024 * 1024
COLS_LANE = 32
HALF = 64
DIAG_LANE = 60


def params(mib=16):
    return pltpu.CompilerParams(vmem_limit_bytes=mib * MIB)


def wheel(count, step):
    return [(i, (i + step) % count) for i in range(count)]


def pairs(count, odd):
    start = 1 if odd else 0
    table = list(range(count))
    for i in range(start, count - 1, 2):
        table[i], table[i + 1] = i + 1, i
    return list(enumerate(table))


def fetch(pairs_of_refs, sems):
    copies = [
        pltpu.make_async_copy(source, target, sems.at[k])
        for k, (source, target) in enumerate(pairs_of_refs)
    ]
    for copy in copies:
        copy.start()
    return copies


def prepare_kernel(
    slot_hbm, len_hbm, ids_hbm, basis_hbm, sol_hbm, label_hbm, src_hbm, table_hbm,
    out_hbm, even_ref, odd_ref, late_even_ref, late_odd_ref, top_ref, bottom_ref,
    slot_ref, len_ref, ids_ref, basis_ref, sol_ref, label_ref, src_ref, table_ref, out_ref, sems, *, capacity
):
    entries, voxels = basis_ref.shape
    rows, depth, width = sol_ref.shape
    cells = len_ref.shape[0]
    support = entries // cells
    border = (out_ref.shape[1] - 128 - voxels) // 2
    chunk, half = voxels // 4, depth // 2
    pieces = [
        (basis_hbm.at[:, pl.ds(k * chunk, chunk)], basis_ref.at[:, pl.ds(k * chunk, chunk)]) for k in range(4)
    ]
    blocks = [
        (hbm.at[:, pl.ds(start, half)], ref.at[:, pl.ds(start, half)])
        for hbm, ref in ((sol_hbm, sol_ref), (label_hbm, label_ref), (src_hbm, src_ref))
        for start in (0, half)
    ]
    small = [(slot_hbm, slot_ref), (len_hbm, len_ref), (ids_hbm, ids_ref), (table_hbm, table_ref)]
    copies = fetch(small + pieces + blocks, sems)
    for copy in copies[:4]:
        copy.wait()
    lane = lax.broadcasted_iota(jnp.int32, (1, entries), 1)
    length = jnp.zeros((1, entries), jnp.int32)
    ident = jnp.zeros((1, entries), jnp.int32)
    for cell in range(cells):
        here = lane // support == cell
        length = jnp.where(here, len_ref[cell], length)
        ident = jnp.where(here, ids_ref[cell], ident)
    live = lane % support < length
    slot = jnp.where(live, slot_ref[...], -1)
    row = lax.broadcasted_iota(jnp.int32, (entries, entries), 0)
    above = jnp.where(row >= entries - capacity, row + capacity - entries, row + capacity)
    below = jnp.where(row < capacity, row - capacity + entries, row - capacity)
    hits = [slot == row, slot == above, slot == below]
    picks = [jnp.where(hit, 1.0, 0.0).astype(jnp.bfloat16) for hit in hits]
    sent = []

    def move(pick, start, size, target):
        out_ref[:, target : target + size] = jnp.dot(
            pick, basis_ref[:, start : start + size], preferred_element_type=jnp.float32
        ).astype(jnp.bfloat16)

    def send(start, size):
        part = pl.ds(start, size)
        copy = pltpu.make_async_copy(out_ref.at[:, part], out_hbm.at[:, part], sems.at[len(copies) + len(sent)])
        copy.start()
        sent.append(copy)

    extra = lax.broadcasted_iota(jnp.int32, (entries, 128), 1)
    tail = jnp.zeros((entries, 128), jnp.float32)
    for k, hit in enumerate(hits):
        low = jnp.sum(jnp.where(hit, ident % 256, 0).astype(jnp.float32), axis=1, keepdims=True)
        high = jnp.sum(jnp.where(hit, ident // 256, 0).astype(jnp.float32), axis=1, keepdims=True)
        tail = jnp.where(extra == 2 * k, low, jnp.where(extra == 2 * k + 1, high, tail))
    out_ref[:, voxels + 2 * border :] = tail.astype(jnp.bfloat16)
    for k in range(4):
        copies[4 + k].wait()
        for start in range(k * chunk, (k + 1) * chunk, 512):
            move(picks[0], start, 512, start)
        send(k * chunk, chunk)
        if k == 0:
            move(picks[1], 0, border, voxels)
    move(picks[2], voxels - border, border, voxels + border)
    send(voxels, 2 * border + 128)

    slots = table_ref.shape[0]
    odd = lax.axis_index("slab") % 2 == 1
    for ref in (even_ref, odd_ref):
        ref[rows + 8 :] = jnp.zeros((ref.shape[0] - rows - 8, width), jnp.float32)
        ref[rows + 8 : rows + 8 + slots, :capacity] = table_ref[...].astype(jnp.float32)
    for copy in copies[8:]:
        copy.wait()

    def planes(start):
        parts = [ref[:, start : start + 2, :].astype(jnp.float32) for ref in (sol_ref, label_ref, src_ref, src_ref)]
        block = jnp.transpose(jnp.concatenate(parts, axis=1), (1, 0, 2))
        return [block[k] for k in range(6)]

    near, far, label, label_far, origin, unused = planes(0)
    down = near, pack_labels(label, label_far), far, origin
    far, near, label_far, label, unused, origin = planes(depth - 2)
    up = near, pack_labels(label, label_far), far, origin
    for first, second, early, late in ((up, down, even_ref, late_even_ref), (down, up, odd_ref, late_odd_ref)):
        mine = [jnp.where(odd, b, a) for a, b in zip(first, second)]
        early[:rows] = mine[0]
        early[rows : rows + 8] = mine[1]
        late[:rows] = mine[2]
        late[rows:] = mine[3]
    for ref, near, far in ((top_ref, 0, 1), (bottom_ref, rows - 1, rows - 2)):
        ref[0, :depth] = sol_ref[near]
        ref[1, :depth] = (label_ref[near] + 3 * label_ref[far]).astype(jnp.float32)
        ref[2, :depth] = src_ref[near]
        for k in range(3):
            ref[k, depth:] = jnp.zeros((ref.shape[1] - depth, width), jnp.float32)
    for copy in sent:
        copy.wait()


def pack_labels(near, far):
    pair = near + 3.0 * far
    packed = pair[0:8]
    for k in range(1, pair.shape[0] // 8):
        packed = packed + float(9**k) * pair[8 * k : 8 * k + 8]
    return packed


def unpack_labels(packed, rows):
    found = []
    for k in range(rows // 8):
        rest = jnp.floor((packed + 0.5) * (1.0 / 9.0))
        found.append(packed - 9.0 * rest)
        packed = rest
    return part_pair(jnp.concatenate(found, axis=0))


def part_pair(pair):
    far = jnp.floor((pair + 0.5) * (1.0 / 3.0))
    return pair - 3.0 * far, far


def halo_labels(even_ref, odd_ref, own):
    swap = lax.axis_index("slab") % 2 == 1
    even, odd = even_ref[own : own + 8], odd_ref[own : own + 8]
    near_high, far_high = unpack_labels(jnp.where(swap, odd, even), own)
    near_low, far_low = unpack_labels(jnp.where(swap, even, odd), own)
    return near_high, far_high, far_low, near_low


def edge_kernel(top_in, bottom_in, even_in, odd_in, top_ref, bottom_ref, even_ref, odd_ref, sems, *, own, depth):
    moves = [(top_in, top_ref), (bottom_in, bottom_ref), (even_in, even_ref), (odd_in, odd_ref)]
    for copy in fetch(moves, sems):
        copy.wait()
    for k, label in enumerate(halo_labels(even_ref, odd_ref, own)):
        z = depth + k
        top_ref[1, z : z + 1] = label[0:1] + 3.0 * label[1:2]
        bottom_ref[1, z : z + 1] = label[own - 1 :] + 3.0 * label[own - 2 : own - 1]


def collect(diag_ref, off_ref, cols_ref, table_ref, even_ref, odd_ref, tables_ref, column_ref, record_ref, own):
    slots, capacity = table_ref.shape
    cells, nnz = off_ref.shape
    line = lax.broadcasted_iota(jnp.int32, record_ref.shape, 0)
    record = jnp.zeros(record_ref.shape, jnp.float32)
    for cell in range(cells):
        record = jnp.where(line == cell, diag_ref[cell], record)
    record_ref[...] = record
    record_ref[:, :nnz] = off_ref[...]
    record_ref[:, COLS_LANE : COLS_LANE + nnz] = cols_ref[...].astype(jnp.float32)
    swap = lax.axis_index("slab") % 2 == 1
    even = even_ref[own + 8 : own + 8 + slots, :capacity]
    odd = odd_ref[own + 8 : own + 8 + slots, :capacity]

    def flat(table):
        return jnp.concatenate([table[at : at + 1] for at in range(slots)], axis=1)

    tables_ref[...] = jnp.zeros(tables_ref.shape, jnp.int32)
    tables_ref[0:1] = flat(table_ref[...])
    tables_ref[1:2] = flat(jnp.where(swap, odd, even).astype(jnp.int32))
    tables_ref[2:3] = flat(jnp.where(swap, even, odd).astype(jnp.int32))
    column_ref[...] = jnp.transpose(tables_ref[...].astype(jnp.float32)).astype(jnp.int32)


def beside(plane, lane):
    rows, width = plane.shape
    left = jnp.where(lane == 0, 0.0, pltpu.roll(plane, 1, 1))
    right = jnp.where(lane == width - 1, 0.0, pltpu.roll(plane, width - 1, 1))
    return left + right + pltpu.roll(plane, 1, 0) + pltpu.roll(plane, rows - 1, 0)


class Grid:
    def __init__(self, diff_ref, upt_ref, labels, even_ref, odd_ref, top_ref, bottom_ref, conduct_ref, uptake_ref):
        self.conduct_ref, self.uptake_ref = conduct_ref, uptake_ref
        depth = len(labels)
        own, width = labels[0].shape
        planes, rows = conduct_ref.shape[0:2]
        phases = diff_ref.shape[0]
        row = lax.broadcasted_iota(jnp.int32, (rows, width), 0)
        self.lane = lax.broadcasted_iota(jnp.int32, (rows, width), 1)
        slab, tile = lax.axis_index("slab"), lax.axis_index("tile")
        tile_first, tile_last = tile == 0, tile == lax.axis_size("tile") - 1
        slab_first, slab_last = slab == 0, slab == lax.axis_size("slab") - 1
        beyond = (row >= own + 2) & (row < rows - 2)
        beyond = beyond | ((row >= own) & (row < own + 4) & tile_last)
        beyond = beyond | ((row >= own + 4) & tile_first)
        blank = jnp.zeros((8, width), jnp.float32)

        def look(z, label, outside):
            conduct_ref[z, :own] = label
            conduct_ref[z, own:] = blank
            near, far = part_pair(top_ref[1, z : z + 1])
            conduct_ref[z, own : own + 1] = near
            conduct_ref[z, own + 1 : own + 2] = far
            near, far = part_pair(bottom_ref[1, z : z + 1])
            conduct_ref[z, rows - 1 :] = near
            conduct_ref[z, rows - 2 : rows - 1] = far
            label = jnp.where(outside, -1.0, conduct_ref[z])
            conduct = jnp.zeros(label.shape, jnp.float32)
            uptake = jnp.zeros(label.shape, jnp.float32)
            for phase in range(phases):
                conduct = jnp.where(label == float(phase), diff_ref[phase], conduct)
                uptake = jnp.where(label == float(phase), upt_ref[phase], uptake)
            conduct_ref[z] = conduct
            uptake_ref[z] = uptake

        for z, label in enumerate(labels):
            look(z, label, beyond)
        for k, label in enumerate(halo_labels(even_ref, odd_ref, own)):
            look(depth + k, label, beyond | (slab_last if k < 2 else slab_first))

    def around(self, z):
        rows, width = self.conduct_ref.shape[1:]
        planes = self.conduct_ref.shape[0]
        plane = self.conduct_ref[z]
        return (
            jnp.where(self.lane == 0, 0.0, pltpu.roll(plane, 1, 1)),
            jnp.where(self.lane == width - 1, 0.0, pltpu.roll(plane, width - 1, 1)),
            pltpu.roll(plane, 1, 0),
            pltpu.roll(plane, rows - 1, 0),
            self.conduct_ref[(z - 1) % planes],
            self.conduct_ref[(z + 1) % planes],
        )

    def diagonal(self, z, near):
        return self.uptake_ref[z] + 3.0 * self.conduct_ref[z] + 0.5 * sum(near[1:], near[0])


def residual_kernel(*refs):
    operands, outputs, scratch = refs[:13], refs[13:19], refs[19:]
    conduct_ref, uptake_ref, sol_ref = scratch[:3]
    local, sems = scratch[3:16], scratch[16]
    diff_ref, upt_ref, diag_ref, off_ref, cols_ref, table_ref, sol_in, label_in, src_in = local[:9]
    even_ref, odd_ref, top_ref, bottom_ref = local[9:]
    res_ref, plain_ref, packed_ref, tables_ref, column_ref, record_ref = outputs
    for copy in fetch(list(zip(operands, local)), sems):
        copy.wait()
    own, depth, width = sol_in.shape
    planes, rows = conduct_ref.shape[0:2]
    collect(diag_ref, off_ref, cols_ref, table_ref, even_ref, odd_ref, tables_ref, column_ref, record_ref, own)
    labels = []
    for start in range(0, depth, 8):
        block = jnp.transpose(label_in[:, start : start + 8, :].astype(jnp.float32), (1, 0, 2))
        labels = labels + [block[at] for at in range(8)]
    for k in range(depth // 2):
        packed_ref[k] = pack_labels(labels[2 * k], labels[2 * k + 1])
    grid = Grid(diff_ref, upt_ref, labels, even_ref, odd_ref, top_ref, bottom_ref, conduct_ref, uptake_ref)
    lane = grid.lane
    blank = jnp.zeros((8, width), jnp.float32)
    swap = lax.axis_index("slab") % 2 == 1
    even, odd = even_ref[:own], odd_ref[:own]
    sources = []

    def settle(z, value):
        sol_ref[z, :own] = value
        sol_ref[z, own:] = blank
        if z < depth:
            sol_ref[z, own : own + 1] = top_ref[0, z : z + 1]
            sol_ref[z, rows - 1 :] = bottom_ref[0, z : z + 1]
        sol_ref[z] = jnp.where(conduct_ref[z] > 0.0, sol_ref[z], 0.0)

    for start in range(0, depth, 8):
        block = jnp.transpose(sol_in[:, start : start + 8, :], (1, 0, 2))
        for at in range(8):
            plain_ref[start + at] = block[at]
            settle(start + at, block[at])
    settle(depth, jnp.where(swap, odd, even))
    settle(planes - 1, jnp.where(swap, even, odd))
    for start in range(0, depth, 8):
        block = jnp.transpose(src_in[:, start : start + 8, :], (1, 0, 2))
        for at in range(8):
            z = start + at
            above, below = z + 1, (z - 1) % planes
            conduct, value, up, down = conduct_ref[z], sol_ref[z], sol_ref[above], sol_ref[below]
            diagonal = grid.diagonal(z, grid.around(z))
            near = beside(value, lane) + up + down
            flow = beside(conduct * value, lane) + conduct_ref[above] * up + conduct_ref[below] * down
            applied = diagonal * value - 0.5 * (conduct * near + flow)
            res_ref[z] = (block[at] - applied[:own]).astype(jnp.bfloat16)


def weigh_kernel(
    diff_ref, upt_ref, packed_ref, src_in, even_ref, odd_ref, top_ref, bottom_ref, late_even_ref, late_odd_ref,
    weight_ref, conduct_ref, uptake_ref,
):
    own, depth, width = src_in.shape
    planes, rows = conduct_ref.shape[0:2]
    labels = []
    for k in range(depth // 2):
        labels = labels + list(unpack_labels(packed_ref[k], own))
    grid = Grid(diff_ref, upt_ref, labels, even_ref, odd_ref, top_ref, bottom_ref, conduct_ref, uptake_ref)
    blank = jnp.zeros((8, width), jnp.float32)
    swap = lax.axis_index("slab") % 2 == 1
    late = late_even_ref[own:], late_odd_ref[own:]
    outer = {depth: jnp.where(swap, late[1], late[0]), planes - 1: jnp.where(swap, late[0], late[1])}
    for start in (0, 8, planes - 1, depth):
        if start < depth:
            block = jnp.transpose(src_in[:, start : start + 8, :], (1, 0, 2))
            sources = {start + at: block[at] for at in range(8)}
        else:
            sources = {start: outer[start]}
        for z, source in sources.items():
            conduct = conduct_ref[z]
            near = grid.around(z)
            inside = conduct > 0.0
            scale = jnp.where(inside, OMEGA / jnp.where(inside, grid.diagonal(z, near), 1.0), 0.0)
            for k, other in enumerate(near):
                weight_ref[k, z] = jnp.where(other > 0.0, 0.5 * scale * (conduct + other), 0.0)
            weight_ref[6, z, :own] = scale[:own] * source
            weight_ref[6, z, own:] = blank
            if z < depth:
                weight_ref[6, z, own : own + 1] = scale[own : own + 1] * top_ref[2, z : z + 1]
                weight_ref[6, z, rows - 1 :] = scale[rows - 1 :] * bottom_ref[2, z : z + 1]


def owners_of(basis_ref, base):
    tail = basis_ref[:, base:].astype(jnp.float32)
    return [
        (tail[:, 2 * k : 2 * k + 1] + 256.0 * tail[:, 2 * k + 1 : 2 * k + 2]).astype(jnp.int32)
        for k in range(3)
    ]


def restrict_kernel(column_ref, record_ref, res_ref, basis_ref, out_ref):
    depth, own, width = res_ref.shape
    entries = basis_ref.shape[0]
    pick = column_ref[:, 0:1] == lax.broadcasted_iota(jnp.int32, (entries, own), 1)
    pick = jnp.where(pick, 1.0, 0.0).astype(jnp.bfloat16)
    total = jnp.zeros((entries, width), jnp.float32)
    for z in range(depth):
        piece = jnp.dot(pick, res_ref[z], preferred_element_type=jnp.float32)
        total = total + piece * basis_ref[:, z * width : (z + 1) * width].astype(jnp.float32)
    product = jnp.sum(total, axis=1, keepdims=True)
    ident = owners_of(basis_ref, basis_ref.shape[1] - 128)[0]
    copies, lines, lanes = out_ref.shape
    lane = lax.broadcasted_iota(jnp.int32, (entries, lanes), 1)
    line = lax.broadcasted_iota(jnp.int32, (8, lanes), 0)
    for base in range(0, lines, 8):
        block = record_ref[...] if base == 0 else jnp.zeros((8, lanes), jnp.float32)
        for row in range(8):
            share = jnp.where(ident == (base + row) * HALF + lane - HALF, product, 0.0)
            share = jnp.sum(jnp.where(lane >= HALF, share, 0.0), axis=0, keepdims=True)
            block = jnp.where((line == row) & (lane[:8] >= HALF), share, block)

        def put(copy, carry):
            out_ref[copy, base : base + 8, :] = block
            return carry

        lax.fori_loop(0, copies, put, 0, unroll=8)


def solve(got_ref, count, nnz):
    devices, lines, lanes = got_ref.shape
    summed = got_ref[0]
    if devices <= 64:
        for device in range(1, devices):
            summed = summed + got_ref[device]
    else:
        summed = lax.fori_loop(1, devices, lambda d, total: total + got_ref[d], summed)
    rhs = jnp.concatenate([summed[at : at + 1, HALF:] for at in range(count // HALF)], axis=1)
    record = jnp.transpose(got_ref[:, 0:8, :].reshape(count, lanes))
    line = lax.broadcasted_iota(jnp.int32, (COLS_LANE, lanes), 0)
    inverse = 1.0 / record[DIAG_LANE : DIAG_LANE + 1]
    chunks = range(0, count, lanes)
    values = [jnp.where(line < nnz, record[:COLS_LANE, at : at + lanes], 0.0) for at in chunks]
    places = [
        jnp.where(line < nnz, record[COLS_LANE : 2 * COLS_LANE, at : at + lanes], 0.0).astype(jnp.int32)
        for at in chunks
    ]
    state = rhs * inverse
    for repeat in range(COARSE_SWEEPS - 1):
        sources = [jnp.broadcast_to(state[:, at : at + lanes], (COLS_LANE, lanes)) for at in chunks]
        pulled = []
        for value, place in zip(values, places):
            found = jnp.zeros((COLS_LANE, lanes), jnp.float32)
            for k, source in enumerate(sources):
                taken = jnp.take_along_axis(source, place % lanes, axis=1, mode="promise_in_bounds")
                found = jnp.where(place // lanes == k, taken, found)
            pulled.append(jnp.sum(value * found, axis=0, keepdims=True))
        state = (rhs - jnp.concatenate(pulled, axis=1)) * inverse
    return state


def prolong_kernel(
    ids_ref, tables_ref, even_ref, odd_ref, late_even_ref, late_odd_ref, got_ref, basis_ref, plain_ref, cor_ref, top_ref, bottom_ref,
    correction_ref, *, nnz, depth,
):
    planes, own, width = cor_ref.shape
    entries = tables_ref.shape[1]
    cells = ids_ref.shape[0]
    count = cells * got_ref.shape[0]
    state = solve(got_ref, count, nnz)

    line = lax.broadcasted_iota(jnp.int32, (cells, 1), 0)
    mine = jnp.zeros((cells, 1), jnp.int32)
    for cell in range(cells):
        mine = jnp.where(line == cell, ids_ref[cell], mine)

    def look_up(ident):
        hit = ident == lax.broadcasted_iota(jnp.int32, (ident.shape[0], count), 1)
        return jnp.sum(jnp.where(hit, state, 0.0), axis=1, keepdims=True)

    diagonal = line == lax.broadcasted_iota(jnp.int32, (cells, cells), 1)
    correction_ref[...] = jnp.sum(jnp.where(diagonal, look_up(mine), 0.0), axis=0, keepdims=True)
    swap = lax.axis_index("slab") % 2 == 1
    early = even_ref[:own], odd_ref[:own]
    late = late_even_ref[:own], late_odd_ref[:own]
    wide = {
        depth: jnp.where(swap, early[1], early[0]),
        depth + 1: jnp.where(swap, late[1], late[0]),
        depth + 2: jnp.where(swap, late[0], late[1]),
        depth + 3: jnp.where(swap, early[0], early[1]),
    }
    base = depth * width
    owners = owners_of(basis_ref, basis_ref.shape[1] - 128)
    for group, owner in enumerate(owners):
        pick = tables_ref[group : group + 1] == lax.broadcasted_iota(jnp.int32, (own, entries), 0)
        pick = jnp.where(pick, 1.0, 0.0).astype(jnp.bfloat16)
        factor = look_up(owner)
        if group == 0:
            places = [(z, z * width) for z in range(depth)]
        else:
            at = depth + 2 * (group - 1)
            places = [(at + k, base + (at + k - depth) * width) for k in range(2)]
        for z, start in places:
            part = (basis_ref[:, start : start + width].astype(jnp.float32) * factor).astype(jnp.bfloat16)
            added = jnp.dot(pick, part, preferred_element_type=jnp.float32)
            value = (plain_ref[z] if z < depth else wide[z]) + added
            cor_ref[z] = value
            top_ref[z] = value[:2]
            bottom_ref[z] = value[own - 2 :]


def smooth_kernel(cor_ref, top_ref, bottom_ref, weight_ref, out_ref, ext_ref, mid_ref):
    planes, rows, width = ext_ref.shape
    own, depth, unused = out_ref.shape
    blank = jnp.zeros((8, width), jnp.float32)
    for z in range(planes):
        ext_ref[z, :own] = cor_ref[z]
        ext_ref[z, own:] = blank
        ext_ref[z, own : own + 2] = top_ref[z]
        ext_ref[z, rows - 2 :] = bottom_ref[z]

    def sweep(ref, z, upto):
        value = ref[z]
        near = (
            pltpu.roll(value, 1, 1)[:upto],
            pltpu.roll(value, width - 1, 1)[:upto],
            pltpu.roll(value, 1, 0)[:upto],
            pltpu.roll(value, rows - 1, 0)[:upto],
            ref[(z - 1) % planes, :upto],
            ref[(z + 1) % planes, :upto],
        )
        total = (1.0 - OMEGA) * value[:upto] + weight_ref[6, z, :upto]
        for k in range(6):
            total = total + weight_ref[k, z, :upto] * near[k]
        return total

    for z in [planes - 1] + list(range(depth + 1)):
        mid_ref[z] = sweep(ext_ref, z, rows)
    for start in range(0, depth, 8):
        for z in range(start, start + 8):
            ext_ref[z, :own] = sweep(mid_ref, z, own)
        out_ref[:, start : start + 8, :] = jnp.transpose(ext_ref[start : start + 8, :own], (1, 0, 2))


def shards(
    solution,
    source,
    phase_label,
    phase_diffusivity,
    phase_uptake,
    send_tiles,
    support_slot,
    support_len,
    coarse_ids,
    basis_values,
    coarse_diag,
    coarse_off,
    coarse_cols,
):
    f32, i32, bf16 = jnp.float32, jnp.int32, jnp.bfloat16
    rows, depth, width = solution.shape
    voxels = depth * width
    slabs, tiles = lax.axis_size("slab"), lax.axis_size("tile")
    devices = slabs * tiles
    capacity = send_tiles.shape[3]
    cells, support, unused = basis_values.shape
    entries = cells * support
    count = cells * devices
    nnz = coarse_off.shape[1]
    shape = jax.ShapeDtypeStruct
    planes, tall = depth + 4, rows + 8
    block = (rows, depth, width)
    table = send_tiles.reshape(slabs, capacity)
    wide = voxels + 4 * width + 128
    early = shape((rows + 8 + max(8, slabs), width), f32)
    late = shape((2 * rows, width), f32)
    edge = shape((3, -(-planes // 8) * 8, width), f32)
    outgoing, even, odd, late_even, late_odd, top, bottom = pl.pallas_call(
        functools.partial(prepare_kernel, capacity=capacity),
        out_shape=(shape((entries, wide), bf16), early, early, late, late, edge, edge),
        in_specs=[HBM] * 8,
        out_specs=(HBM,) + (VMEM,) * 6,
        scratch_shapes=[
            pltpu.VMEM((1, entries), i32),
            pltpu.SMEM((cells,), i32),
            pltpu.SMEM((cells,), i32),
            pltpu.VMEM((entries, voxels), bf16),
            pltpu.VMEM(block, f32),
            pltpu.VMEM(block, i32),
            pltpu.VMEM(block, f32),
            pltpu.VMEM((slabs, capacity), i32),
            pltpu.VMEM((entries, wide), bf16),
            pltpu.SemaphoreType.DMA((19,)),
        ],
        compiler_params=params(60),
        name="prepare",
    )(
        support_slot.reshape(1, entries),
        support_len.reshape(cells),
        coarse_ids,
        basis_values.reshape(entries, voxels),
        solution,
        phase_label,
        source,
        table,
    )
    even = lax.ppermute(even, "slab", pairs(slabs, False))
    odd = lax.ppermute(odd, "slab", pairs(slabs, True))
    outgoing, even, odd = lax.optimization_barrier((outgoing, even, odd))
    basis = lax.all_to_all(
        outgoing.reshape(slabs, capacity, wide), "slab", split_axis=0, concat_axis=0, tiled=True
    ).reshape(entries, wide)

    late_even, late_odd, outgoing = lax.optimization_barrier((late_even, late_odd, outgoing))
    top, bottom = pl.pallas_call(
        functools.partial(edge_kernel, own=rows, depth=depth),
        out_shape=(edge, edge),
        in_specs=[HBM] * 4,
        out_specs=(VMEM,) * 2,
        scratch_shapes=[
            pltpu.VMEM(early.shape, f32),
            pltpu.VMEM(early.shape, f32),
            pltpu.SemaphoreType.DMA((4,)),
        ],
        compiler_params=params(8),
        name="edge",
    )(*[pltpu.with_memory_space_constraint(array, pltpu.HBM) for array in (top, bottom)], even, odd)
    top = lax.ppermute(top, "tile", wheel(tiles, -1))
    bottom = lax.ppermute(bottom, "tile", wheel(tiles, 1))
    row_top, row_bottom = top, bottom
    late_even = lax.ppermute(late_even, "slab", pairs(slabs, False))
    late_odd = lax.ppermute(late_odd, "slab", pairs(slabs, True))

    wide_block = pltpu.VMEM((planes, tall, width), f32)
    operands = [
        phase_diffusivity, phase_uptake, coarse_diag, coarse_off, coarse_cols, table,
        solution, phase_label, source, even, odd, top, bottom,
    ]
    residual, plain, packed, tables, column, record = pl.pallas_call(
        residual_kernel,
        out_shape=(
            shape((depth, rows, width), bf16),
            shape((depth, rows, width), f32),
            shape((depth // 2, 8, width), f32),
            shape((8, entries), i32),
            shape((entries, 8), i32),
            shape((cells, 128), f32),
        ),
        in_specs=[HBM] * 13,
        out_specs=(VMEM,) * 6,
        scratch_shapes=[wide_block] * 3
        + [pltpu.SMEM(array.shape, array.dtype) for array in operands[:3]]
        + [pltpu.VMEM(array.shape, array.dtype) for array in operands[3:]]
        + [pltpu.SemaphoreType.DMA((13,))],
        compiler_params=params(12),
        name="residual",
    )(*[pltpu.with_memory_space_constraint(array, pltpu.HBM) for array in operands[:9]], *operands[9:])

    basis, late_even, late_odd = lax.optimization_barrier((basis, late_even, late_odd))
    lines = max(8, count // HALF)
    payload = pl.pallas_call(
        restrict_kernel,
        out_shape=shape((devices, lines, 128), f32),
        in_specs=[VMEM, VMEM, VMEM, VMEM],
        out_specs=VMEM,
        compiler_params=params(8),
        name="restrict",
    )(column, record, residual, basis)
    got = lax.all_to_all(payload, ("slab", "tile"), split_axis=0, concat_axis=0, tiled=True)

    edge = shape((planes, 2, width), f32)
    corrected, top, bottom, coarse_correction = pl.pallas_call(
        functools.partial(prolong_kernel, nnz=nnz, depth=depth),
        out_shape=(shape((planes, rows, width), f32), edge, edge, shape((1, cells), f32)),
        in_specs=[SMEM] + [VMEM] * 8,
        out_specs=(VMEM, VMEM, VMEM, VMEM),
        compiler_params=params(12 + count * count // (8 * MIB)),
        name="prolong",
    )(coarse_ids, tables, even, odd, late_even, late_odd, got, basis, plain)
    corrected, packed = lax.optimization_barrier((corrected, packed))
    weights = pl.pallas_call(
        weigh_kernel,
        out_shape=shape((7, planes, tall, width), f32),
        in_specs=[SMEM, SMEM] + [VMEM] * 8,
        out_specs=VMEM,
        scratch_shapes=[wide_block] * 2,
        compiler_params=params(12),
        name="weigh",
    )(phase_diffusivity, phase_uptake, packed, source, even, odd, row_top, row_bottom, late_even, late_odd)
    top = lax.ppermute(top, "tile", wheel(tiles, -1))
    bottom = lax.ppermute(bottom, "tile", wheel(tiles, 1))
    smooth = pl.pallas_call(
        smooth_kernel,
        out_shape=shape((rows, depth, width), f32),
        in_specs=[VMEM] * 4,
        out_specs=VMEM,
        scratch_shapes=[wide_block] * 2,
        compiler_params=params(16),
        name="smooth",
    )(corrected, top, bottom, weights)
    return smooth, coarse_correction.reshape(cells)


def solution(mesh):
    placed = (
        P("tile", "slab", None),
        P("tile", "slab", None),
        P("tile", "slab", None),
        P(),
        P(),
        P("slab", "tile", None, None),
        P("slab", "tile", None),
        P("slab", "tile", None),
        P(("slab", "tile")),
        P(("slab", "tile"), None, None),
        P(("slab", "tile")),
        P(("slab", "tile"), None),
        P(("slab", "tile"), None),
    )
    return jax.shard_map(
        shards,
        mesh=mesh,
        in_specs=placed,
        out_specs=(P("tile", "slab", None), P(("slab", "tile"))),
        check_vma=False,
    )
```

```python
import functools

import jax
import jax.numpy as jnp
from jax import lax
from jax.experimental import pallas as pl
from jax.experimental.pallas import tpu as pltpu
from jax.sharding import PartitionSpec as P

COARSE_SWEEPS = 4
SMOOTH_SWEEPS = 2
OMEGA = 0.8

VMEM = pl.BlockSpec(memory_space=pltpu.VMEM)
SMEM = pl.BlockSpec(memory_space=pltpu.SMEM)
HBM = pl.BlockSpec(memory_space=pltpu.HBM)
MIB = 1024 * 1024
COLS_LANE = 32
HALF = 64
DIAG_LANE = 60


def params(mib=16):
    return pltpu.CompilerParams(vmem_limit_bytes=mib * MIB)


def wheel(count, step):
    return [(i, (i + step) % count) for i in range(count)]


def pairs(count, odd):
    start = 1 if odd else 0
    table = list(range(count))
    for i in range(start, count - 1, 2):
        table[i], table[i + 1] = i + 1, i
    return list(enumerate(table))


def fetch(pairs_of_refs, sems):
    copies = [
        pltpu.make_async_copy(source, target, sems.at[k])
        for k, (source, target) in enumerate(pairs_of_refs)
    ]
    for copy in copies:
        copy.start()
    return copies


def sort_kernel(
    slot_hbm, len_hbm, ids_hbm, basis_hbm, out_hbm, slot_ref, len_ref, ids_ref, basis_ref, out_ref, sems, *, capacity
):
    entries, voxels = basis_ref.shape
    cells = len_ref.shape[0]
    support = entries // cells
    border = (out_ref.shape[1] - 128 - voxels) // 2
    chunk = voxels // 4
    pieces = [
        (basis_hbm.at[:, pl.ds(k * chunk, chunk)], basis_ref.at[:, pl.ds(k * chunk, chunk)]) for k in range(4)
    ]
    small = [(slot_hbm, slot_ref), (len_hbm, len_ref), (ids_hbm, ids_ref)]
    copies = fetch(small + pieces, sems)
    for copy in copies[:3]:
        copy.wait()
    lane = lax.broadcasted_iota(jnp.int32, (1, entries), 1)
    length = jnp.zeros((1, entries), jnp.int32)
    ident = jnp.zeros((1, entries), jnp.int32)
    for cell in range(cells):
        here = lane // support == cell
        length = jnp.where(here, len_ref[cell], length)
        ident = jnp.where(here, ids_ref[cell], ident)
    live = lane % support < length
    slot = jnp.where(live, slot_ref[...], -1)
    row = lax.broadcasted_iota(jnp.int32, (entries, entries), 0)
    above = jnp.where(row >= entries - capacity, row + capacity - entries, row + capacity)
    below = jnp.where(row < capacity, row - capacity + entries, row - capacity)
    hits = [slot == row, slot == above, slot == below]
    picks = [jnp.where(hit, 1.0, 0.0).astype(jnp.bfloat16) for hit in hits]
    sent = []

    def move(pick, start, size, target):
        out_ref[:, target : target + size] = jnp.dot(
            pick, basis_ref[:, start : start + size], preferred_element_type=jnp.float32
        ).astype(jnp.bfloat16)

    def send(start, size):
        part = pl.ds(start, size)
        copy = pltpu.make_async_copy(out_ref.at[:, part], out_hbm.at[:, part], sems.at[len(copies) + len(sent)])
        copy.start()
        sent.append(copy)

    extra = lax.broadcasted_iota(jnp.int32, (entries, 128), 1)
    tail = jnp.zeros((entries, 128), jnp.float32)
    for k, hit in enumerate(hits):
        low = jnp.sum(jnp.where(hit, ident % 256, 0).astype(jnp.float32), axis=1, keepdims=True)
        high = jnp.sum(jnp.where(hit, ident // 256, 0).astype(jnp.float32), axis=1, keepdims=True)
        tail = jnp.where(extra == 2 * k, low, jnp.where(extra == 2 * k + 1, high, tail))
    out_ref[:, voxels + 2 * border :] = tail.astype(jnp.bfloat16)
    for k in range(4):
        copies[3 + k].wait()
        for start in range(k * chunk, (k + 1) * chunk, 512):
            move(picks[0], start, 512, start)
        send(k * chunk, chunk)
        if k == 0:
            move(picks[1], 0, border, voxels)
    move(picks[2], voxels - border, border, voxels + border)
    send(voxels, 2 * border + 128)
    for copy in sent:
        copy.wait()


LOW, FAR, SOURCE, LABELS, CORNERS, TABLE = 32, 64, 96, 128, 144, 148
MESSAGE = 160


def border_kernel(
    sol_hbm, label_hbm, src_hbm, table_hbm, even_ref, odd_ref, top_ref, bottom_ref,
    sol_ref, label_ref, src_ref, table_ref, sems,
):
    rows, depth, width = sol_ref.shape
    blocks = ((sol_hbm, sol_ref), (label_hbm, label_ref), (src_hbm, src_ref), (table_hbm, table_ref))
    for copy in fetch(blocks, sems):
        copy.wait()
    odd = lax.axis_index("slab") % 2 == 1

    def planes(start):
        parts = [ref[:, start : start + 2, :].astype(jnp.float32) for ref in (sol_ref, label_ref, src_ref, src_ref)]
        block = jnp.transpose(jnp.concatenate(parts, axis=1), (1, 0, 2))
        return [block[k] for k in range(6)]

    near, far, label, label_far, origin, unused = planes(0)
    down = near, far, origin, pack_labels(label, label_far, 16)
    far, near, label_far, label, unused, origin = planes(depth - 2)
    up = near, far, origin, pack_labels(label, label_far, 16)
    table = flat(table_ref[...]).astype(jnp.float32)
    entries = table.shape[1]
    table = jnp.concatenate([table, jnp.zeros((1, width - entries), jnp.float32)], axis=1)
    line = lax.broadcasted_iota(jnp.int32, (16, width), 0) + CORNERS
    table = jnp.where(line == TABLE, table, 0.0)
    for first, second, ref in ((up, down, even_ref), (down, up, odd_ref)):
        near, far, origin, labels = [jnp.where(odd, b, a) for a, b in zip(first, second)]
        high = near.astype(jnp.bfloat16)
        ref[:LOW] = high
        ref[LOW:FAR] = (near - high.astype(jnp.float32)).astype(jnp.bfloat16)
        ref[FAR:SOURCE] = far.astype(jnp.bfloat16)
        ref[SOURCE:LABELS] = origin.astype(jnp.bfloat16)
        ref[LABELS:CORNERS] = labels.astype(jnp.bfloat16)
        ref[CORNERS:] = table.astype(jnp.bfloat16)
    for ref, near, far in ((top_ref, 0, 1), (bottom_ref, rows - 1, rows - 2)):
        ref[0] = sol_ref[near]
        ref[1] = (label_ref[near] + 3 * label_ref[far]).astype(jnp.float32)
        ref[2] = src_ref[near]


def flat(table):
    return jnp.concatenate([table[at : at + 1] for at in range(table.shape[0])], axis=1)


def pack_labels(near, far, lines):
    pair = near + 3.0 * far
    packed = pair[0:lines]
    for k in range(1, pair.shape[0] // lines):
        packed = packed + float(9**k) * pair[lines * k : lines * (k + 1)]
    return packed


def unpack_labels(packed, rows):
    found = []
    for k in range(rows // packed.shape[0]):
        rest = jnp.floor((packed + 0.5) * (1.0 / 9.0))
        found.append(packed - 9.0 * rest)
        packed = rest
    return part_pair(jnp.concatenate(found, axis=0))


def part_pair(pair):
    far = jnp.floor((pair + 0.5) * (1.0 / 3.0))
    return pair - 3.0 * far, far


def from_slab(even_ref, odd_ref, start, stop):
    swap = lax.axis_index("slab") % 2 == 1
    even, odd = even_ref[start:stop].astype(jnp.float32), odd_ref[start:stop].astype(jnp.float32)
    return jnp.where(swap, odd, even), jnp.where(swap, even, odd)


def nearest_planes(even_ref, odd_ref):
    upper, lower = from_slab(even_ref, odd_ref, 0, LOW), from_slab(even_ref, odd_ref, LOW, FAR)
    return upper[0] + lower[0], upper[1] + lower[1]


def corner_kernel(even_in, odd_in, top_in, bottom_in, even_ref, odd_ref, top_ref, bottom_ref, sems):
    for copy in fetch([(even_in, even_ref), (odd_in, odd_ref), (top_in, top_ref), (bottom_in, bottom_ref)], sems):
        copy.wait()
    depth, width = top_ref.shape[1:]
    odd = lax.axis_index("slab") % 2 == 1
    line = lax.broadcasted_iota(jnp.int32, (16, width), 0)
    for ref, upward in ((even_ref, jnp.logical_not(odd)), (odd_ref, odd)):
        block = ref[CORNERS:].astype(jnp.float32)
        for k in range(4):
            edge_ref, low = (top_ref, bottom_ref)[k // 2], k % 2
            high = depth - 1 - low
            pair = jnp.where(upward, edge_ref[1, high : high + 1], edge_ref[1, low : low + 1])
            block = jnp.where(line == k, pair, block)
        ref[CORNERS:] = block.astype(jnp.bfloat16)


def beside(plane, lane):
    rows, width = plane.shape
    left = jnp.where(lane == 0, 0.0, pltpu.roll(plane, 1, 1))
    right = jnp.where(lane == width - 1, 0.0, pltpu.roll(plane, width - 1, 1))
    return left + right + pltpu.roll(plane, 1, 0) + pltpu.roll(plane, rows - 1, 0)


class Grid:
    def __init__(self, diff_ref, upt_ref, labels, top_pairs, bottom_pairs, outside, conduct_ref, uptake_ref):
        self.conduct_ref, self.uptake_ref = conduct_ref, uptake_ref
        self.planes, rows, width = conduct_ref.shape
        own = labels[0].shape[0]
        phases = diff_ref.shape[0]
        row = lax.broadcasted_iota(jnp.int32, (rows, width), 0)
        self.lane = lax.broadcasted_iota(jnp.int32, (rows, width), 1)
        tile = lax.axis_index("tile")
        beyond = (row >= own + 2) & (row < rows - 2)
        beyond = beyond | ((row >= own) & (row < own + 4) & (tile == lax.axis_size("tile") - 1))
        beyond = beyond | ((row >= own + 4) & (tile == 0))
        blank = jnp.zeros((8, width), jnp.float32)
        for z, (label, top, bottom) in enumerate(zip(labels, top_pairs, bottom_pairs)):
            conduct_ref[z, :own] = label
            conduct_ref[z, own:] = blank
            near, far = part_pair(top)
            conduct_ref[z, own : own + 1] = near
            conduct_ref[z, own + 1 : own + 2] = far
            near, far = part_pair(bottom)
            conduct_ref[z, rows - 1 :] = near
            conduct_ref[z, rows - 2 : rows - 1] = far
            label = jnp.where(beyond | outside[z] if z in outside else beyond, -1.0, conduct_ref[z])
            conduct = jnp.zeros(label.shape, jnp.float32)
            uptake = jnp.zeros(label.shape, jnp.float32)
            for phase in range(phases):
                conduct = jnp.where(label == float(phase), diff_ref[phase], conduct)
                uptake = jnp.where(label == float(phase), upt_ref[phase], uptake)
            conduct_ref[z] = conduct
            uptake_ref[z] = uptake

    def in_plane(self, z):
        rows, width = self.conduct_ref.shape[1:]
        plane = self.conduct_ref[z]
        return (
            jnp.where(self.lane == 0, 0.0, pltpu.roll(plane, 1, 1)),
            jnp.where(self.lane == width - 1, 0.0, pltpu.roll(plane, width - 1, 1)),
            pltpu.roll(plane, 1, 0),
            pltpu.roll(plane, rows - 1, 0),
        )


def ends():
    slab = lax.axis_index("slab")
    return slab == lax.axis_size("slab") - 1, slab == 0


def residual_kernel(*refs):
    operands, outputs, scratch = refs[:11], refs[11:18], refs[18:]
    conduct_ref, uptake_ref, sol_ref = scratch[:3]
    local, sems = scratch[3:14], scratch[14]
    diff_ref, upt_ref, diag_ref, off_ref, cols_ref, table_ref, sol_in, label_in, src_in, top_ref, bottom_ref = local
    res_ref, face_ref, plain_ref, packed_ref, tables_ref, column_ref, record_ref = outputs
    for copy in fetch(list(zip(operands, local)), sems):
        copy.wait()
    own, depth, width = sol_in.shape
    rows = conduct_ref.shape[1]
    cells, nnz = off_ref.shape

    line = lax.broadcasted_iota(jnp.int32, record_ref.shape, 0)
    record = jnp.zeros(record_ref.shape, jnp.float32)
    for cell in range(cells):
        record = jnp.where(line == cell, diag_ref[cell], record)
    record_ref[...] = record
    record_ref[:, :nnz] = off_ref[...]
    record_ref[:, COLS_LANE : COLS_LANE + nnz] = cols_ref[...].astype(jnp.float32)
    tables_ref[...] = jnp.broadcast_to(flat(table_ref[...]), tables_ref.shape)
    column_ref[...] = jnp.transpose(tables_ref[...].astype(jnp.float32)).astype(jnp.int32)

    labels = []
    for start in range(0, depth, 8):
        block = jnp.transpose(label_in[:, start : start + 8, :].astype(jnp.float32), (1, 0, 2))
        labels = labels + [block[at] for at in range(8)]
    for k in range(depth // 2):
        packed_ref[k] = pack_labels(labels[2 * k], labels[2 * k + 1], 8)
    top_pairs = [top_ref[1, z : z + 1] for z in range(depth)]
    bottom_pairs = [bottom_ref[1, z : z + 1] for z in range(depth)]
    grid = Grid(diff_ref, upt_ref, labels, top_pairs, bottom_pairs, {}, conduct_ref, uptake_ref)
    blank = jnp.zeros((8, width), jnp.float32)
    for start in range(0, depth, 8):
        block = jnp.transpose(sol_in[:, start : start + 8, :], (1, 0, 2))
        for at in range(8):
            z = start + at
            plain_ref[z] = block[at]
            sol_ref[z, :own] = block[at]
            sol_ref[z, own:] = blank
            sol_ref[z, own : own + 1] = top_ref[0, z : z + 1]
            sol_ref[z, rows - 1 :] = bottom_ref[0, z : z + 1]
            sol_ref[z] = jnp.where(conduct_ref[z] > 0.0, sol_ref[z], 0.0)
    for start in range(0, depth, 8):
        block = jnp.transpose(src_in[:, start : start + 8, :], (1, 0, 2))
        for at in range(8):
            z = start + at
            conduct, value = conduct_ref[z], sol_ref[z]
            near = sum(grid.in_plane(z))
            diagonal = uptake_ref[z] + 2.0 * conduct + 0.5 * near
            flow = conduct * beside(value, grid.lane) + beside(conduct * value, grid.lane)
            applied = (diagonal * value - 0.5 * flow)[:own]
            conduct, value = conduct[:own], value[:own]
            for other in (z - 1, z + 1):
                if 0 <= other < depth:
                    applied = applied + 0.5 * (conduct + conduct_ref[other, :own]) * (value - sol_ref[other, :own])
            left = block[at] - applied
            res_ref[z] = left.astype(jnp.bfloat16)
            if z in (0, depth - 1):
                side = 0 if z == 0 else 3
                face_ref[side] = left
                face_ref[side + 1] = conduct
                face_ref[side + 2] = value


def weigh_kernel(
    diff_ref, upt_ref, packed_ref, src_in, even_ref, odd_ref, top_ref, bottom_ref, weight_ref,
    conduct_ref, uptake_ref,
):
    own, depth, width = src_in.shape
    planes, rows = conduct_ref.shape[0:2]
    labels = []
    for k in range(depth // 2):
        labels = labels + list(unpack_labels(packed_ref[k], own))
    high, low = from_slab(even_ref, odd_ref, LABELS, CORNERS)
    (high_near, high_far), (low_near, low_far) = unpack_labels(high, own), unpack_labels(low, own)
    labels = labels + [high_near, high_far, low_far, low_near]
    high, low = from_slab(even_ref, odd_ref, CORNERS, MESSAGE)
    top_pairs = [top_ref[1, z : z + 1] for z in range(depth)] + [high[0:1], high[1:2], low[1:2], low[0:1]]
    bottom_pairs = [bottom_ref[1, z : z + 1] for z in range(depth)] + [high[2:3], high[3:4], low[3:4], low[2:3]]
    above, below = ends()
    outside = {depth: above, depth + 1: above, depth + 2: below, depth + 3: below}
    grid = Grid(diff_ref, upt_ref, labels, top_pairs, bottom_pairs, outside, conduct_ref, uptake_ref)
    blank = jnp.zeros((8, width), jnp.float32)
    outer = dict(zip((depth, planes - 1), from_slab(even_ref, odd_ref, SOURCE, LABELS)))
    for start in (0, 8, planes - 1, depth):
        if start < depth:
            block = jnp.transpose(src_in[:, start : start + 8, :], (1, 0, 2))
            sources = {start + at: block[at] for at in range(8)}
        else:
            sources = {start: outer[start]}
        for z, source in sources.items():
            conduct = conduct_ref[z]
            near = grid.in_plane(z) + (conduct_ref[(z - 1) % planes], conduct_ref[(z + 1) % planes])
            diagonal = uptake_ref[z] + 3.0 * conduct + 0.5 * sum(near[1:], near[0])
            inside = conduct > 0.0
            scale = jnp.where(inside, OMEGA / jnp.where(inside, diagonal, 1.0), 0.0)
            for k, other in enumerate(near):
                weight_ref[k, z] = jnp.where(other > 0.0, 0.5 * scale * (conduct + other), 0.0)
            weight_ref[6, z, :own] = scale[:own] * source
            weight_ref[6, z, own:] = blank
            if z < depth:
                weight_ref[6, z, own : own + 1] = scale[own : own + 1] * top_ref[2, z : z + 1]
                weight_ref[6, z, rows - 1 :] = scale[rows - 1 :] * bottom_ref[2, z : z + 1]


def owners_of(basis_ref, base):
    tail = basis_ref[:, base:].astype(jnp.float32)
    return [
        (tail[:, 2 * k : 2 * k + 1] + 256.0 * tail[:, 2 * k + 1 : 2 * k + 2]).astype(jnp.int32)
        for k in range(3)
    ]


def restrict_kernel(diff_ref, column_ref, record_ref, even_ref, odd_ref, face_ref, res_ref, basis_ref, out_ref):
    depth, own, width = res_ref.shape
    entries = basis_ref.shape[0]
    pick = column_ref[:, 0:1] == lax.broadcasted_iota(jnp.int32, (entries, own), 1)
    pick = jnp.where(pick, 1.0, 0.0).astype(jnp.bfloat16)
    values = nearest_planes(even_ref, odd_ref)
    packed = from_slab(even_ref, odd_ref, LABELS, CORNERS)
    faces = {}
    for z, side, at in ((0, 0, 1), (depth - 1, 3, 0)):
        label = unpack_labels(packed[at], own)[0]
        beyond = jnp.zeros(label.shape, jnp.float32)
        for phase in range(diff_ref.shape[0]):
            beyond = jnp.where(label == float(phase), diff_ref[phase], beyond)
        beyond = jnp.where(ends()[at], 0.0, beyond)
        value = jnp.where(ends()[at], 0.0, values[at])
        applied = 0.5 * (face_ref[side + 1] + beyond) * (face_ref[side + 2] - value)
        faces[z] = (face_ref[side] - applied).astype(jnp.bfloat16)
    total = jnp.zeros((entries, width), jnp.float32)
    for z in range(depth):
        plane = faces[z] if z in faces else res_ref[z]
        piece = jnp.dot(pick, plane, preferred_element_type=jnp.float32)
        total = total + piece * basis_ref[:, z * width : (z + 1) * width].astype(jnp.float32)
    product = jnp.sum(total, axis=1, keepdims=True)
    ident = owners_of(basis_ref, basis_ref.shape[1] - 128)[0]
    copies, lines, lanes = out_ref.shape
    lane = lax.broadcasted_iota(jnp.int32, (entries, lanes), 1)
    line = lax.broadcasted_iota(jnp.int32, (8, lanes), 0)
    for base in range(0, lines, 8):
        block = record_ref[...] if base == 0 else jnp.zeros((8, lanes), jnp.float32)
        for row in range(8):
            share = jnp.where(ident == (base + row) * HALF + lane - HALF, product, 0.0)
            share = jnp.sum(jnp.where(lane >= HALF, share, 0.0), axis=0, keepdims=True)
            block = jnp.where((line == row) & (lane[:8] >= HALF), share, block)

        def put(copy, carry):
            out_ref[copy, base : base + 8, :] = block
            return carry

        lax.fori_loop(0, copies, put, 0, unroll=8)


def solve(got_ref, count, nnz):
    devices, lines, lanes = got_ref.shape
    summed = got_ref[0]
    if devices <= 64:
        for device in range(1, devices):
            summed = summed + got_ref[device]
    else:
        summed = lax.fori_loop(1, devices, lambda d, total: total + got_ref[d], summed)
    rhs = jnp.concatenate([summed[at : at + 1, HALF:] for at in range(count // HALF)], axis=1)
    record = jnp.transpose(got_ref[:, 0:8, :].reshape(count, lanes))
    line = lax.broadcasted_iota(jnp.int32, (COLS_LANE, lanes), 0)
    inverse = 1.0 / record[DIAG_LANE : DIAG_LANE + 1]
    chunks = range(0, count, lanes)
    values = [jnp.where(line < nnz, record[:COLS_LANE, at : at + lanes], 0.0) for at in chunks]
    places = [
        jnp.where(line < nnz, record[COLS_LANE : 2 * COLS_LANE, at : at + lanes], 0.0).astype(jnp.int32)
        for at in chunks
    ]
    state = rhs * inverse
    for repeat in range(COARSE_SWEEPS - 1):
        sources = [jnp.broadcast_to(state[:, at : at + lanes], (COLS_LANE, lanes)) for at in chunks]
        pulled = []
        for value, place in zip(values, places):
            found = jnp.zeros((COLS_LANE, lanes), jnp.float32)
            for k, source in enumerate(sources):
                taken = jnp.take_along_axis(source, place % lanes, axis=1, mode="promise_in_bounds")
                found = jnp.where(place // lanes == k, taken, found)
            pulled.append(jnp.sum(value * found, axis=0, keepdims=True))
        state = (rhs - jnp.concatenate(pulled, axis=1)) * inverse
    return state


def prolong_kernel(
    ids_ref, tables_ref, even_ref, odd_ref, got_ref, basis_ref, plain_ref, cor_ref, top_ref, bottom_ref,
    correction_ref, *, nnz, depth,
):
    planes, own, width = cor_ref.shape
    entries = tables_ref.shape[1]
    cells = ids_ref.shape[0]
    count = cells * got_ref.shape[0]
    state = solve(got_ref, count, nnz)

    line = lax.broadcasted_iota(jnp.int32, (cells, 1), 0)
    mine = jnp.zeros((cells, 1), jnp.int32)
    for cell in range(cells):
        mine = jnp.where(line == cell, ids_ref[cell], mine)

    def look_up(ident):
        hit = ident == lax.broadcasted_iota(jnp.int32, (ident.shape[0], count), 1)
        return jnp.sum(jnp.where(hit, state, 0.0), axis=1, keepdims=True)

    diagonal = line == lax.broadcasted_iota(jnp.int32, (cells, cells), 1)
    correction_ref[...] = jnp.sum(jnp.where(diagonal, look_up(mine), 0.0), axis=0, keepdims=True)
    near_high, near_low = nearest_planes(even_ref, odd_ref)
    far_high, far_low = from_slab(even_ref, odd_ref, FAR, SOURCE)
    wide = {depth: near_high, depth + 1: far_high, depth + 2: far_low, depth + 3: near_low}
    high, low = from_slab(even_ref, odd_ref, CORNERS, MESSAGE)
    line = TABLE - CORNERS
    table_high, table_low = high[line : line + 1, :entries], low[line : line + 1, :entries]
    tables = (tables_ref[0:1], table_high.astype(jnp.int32), table_low.astype(jnp.int32))
    base = depth * width
    owners = owners_of(basis_ref, basis_ref.shape[1] - 128)
    for group, owner in enumerate(owners):
        pick = tables[group] == lax.broadcasted_iota(jnp.int32, (own, entries), 0)
        pick = jnp.where(pick, 1.0, 0.0).astype(jnp.bfloat16)
        factor = look_up(owner)
        if group == 0:
            places = [(z, z * width) for z in range(depth)]
        else:
            at = depth + 2 * (group - 1)
            places = [(at + k, base + (at + k - depth) * width) for k in range(2)]
        for z, start in places:
            part = (basis_ref[:, start : start + width].astype(jnp.float32) * factor).astype(jnp.bfloat16)
            added = jnp.dot(pick, part, preferred_element_type=jnp.float32)
            value = (plain_ref[z] if z < depth else wide[z]) + added
            cor_ref[z] = value
            top_ref[z] = value[:2]
            bottom_ref[z] = value[own - 2 :]


def smooth_kernel(cor_ref, top_ref, bottom_ref, weight_ref, out_ref, ext_ref, mid_ref):
    planes, rows, width = ext_ref.shape
    own, depth, unused = out_ref.shape
    blank = jnp.zeros((8, width), jnp.float32)
    for z in range(planes):
        ext_ref[z, :own] = cor_ref[z]
        ext_ref[z, own:] = blank
        ext_ref[z, own : own + 2] = top_ref[z]
        ext_ref[z, rows - 2 :] = bottom_ref[z]

    def sweep(ref, z, upto):
        value = ref[z]
        near = (
            pltpu.roll(value, 1, 1)[:upto],
            pltpu.roll(value, width - 1, 1)[:upto],
            pltpu.roll(value, 1, 0)[:upto],
            pltpu.roll(value, rows - 1, 0)[:upto],
            ref[(z - 1) % planes, :upto],
            ref[(z + 1) % planes, :upto],
        )
        total = (1.0 - OMEGA) * value[:upto] + weight_ref[6, z, :upto]
        for k in range(6):
            total = total + weight_ref[k, z, :upto] * near[k]
        return total

    for z in [planes - 1] + list(range(depth + 1)):
        mid_ref[z] = sweep(ext_ref, z, rows)
    for start in range(0, depth, 8):
        for z in range(start, start + 8):
            ext_ref[z, :own] = sweep(mid_ref, z, own)
        out_ref[:, start : start + 8, :] = jnp.transpose(ext_ref[start : start + 8, :own], (1, 0, 2))


def shards(
    solution,
    source,
    phase_label,
    phase_diffusivity,
    phase_uptake,
    send_tiles,
    support_slot,
    support_len,
    coarse_ids,
    basis_values,
    coarse_diag,
    coarse_off,
    coarse_cols,
):
    f32, i32, bf16 = jnp.float32, jnp.int32, jnp.bfloat16
    rows, depth, width = solution.shape
    voxels = depth * width
    slabs, tiles = lax.axis_size("slab"), lax.axis_size("tile")
    devices = slabs * tiles
    capacity = send_tiles.shape[3]
    cells, support, unused = basis_values.shape
    entries = cells * support
    count = cells * devices
    nnz = coarse_off.shape[1]
    shape = jax.ShapeDtypeStruct
    planes, tall = depth + 4, rows + 8
    block = (rows, depth, width)
    table = send_tiles.reshape(slabs, capacity)
    wide = voxels + 4 * width + 128
    outgoing = pl.pallas_call(
        functools.partial(sort_kernel, capacity=capacity),
        out_shape=shape((entries, wide), bf16),
        in_specs=[HBM] * 4,
        out_specs=HBM,
        scratch_shapes=[
            pltpu.VMEM((1, entries), i32),
            pltpu.SMEM((cells,), i32),
            pltpu.SMEM((cells,), i32),
            pltpu.VMEM((entries, voxels), bf16),
            pltpu.VMEM((entries, wide), bf16),
            pltpu.SemaphoreType.DMA((12,)),
        ],
        compiler_params=params(60),
        name="sort_basis",
    )(
        support_slot.reshape(1, entries),
        support_len.reshape(cells),
        coarse_ids,
        basis_values.reshape(entries, voxels),
    )
    basis = lax.all_to_all(
        outgoing.reshape(slabs, capacity, wide), "slab", split_axis=0, concat_axis=0, tiled=True
    ).reshape(entries, wide)

    outgoing, solution, phase_label, source, table = lax.optimization_barrier(
        (outgoing, solution, phase_label, source, table)
    )

    def pinned(*arrays):
        return [pltpu.with_memory_space_constraint(array, pltpu.HBM) for array in arrays]

    message = shape((MESSAGE, width), bf16)
    edge = shape((3, depth, width), f32)
    even, odd, top, bottom = pl.pallas_call(
        border_kernel,
        out_shape=(message, message, edge, edge),
        in_specs=[HBM] * 4,
        out_specs=(VMEM,) * 4,
        scratch_shapes=[
            pltpu.VMEM(block, f32),
            pltpu.VMEM(block, i32),
            pltpu.VMEM(block, f32),
            pltpu.VMEM((slabs, capacity), i32),
            pltpu.SemaphoreType.DMA((4,)),
        ],
        compiler_params=params(8),
        name="border",
    )(*pinned(solution, phase_label, source, table))
    top = lax.ppermute(top, "tile", wheel(tiles, -1))
    bottom = lax.ppermute(bottom, "tile", wheel(tiles, 1))
    even, odd = pl.pallas_call(
        corner_kernel,
        out_shape=(message, message),
        in_specs=[HBM] * 4,
        out_specs=(VMEM,) * 2,
        scratch_shapes=[pltpu.VMEM(edge.shape, f32)] * 2 + [pltpu.SemaphoreType.DMA((4,))],
        compiler_params=params(8),
        name="corner",
    )(even, odd, top, bottom)
    even = lax.ppermute(even, "slab", pairs(slabs, False))
    odd = lax.ppermute(odd, "slab", pairs(slabs, True))
    row_top, row_bottom = top, bottom

    wide_block = pltpu.VMEM((planes, tall, width), f32)
    operands = [
        phase_diffusivity, phase_uptake, coarse_diag, coarse_off, coarse_cols, table,
        solution, phase_label, source, top, bottom,
    ]
    residual, face, plain, packed, tables, column, record = pl.pallas_call(
        residual_kernel,
        out_shape=(
            shape((depth, rows, width), bf16),
            shape((6, rows, width), f32),
            shape((depth, rows, width), f32),
            shape((depth // 2, 8, width), f32),
            shape((8, entries), i32),
            shape((entries, 8), i32),
            shape((cells, 128), f32),
        ),
        in_specs=[HBM] * 11,
        out_specs=(VMEM,) * 7,
        scratch_shapes=[pltpu.VMEM((depth, tall, width), f32)] * 3
        + [pltpu.SMEM(array.shape, array.dtype) for array in operands[:3]]
        + [pltpu.VMEM(array.shape, array.dtype) for array in operands[3:]]
        + [pltpu.SemaphoreType.DMA((11,))],
        compiler_params=params(12),
        name="residual",
    )(*pinned(*operands[:9]), *operands[9:])

    lines = max(8, count // HALF)
    payload = pl.pallas_call(
        restrict_kernel,
        out_shape=shape((devices, lines, 128), f32),
        in_specs=[SMEM] + [VMEM] * 7,
        out_specs=VMEM,
        compiler_params=params(8),
        name="restrict",
    )(phase_diffusivity, column, record, even, odd, face, residual, basis)
    got = lax.all_to_all(payload, ("slab", "tile"), split_axis=0, concat_axis=0, tiled=True)

    edge = shape((planes, 2, width), f32)
    corrected, top, bottom, coarse_correction = pl.pallas_call(
        functools.partial(prolong_kernel, nnz=nnz, depth=depth),
        out_shape=(shape((planes, rows, width), f32), edge, edge, shape((1, cells), f32)),
        in_specs=[SMEM] + [VMEM] * 6,
        out_specs=(VMEM, VMEM, VMEM, VMEM),
        compiler_params=params(12 + count * count // (8 * MIB)),
        name="prolong",
    )(coarse_ids, tables, even, odd, got, basis, plain)
    corrected, packed = lax.optimization_barrier((corrected, packed))
    weights = pl.pallas_call(
        weigh_kernel,
        out_shape=shape((7, planes, tall, width), f32),
        in_specs=[SMEM, SMEM] + [VMEM] * 6,
        out_specs=VMEM,
        scratch_shapes=[wide_block] * 2,
        compiler_params=params(12),
        name="weigh",
    )(phase_diffusivity, phase_uptake, packed, source, even, odd, row_top, row_bottom)
    top = lax.ppermute(top, "tile", wheel(tiles, -1))
    bottom = lax.ppermute(bottom, "tile", wheel(tiles, 1))
    smooth = pl.pallas_call(
        smooth_kernel,
        out_shape=shape((rows, depth, width), f32),
        in_specs=[VMEM] * 4,
        out_specs=VMEM,
        scratch_shapes=[wide_block] * 2,
        compiler_params=params(16),
        name="smooth",
    )(corrected, top, bottom, weights)
    return smooth, coarse_correction.reshape(cells)


def solution(mesh):
    placed = (
        P("tile", "slab", None),
        P("tile", "slab", None),
        P("tile", "slab", None),
        P(),
        P(),
        P("slab", "tile", None, None),
        P("slab", "tile", None),
        P("slab", "tile", None),
        P(("slab", "tile")),
        P(("slab", "tile"), None, None),
        P(("slab", "tile")),
        P(("slab", "tile"), None),
        P(("slab", "tile"), None),
    )
    return jax.shard_map(
        shards,
        mesh=mesh,
        in_specs=placed,
        out_specs=(P("tile", "slab", None), P(("slab", "tile"))),
        check_vma=False,
    )
```

```python
import functools

import jax
import jax.numpy as jnp
from jax import lax
from jax.experimental import pallas as pl
from jax.experimental.pallas import tpu as pltpu
from jax.sharding import PartitionSpec as P

COARSE_SWEEPS = 4
SMOOTH_SWEEPS = 2
OMEGA = 0.8

VMEM = pl.BlockSpec(memory_space=pltpu.VMEM)
SMEM = pl.BlockSpec(memory_space=pltpu.SMEM)
HBM = pl.BlockSpec(memory_space=pltpu.HBM)
MIB = 1024 * 1024
COLS_LANE = 32
HALF = 64
DIAG_LANE = 60


def params(mib=16):
    return pltpu.CompilerParams(vmem_limit_bytes=mib * MIB)


def wheel(count, step):
    return [(i, (i + step) % count) for i in range(count)]


def pairs(count, odd):
    start = 1 if odd else 0
    table = list(range(count))
    for i in range(start, count - 1, 2):
        table[i], table[i + 1] = i + 1, i
    return list(enumerate(table))


def fetch(pairs_of_refs, sems):
    copies = [
        pltpu.make_async_copy(source, target, sems.at[k])
        for k, (source, target) in enumerate(pairs_of_refs)
    ]
    for copy in copies:
        copy.start()
    return copies


def sort_kernel(slot_hbm, len_hbm, ids_hbm, basis_hbm, *refs, capacity):
    slot_ref, len_ref, ids_ref, basis_ref, sems = refs[-5:]
    outs = refs[:-5]
    entries, voxels = basis_ref.shape
    lines = entries // len(outs)
    cells = len_ref.shape[0]
    support = entries // cells
    wide = outs[0].shape[1]
    border = (wide - 128 - voxels) // 2
    chunk = voxels // 4
    pieces = [
        (basis_hbm.at[:, pl.ds(k * chunk, chunk)], basis_ref.at[:, pl.ds(k * chunk, chunk)]) for k in range(4)
    ]
    small = [(slot_hbm, slot_ref), (len_hbm, len_ref), (ids_hbm, ids_ref)]
    copies = fetch(small + pieces, sems)
    for copy in copies[:3]:
        copy.wait()
    lane = lax.broadcasted_iota(jnp.int32, (1, entries), 1)
    length = jnp.zeros((1, entries), jnp.int32)
    ident = jnp.zeros((1, entries), jnp.int32)
    for cell in range(cells):
        here = lane // support == cell
        length = jnp.where(here, len_ref[cell], length)
        ident = jnp.where(here, ids_ref[cell], ident)
    live = lane % support < length
    slot = jnp.where(live, slot_ref[...], -1)
    row = lax.broadcasted_iota(jnp.int32, (entries, entries), 0)
    if len(outs) > 1:
        row = row ^ (lax.axis_index("slab") * capacity)
    above = jnp.where(row >= entries - capacity, row + capacity - entries, row + capacity)
    below = jnp.where(row < capacity, row - capacity + entries, row - capacity)
    hits = [slot == row, slot == above, slot == below]
    picks = [jnp.where(hit, 1.0, 0.0).astype(jnp.bfloat16) for hit in hits]

    def put(block, start):
        for k, out in enumerate(outs):
            part = block[k * lines : (k + 1) * lines]
            out[:, start : start + block.shape[1]] = part.astype(jnp.bfloat16)

    def move(pick, start, size, target):
        block = basis_ref[:, start : start + size]
        put(jnp.dot(pick, block, preferred_element_type=jnp.float32), target)

    extra = lax.broadcasted_iota(jnp.int32, (entries, 128), 1)
    tail = jnp.zeros((entries, 128), jnp.float32)
    for k, hit in enumerate(hits):
        low = jnp.sum(jnp.where(hit, ident % 256, 0).astype(jnp.float32), axis=1, keepdims=True)
        high = jnp.sum(jnp.where(hit, ident // 256, 0).astype(jnp.float32), axis=1, keepdims=True)
        tail = jnp.where(extra == 2 * k, low, jnp.where(extra == 2 * k + 1, high, tail))
    put(tail, voxels + 2 * border)
    for k in range(4):
        copies[3 + k].wait()
        for start in range(k * chunk, (k + 1) * chunk, 512):
            move(picks[0], start, 512, start)
        if k == 0:
            move(picks[1], 0, border, voxels)
    move(picks[2], voxels - border, border, voxels + border)


def shuffle(table, slab, slots, capacity):
    lane = lax.broadcasted_iota(jnp.int32, table.shape, 1)
    size = table.shape[1]
    bit = 1
    while bit < slots:
        shift = bit * capacity
        other = jnp.where((lane // shift) % 2 == 1, pltpu.roll(table, shift, 1), pltpu.roll(table, size - shift, 1))
        table = jnp.where((slab // bit) % 2 == 1, other, table)
        bit *= 2
    return table


LOW, FAR, SOURCE, LABELS, CORNERS, TABLE = 32, 64, 96, 128, 144, 148
MESSAGE = 160


def border_kernel(
    sol_hbm, label_hbm, src_hbm, table_hbm, even_ref, odd_ref, top_ref, bottom_ref,
    sol_ref, label_ref, src_ref, table_ref, sems, *, direct,
):
    rows, depth, width = sol_ref.shape
    blocks = ((sol_hbm, sol_ref), (label_hbm, label_ref), (src_hbm, src_ref), (table_hbm, table_ref))
    for copy in fetch(blocks, sems):
        copy.wait()
    odd = lax.axis_index("slab") % 2 == 1

    def planes(start):
        parts = [ref[:, start : start + 2, :].astype(jnp.float32) for ref in (sol_ref, label_ref, src_ref, src_ref)]
        block = jnp.transpose(jnp.concatenate(parts, axis=1), (1, 0, 2))
        return [block[k] for k in range(6)]

    near, far, label, label_far, origin, unused = planes(0)
    down = near, far, origin, pack_labels(label, label_far, 16)
    far, near, label_far, label, unused, origin = planes(depth - 2)
    up = near, far, origin, pack_labels(label, label_far, 16)
    slots, capacity = table_ref.shape
    table = flat(table_ref[...]).astype(jnp.float32)
    table = jnp.concatenate([table, jnp.zeros((1, width - table.shape[1]), jnp.float32)], axis=1)
    tables = [table, table]
    if direct:
        slab, slabs = lax.axis_index("slab"), lax.axis_size("slab")
        tables = [shuffle(table, (slab + step) % slabs, slots, capacity) for step in (1, slabs - 1)]
    line = lax.broadcasted_iota(jnp.int32, (16, width), 0) + CORNERS
    up = up + (jnp.where(line == TABLE, tables[0], 0.0),)
    down = down + (jnp.where(line == TABLE, tables[1], 0.0),)
    for first, second, ref in ((up, down, even_ref), (down, up, odd_ref)):
        near, far, origin, labels, table = [jnp.where(odd, b, a) for a, b in zip(first, second)]
        high = near.astype(jnp.bfloat16)
        ref[:LOW] = high
        ref[LOW:FAR] = (near - high.astype(jnp.float32)).astype(jnp.bfloat16)
        ref[FAR:SOURCE] = far.astype(jnp.bfloat16)
        ref[SOURCE:LABELS] = origin.astype(jnp.bfloat16)
        ref[LABELS:CORNERS] = labels.astype(jnp.bfloat16)
        ref[CORNERS:] = table.astype(jnp.bfloat16)
    for ref, near, far in ((top_ref, 0, 1), (bottom_ref, rows - 1, rows - 2)):
        ref[0] = sol_ref[near]
        ref[1] = (label_ref[near] + 3 * label_ref[far]).astype(jnp.float32)
        ref[2] = src_ref[near]


def flat(table):
    return jnp.concatenate([table[at : at + 1] for at in range(table.shape[0])], axis=1)


def pack_labels(near, far, lines):
    pair = near + 3.0 * far
    packed = pair[0:lines]
    for k in range(1, pair.shape[0] // lines):
        packed = packed + float(9**k) * pair[lines * k : lines * (k + 1)]
    return packed


def unpack_labels(packed, rows):
    found = []
    for k in range(rows // packed.shape[0]):
        rest = jnp.floor((packed + 0.5) * (1.0 / 9.0))
        found.append(packed - 9.0 * rest)
        packed = rest
    return part_pair(jnp.concatenate(found, axis=0))


def part_pair(pair):
    far = jnp.floor((pair + 0.5) * (1.0 / 3.0))
    return pair - 3.0 * far, far


def from_slab(even_ref, odd_ref, start, stop):
    swap = lax.axis_index("slab") % 2 == 1
    even, odd = even_ref[start:stop].astype(jnp.float32), odd_ref[start:stop].astype(jnp.float32)
    return jnp.where(swap, odd, even), jnp.where(swap, even, odd)


def nearest_planes(even_ref, odd_ref):
    upper, lower = from_slab(even_ref, odd_ref, 0, LOW), from_slab(even_ref, odd_ref, LOW, FAR)
    return upper[0] + lower[0], upper[1] + lower[1]


def corner_kernel(even_in, odd_in, top_in, bottom_in, even_ref, odd_ref, top_ref, bottom_ref, sems):
    for copy in fetch([(even_in, even_ref), (odd_in, odd_ref), (top_in, top_ref), (bottom_in, bottom_ref)], sems):
        copy.wait()
    depth, width = top_ref.shape[1:]
    odd = lax.axis_index("slab") % 2 == 1
    line = lax.broadcasted_iota(jnp.int32, (16, width), 0)
    for ref, upward in ((even_ref, jnp.logical_not(odd)), (odd_ref, odd)):
        block = ref[CORNERS:].astype(jnp.float32)
        for k in range(4):
            edge_ref, low = (top_ref, bottom_ref)[k // 2], k % 2
            high = depth - 1 - low
            pair = jnp.where(upward, edge_ref[1, high : high + 1], edge_ref[1, low : low + 1])
            block = jnp.where(line == k, pair, block)
        ref[CORNERS:] = block.astype(jnp.bfloat16)


def beside(plane, lane):
    rows, width = plane.shape
    left = jnp.where(lane == 0, 0.0, pltpu.roll(plane, 1, 1))
    right = jnp.where(lane == width - 1, 0.0, pltpu.roll(plane, width - 1, 1))
    return left + right + pltpu.roll(plane, 1, 0) + pltpu.roll(plane, rows - 1, 0)


class Grid:
    def __init__(self, diffs, uptakes, labels, top_pairs, bottom_pairs, outside, conduct_ref, uptake_ref):
        self.conduct_ref, self.uptake_ref = conduct_ref, uptake_ref
        self.planes, rows, width = conduct_ref.shape
        own = labels[0].shape[0]
        row = lax.broadcasted_iota(jnp.int32, (rows, width), 0)
        self.lane = lax.broadcasted_iota(jnp.int32, (rows, width), 1)
        tile = lax.axis_index("tile")
        beyond = (row >= own + 2) & (row < rows - 2)
        beyond = beyond | ((row >= own) & (row < own + 4) & (tile == lax.axis_size("tile") - 1))
        beyond = beyond | ((row >= own + 4) & (tile == 0))
        blank = jnp.zeros((8, width), jnp.float32)
        for z, (label, top, bottom) in enumerate(zip(labels, top_pairs, bottom_pairs)):
            conduct_ref[z, :own] = label
            conduct_ref[z, own:] = blank
            near, far = part_pair(top)
            conduct_ref[z, own : own + 1] = near
            conduct_ref[z, own + 1 : own + 2] = far
            near, far = part_pair(bottom)
            conduct_ref[z, rows - 1 :] = near
            conduct_ref[z, rows - 2 : rows - 1] = far
            label = jnp.where(beyond | outside[z] if z in outside else beyond, -1.0, conduct_ref[z])
            conduct = jnp.zeros(label.shape, jnp.float32)
            uptake = jnp.zeros(label.shape, jnp.float32)
            for phase, (diff, upt) in enumerate(zip(diffs, uptakes)):
                conduct = jnp.where(label == float(phase), diff, conduct)
                uptake = jnp.where(label == float(phase), upt, uptake)
            conduct_ref[z] = conduct
            uptake_ref[z] = uptake

    def in_plane(self, z):
        rows, width = self.conduct_ref.shape[1:]
        plane = self.conduct_ref[z]
        return (
            jnp.where(self.lane == 0, 0.0, pltpu.roll(plane, 1, 1)),
            jnp.where(self.lane == width - 1, 0.0, pltpu.roll(plane, width - 1, 1)),
            pltpu.roll(plane, 1, 0),
            pltpu.roll(plane, rows - 1, 0),
        )


def ends():
    slab = lax.axis_index("slab")
    return slab == lax.axis_size("slab") - 1, slab == 0


def residual_kernel(*refs, direct):
    operands, outputs, scratch = refs[:12], refs[12:20], refs[20:]
    conduct_ref, uptake_ref, sol_ref = scratch[:3]
    local, sems = scratch[3:15], scratch[15]
    diff_ref, upt_ref, diag_ref, ids_ref = local[:4]
    off_ref, cols_ref, table_ref, sol_in, label_in, src_in, top_ref, bottom_ref = local[4:]
    res_ref, face_ref, plain_ref, packed_ref, tables_ref, column_ref, record_ref, scalar_ref = outputs
    for copy in fetch(list(zip(operands, local)), sems):
        copy.wait()
    own, depth, width = sol_in.shape
    rows = conduct_ref.shape[1]
    cells, nnz = off_ref.shape

    for phase in range(diff_ref.shape[0]):
        scalar_ref[0, phase] = jnp.full((8, 128), diff_ref[phase])
        scalar_ref[1, phase] = jnp.full((8, 128), upt_ref[phase])
    line = lax.broadcasted_iota(jnp.int32, record_ref.shape, 0)
    mine = jnp.zeros(record_ref.shape, jnp.int32)
    for cell in range(cells):
        mine = jnp.where(line == cell, ids_ref[cell], mine)
    scalar_ref[2, 0] = mine.astype(jnp.float32)
    record = jnp.zeros(record_ref.shape, jnp.float32)
    for cell in range(cells):
        record = jnp.where(line == cell, diag_ref[cell], record)
    record_ref[...] = record
    record_ref[:, :nnz] = off_ref[...]
    record_ref[:, COLS_LANE : COLS_LANE + nnz] = cols_ref[...].astype(jnp.float32)
    slots, capacity = table_ref.shape
    entries = slots * capacity
    table = flat(table_ref[...]).astype(jnp.float32)
    table = jnp.concatenate([table, jnp.zeros((1, 128 - entries), jnp.float32)], axis=1)
    if direct:
        table = shuffle(table, lax.axis_index("slab"), slots, capacity)
    table = jnp.broadcast_to(table, (8, 128))
    tables_ref[...] = table[:, :entries].astype(jnp.int32)
    column_ref[...] = jnp.transpose(table)[:entries].astype(jnp.int32)

    labels = []
    for start in range(0, depth, 8):
        block = jnp.transpose(label_in[:, start : start + 8, :].astype(jnp.float32), (1, 0, 2))
        labels = labels + [block[at] for at in range(8)]
    for k in range(depth // 2):
        packed_ref[k] = pack_labels(labels[2 * k], labels[2 * k + 1], 8)
    top_pairs = [top_ref[1, z : z + 1] for z in range(depth)]
    bottom_pairs = [bottom_ref[1, z : z + 1] for z in range(depth)]
    phases = range(diff_ref.shape[0])
    diffs, uptakes = [diff_ref[phase] for phase in phases], [upt_ref[phase] for phase in phases]
    grid = Grid(diffs, uptakes, labels, top_pairs, bottom_pairs, {}, conduct_ref, uptake_ref)
    blank = jnp.zeros((8, width), jnp.float32)
    for start in range(0, depth, 8):
        block = jnp.transpose(sol_in[:, start : start + 8, :], (1, 0, 2))
        for at in range(8):
            z = start + at
            plain_ref[z] = block[at]
            sol_ref[z, :own] = block[at]
            sol_ref[z, own:] = blank
            sol_ref[z, own : own + 1] = top_ref[0, z : z + 1]
            sol_ref[z, rows - 1 :] = bottom_ref[0, z : z + 1]
            sol_ref[z] = jnp.where(conduct_ref[z] > 0.0, sol_ref[z], 0.0)
    for start in range(0, depth, 8):
        block = jnp.transpose(src_in[:, start : start + 8, :], (1, 0, 2))
        for at in range(8):
            z = start + at
            conduct, value = conduct_ref[z], sol_ref[z]
            near = sum(grid.in_plane(z))
            diagonal = uptake_ref[z] + 2.0 * conduct + 0.5 * near
            flow = conduct * beside(value, grid.lane) + beside(conduct * value, grid.lane)
            applied = (diagonal * value - 0.5 * flow)[:own]
            conduct, value = conduct[:own], value[:own]
            for other in (z - 1, z + 1):
                if 0 <= other < depth:
                    applied = applied + 0.5 * (conduct + conduct_ref[other, :own]) * (value - sol_ref[other, :own])
            left = block[at] - applied
            res_ref[z] = left.astype(jnp.bfloat16)
            if z in (0, depth - 1):
                side = 0 if z == 0 else 3
                face_ref[side] = left
                face_ref[side + 1] = conduct
                face_ref[side + 2] = value


def phase_rows(scalar_ref, kind, width):
    found = []
    for phase in range(scalar_ref.shape[1]):
        row = scalar_ref[kind, phase, 0:1]
        found.append(jnp.concatenate([row] * (width // row.shape[1]), axis=1))
    return found


def weigh_kernel(
    scalar_ref, packed_ref, src_in, even_ref, odd_ref, top_ref, bottom_ref, weight_ref,
    conduct_ref, uptake_ref,
):
    own, depth, width = src_in.shape
    planes, rows = conduct_ref.shape[0:2]
    labels = []
    for k in range(depth // 2):
        labels = labels + list(unpack_labels(packed_ref[k], own))
    high, low = from_slab(even_ref, odd_ref, LABELS, CORNERS)
    (high_near, high_far), (low_near, low_far) = unpack_labels(high, own), unpack_labels(low, own)
    labels = labels + [high_near, high_far, low_far, low_near]
    high, low = from_slab(even_ref, odd_ref, CORNERS, MESSAGE)
    top_pairs = [top_ref[1, z : z + 1] for z in range(depth)] + [high[0:1], high[1:2], low[1:2], low[0:1]]
    bottom_pairs = [bottom_ref[1, z : z + 1] for z in range(depth)] + [high[2:3], high[3:4], low[3:4], low[2:3]]
    above, below = ends()
    outside = {depth: above, depth + 1: above, depth + 2: below, depth + 3: below}
    diffs, uptakes = phase_rows(scalar_ref, 0, width), phase_rows(scalar_ref, 1, width)
    grid = Grid(diffs, uptakes, labels, top_pairs, bottom_pairs, outside, conduct_ref, uptake_ref)
    blank = jnp.zeros((8, width), jnp.float32)
    outer = dict(zip((depth, planes - 1), from_slab(even_ref, odd_ref, SOURCE, LABELS)))
    for start in (0, 8, planes - 1, depth):
        if start < depth:
            block = jnp.transpose(src_in[:, start : start + 8, :], (1, 0, 2))
            sources = {start + at: block[at] for at in range(8)}
        else:
            sources = {start: outer[start]}
        for z, source in sources.items():
            conduct = conduct_ref[z]
            near = grid.in_plane(z) + (conduct_ref[(z - 1) % planes], conduct_ref[(z + 1) % planes])
            diagonal = uptake_ref[z] + 3.0 * conduct + 0.5 * sum(near[1:], near[0])
            inside = conduct > 0.0
            scale = jnp.where(inside, OMEGA / jnp.where(inside, diagonal, 1.0), 0.0)
            for k, other in enumerate(near):
                weight_ref[k, z] = jnp.where(other > 0.0, 0.5 * scale * (conduct + other), 0.0)
            weight_ref[6, z, :own] = scale[:own] * source
            weight_ref[6, z, own:] = blank
            if z < depth:
                weight_ref[6, z, own : own + 1] = scale[own : own + 1] * top_ref[2, z : z + 1]
                weight_ref[6, z, rows - 1 :] = scale[rows - 1 :] * bottom_ref[2, z : z + 1]


def rows_of(basis, start, size):
    parts = [ref[:, start : start + size].astype(jnp.float32) for ref in basis]
    return parts[0] if len(parts) == 1 else jnp.concatenate(parts, axis=0)


def owners_of(basis):
    tail = rows_of(basis, basis[0].shape[1] - 128, 128)
    return [
        (tail[:, 2 * k : 2 * k + 1] + 256.0 * tail[:, 2 * k + 1 : 2 * k + 2]).astype(jnp.int32)
        for k in range(3)
    ]


def restrict_kernel(scalar_ref, column_ref, record_ref, even_ref, odd_ref, face_ref, res_ref, *refs):
    basis, out_ref = refs[-2::-1], refs[-1]
    depth, own, width = res_ref.shape
    entries = column_ref.shape[0]
    pick = column_ref[:, 0:1] == lax.broadcasted_iota(jnp.int32, (entries, own), 1)
    pick = jnp.where(pick, 1.0, 0.0).astype(jnp.bfloat16)
    values = nearest_planes(even_ref, odd_ref)
    packed = from_slab(even_ref, odd_ref, LABELS, CORNERS)
    diffs = phase_rows(scalar_ref, 0, width)
    faces = {}
    for z, side, at in ((0, 0, 1), (depth - 1, 3, 0)):
        label = unpack_labels(packed[at], own)[0]
        beyond = jnp.zeros(label.shape, jnp.float32)
        for phase, diff in enumerate(diffs):
            beyond = jnp.where(label == float(phase), diff, beyond)
        beyond = jnp.where(ends()[at], 0.0, beyond)
        value = jnp.where(ends()[at], 0.0, values[at])
        applied = 0.5 * (face_ref[side + 1] + beyond) * (face_ref[side + 2] - value)
        faces[z] = (face_ref[side] - applied).astype(jnp.bfloat16)
    total = jnp.zeros((entries, width), jnp.float32)
    for z in range(depth):
        plane = faces[z] if z in faces else res_ref[z]
        piece = jnp.dot(pick, plane, preferred_element_type=jnp.float32)
        total = total + piece * rows_of(basis, z * width, width)
    product = jnp.sum(total, axis=1, keepdims=True)
    ident = owners_of(basis)[0]
    copies, lines, lanes = out_ref.shape
    lane = lax.broadcasted_iota(jnp.int32, (entries, lanes), 1)
    line = lax.broadcasted_iota(jnp.int32, (8, lanes), 0)
    for base in range(0, lines, 8):
        block = record_ref[...] if base == 0 else jnp.zeros((8, lanes), jnp.float32)
        for row in range(8):
            share = jnp.where(ident == (base + row) * HALF + lane - HALF, product, 0.0)
            share = jnp.sum(jnp.where(lane >= HALF, share, 0.0), axis=0, keepdims=True)
            block = jnp.where((line == row) & (lane[:8] >= HALF), share, block)

        def put(copy, carry):
            out_ref[copy, base : base + 8, :] = block
            return carry

        lax.fori_loop(0, copies, put, 0, unroll=8)


def solve(got_ref, count, nnz):
    devices, lines, lanes = got_ref.shape
    summed = got_ref[0]
    if devices <= 64:
        for device in range(1, devices):
            summed = summed + got_ref[device]
    else:
        summed = lax.fori_loop(1, devices, lambda d, total: total + got_ref[d], summed)
    rhs = jnp.concatenate([summed[at : at + 1, HALF:] for at in range(count // HALF)], axis=1)
    record = jnp.transpose(got_ref[:, 0:8, :].reshape(count, lanes))
    line = lax.broadcasted_iota(jnp.int32, (COLS_LANE, lanes), 0)
    inverse = 1.0 / record[DIAG_LANE : DIAG_LANE + 1]
    chunks = range(0, count, lanes)
    values = [jnp.where(line < nnz, record[:COLS_LANE, at : at + lanes], 0.0) for at in chunks]
    places = [
        jnp.where(line < nnz, record[COLS_LANE : 2 * COLS_LANE, at : at + lanes], 0.0).astype(jnp.int32)
        for at in chunks
    ]
    state = rhs * inverse
    for repeat in range(COARSE_SWEEPS - 1):
        sources = [jnp.broadcast_to(state[:, at : at + lanes], (COLS_LANE, lanes)) for at in chunks]
        pulled = []
        for value, place in zip(values, places):
            found = jnp.zeros((COLS_LANE, lanes), jnp.float32)
            for k, source in enumerate(sources):
                taken = jnp.take_along_axis(source, place % lanes, axis=1, mode="promise_in_bounds")
                found = jnp.where(place // lanes == k, taken, found)
            pulled.append(jnp.sum(value * found, axis=0, keepdims=True))
        state = (rhs - jnp.concatenate(pulled, axis=1)) * inverse
    return state


def prolong_kernel(scalar_ref, tables_ref, even_ref, odd_ref, got_ref, plain_ref, *refs, nnz):
    basis = refs[-5::-1]
    cor_ref, top_ref, bottom_ref, correction_ref = refs[-4:]
    planes, own, width = cor_ref.shape
    depth = plain_ref.shape[0]
    entries = tables_ref.shape[1]
    cells = correction_ref.shape[1]
    count = cells * got_ref.shape[0]
    state = solve(got_ref, count, nnz)
    line = lax.broadcasted_iota(jnp.int32, (cells, 1), 0)
    mine = scalar_ref[2, 0, :, 0:1].astype(jnp.int32)

    def look_up(ident):
        hit = ident == lax.broadcasted_iota(jnp.int32, (ident.shape[0], count), 1)
        return jnp.sum(jnp.where(hit, state, 0.0), axis=1, keepdims=True)

    diagonal = line == lax.broadcasted_iota(jnp.int32, (cells, cells), 1)
    correction_ref[...] = jnp.sum(jnp.where(diagonal, look_up(mine), 0.0), axis=0, keepdims=True)
    near_high, near_low = nearest_planes(even_ref, odd_ref)
    far_high, far_low = from_slab(even_ref, odd_ref, FAR, SOURCE)
    wide = {depth: near_high, depth + 1: far_high, depth + 2: far_low, depth + 3: near_low}
    high, low = from_slab(even_ref, odd_ref, CORNERS, MESSAGE)
    line = TABLE - CORNERS
    table_high, table_low = high[line : line + 1, :entries], low[line : line + 1, :entries]
    tables = (tables_ref[0:1], table_high.astype(jnp.int32), table_low.astype(jnp.int32))
    base = depth * width
    owners = owners_of(basis)
    for group, owner in enumerate(owners):
        pick = tables[group] == lax.broadcasted_iota(jnp.int32, (own, entries), 0)
        pick = jnp.where(pick, 1.0, 0.0).astype(jnp.bfloat16)
        factor = look_up(owner)
        if group == 0:
            places = [(z, z * width) for z in range(depth)]
        else:
            at = depth + 2 * (group - 1)
            places = [(at + k, base + (at + k - depth) * width) for k in range(2)]
        for z, start in places:
            part = (rows_of(basis, start, width) * factor).astype(jnp.bfloat16)
            added = jnp.dot(pick, part, preferred_element_type=jnp.float32)
            value = (plain_ref[z] if z < depth else wide[z]) + added
            cor_ref[z] = value
            top_ref[z] = value[:2]
            bottom_ref[z] = value[own - 2 :]


def smooth_kernel(cor_ref, top_ref, bottom_ref, weight_ref, out_hbm, ext_ref, mid_ref, out_ref, sems):
    planes, rows, width = ext_ref.shape
    own, depth, unused = out_ref.shape
    blank = jnp.zeros((8, width), jnp.float32)
    for z in range(planes):
        ext_ref[z, :own] = cor_ref[z]
        ext_ref[z, own:] = blank
        ext_ref[z, own : own + 2] = top_ref[z]
        ext_ref[z, rows - 2 :] = bottom_ref[z]

    def sweep(ref, z, upto):
        value = ref[z]
        near = (
            pltpu.roll(value, 1, 1)[:upto],
            pltpu.roll(value, width - 1, 1)[:upto],
            pltpu.roll(value, 1, 0)[:upto],
            pltpu.roll(value, rows - 1, 0)[:upto],
            ref[(z - 1) % planes, :upto],
            ref[(z + 1) % planes, :upto],
        )
        total = (1.0 - OMEGA) * value[:upto] + weight_ref[6, z, :upto]
        for k in range(6):
            total = total + weight_ref[k, z, :upto] * near[k]
        return total

    for z in [planes - 1] + list(range(depth + 1)):
        mid_ref[z] = sweep(ext_ref, z, rows)
    copies = []
    for start in range(0, depth, 8):
        for z in range(start, start + 8):
            ext_ref[z, :own] = sweep(mid_ref, z, own)
        out_ref[:, start : start + 8, :] = jnp.transpose(ext_ref[start : start + 8, :own], (1, 0, 2))
        part = pl.ds(start, 8)
        copies.append(pltpu.make_async_copy(out_ref.at[:, part], out_hbm.at[:, part], sems.at[start // 8]))
        copies[-1].start()
    for copy in copies:
        copy.wait()


def shards(
    solution,
    source,
    phase_label,
    phase_diffusivity,
    phase_uptake,
    send_tiles,
    support_slot,
    support_len,
    coarse_ids,
    basis_values,
    coarse_diag,
    coarse_off,
    coarse_cols,
):
    f32, i32, bf16 = jnp.float32, jnp.int32, jnp.bfloat16
    rows, depth, width = solution.shape
    voxels = depth * width
    slabs, tiles = lax.axis_size("slab"), lax.axis_size("tile")
    devices = slabs * tiles
    capacity = send_tiles.shape[3]
    cells, support, unused = basis_values.shape
    entries = cells * support
    count = cells * devices
    nnz = coarse_off.shape[1]
    shape = jax.ShapeDtypeStruct
    planes, tall = depth + 4, rows + 8
    block = (rows, depth, width)
    table = send_tiles.reshape(slabs, capacity)
    wide = voxels + 4 * width + 128

    def pinned(*arrays):
        return [pltpu.with_memory_space_constraint(array, pltpu.HBM) for array in arrays]

    direct = False
    parts = slabs if direct else 1
    outgoing = pl.pallas_call(
        functools.partial(sort_kernel, capacity=capacity),
        out_shape=(shape((entries // parts, wide), bf16),) * parts,
        in_specs=[HBM] * 4,
        out_specs=(VMEM,) * parts,
        scratch_shapes=[
            pltpu.VMEM((1, entries), i32),
            pltpu.SMEM((cells,), i32),
            pltpu.SMEM((cells,), i32),
            pltpu.VMEM((entries, voxels), bf16),
            pltpu.SemaphoreType.DMA((7,)),
        ],
        compiler_params=params(12),
        name="sort_basis",
    )(
        *pinned(
            support_slot.reshape(1, entries),
            support_len.reshape(cells),
            coarse_ids,
            basis_values.reshape(entries, voxels),
        )
    )
    if direct:
        basis = [
            lax.ppermute(outgoing[s], "slab", [(i, i ^ s) for i in range(slabs)]) for s in range(slabs - 1, 0, -1)
        ] + [outgoing[0]]
    else:
        basis = lax.all_to_all(
            outgoing[0].reshape(slabs, capacity, wide), "slab", split_axis=0, concat_axis=0, tiled=True
        )
        basis = [basis.reshape(entries, wide)]
    outgoing, solution, phase_label, source, table = lax.optimization_barrier(
        (outgoing, solution, phase_label, source, table)
    )
    message = shape((MESSAGE, width), bf16)
    edge = shape((3, depth, width), f32)
    even, odd, top, bottom = pl.pallas_call(
        functools.partial(border_kernel, direct=direct),
        out_shape=(message, message, edge, edge),
        in_specs=[HBM] * 4,
        out_specs=(VMEM,) * 4,
        scratch_shapes=[
            pltpu.VMEM(block, f32),
            pltpu.VMEM(block, i32),
            pltpu.VMEM(block, f32),
            pltpu.VMEM((slabs, capacity), i32),
            pltpu.SemaphoreType.DMA((4,)),
        ],
        compiler_params=params(8),
        name="border",
    )(*pinned(solution, phase_label, source, table))
    top = lax.ppermute(top, "tile", wheel(tiles, -1))
    bottom = lax.ppermute(bottom, "tile", wheel(tiles, 1))
    even, odd = pl.pallas_call(
        corner_kernel,
        out_shape=(message, message),
        in_specs=[HBM] * 4,
        out_specs=(VMEM,) * 2,
        scratch_shapes=[pltpu.VMEM(edge.shape, f32)] * 2 + [pltpu.SemaphoreType.DMA((4,))],
        compiler_params=params(8),
        name="corner",
    )(even, odd, top, bottom)
    even = lax.ppermute(even, "slab", pairs(slabs, False))
    odd = lax.ppermute(odd, "slab", pairs(slabs, True))
    row_top, row_bottom = top, bottom

    wide_block = pltpu.VMEM((planes, tall, width), f32)
    operands = [
        phase_diffusivity, phase_uptake, coarse_diag, coarse_ids, coarse_off, coarse_cols, table,
        solution, phase_label, source, top, bottom,
    ]
    phases = phase_diffusivity.shape[0]
    residual, face, plain, packed, tables, column, record, scalars = pl.pallas_call(
        functools.partial(residual_kernel, direct=direct),
        out_shape=(
            shape((depth, rows, width), bf16),
            shape((6, rows, width), f32),
            shape((depth, rows, width), f32),
            shape((depth // 2, 8, width), f32),
            shape((8, entries), i32),
            shape((entries, 8), i32),
            shape((cells, 128), f32),
            shape((3, phases, 8, 128), f32),
        ),
        in_specs=[HBM] * 12,
        out_specs=(VMEM,) * 8,
        scratch_shapes=[pltpu.VMEM((depth, tall, width), f32)] * 3
        + [pltpu.SMEM(array.shape, array.dtype) for array in operands[:4]]
        + [pltpu.VMEM(array.shape, array.dtype) for array in operands[4:]]
        + [pltpu.SemaphoreType.DMA((12,))],
        compiler_params=params(12),
        name="residual",
    )(*pinned(*operands[:10]), *operands[10:])

    lines = max(8, count // HALF)
    payload = pl.pallas_call(
        restrict_kernel,
        out_shape=shape((devices, lines, 128), f32),
        in_specs=[VMEM] * (7 + parts),
        out_specs=VMEM,
        compiler_params=params(8),
        name="restrict",
    )(scalars, column, record, even, odd, face, residual, *basis)
    got = lax.all_to_all(payload, ("slab", "tile"), split_axis=0, concat_axis=0, tiled=True)

    edge = shape((planes, 2, width), f32)
    corrected, top, bottom, coarse_correction = pl.pallas_call(
        functools.partial(prolong_kernel, nnz=nnz),
        out_shape=(shape((planes, rows, width), f32), edge, edge, shape((1, cells), f32)),
        in_specs=[VMEM] * (6 + parts),
        out_specs=(VMEM, VMEM, VMEM, VMEM),
        compiler_params=params(12 + count * count // (8 * MIB)),
        name="prolong",
    )(scalars, tables, even, odd, got, plain, *basis)
    corrected, packed = lax.optimization_barrier((corrected, packed))
    weights = pl.pallas_call(
        weigh_kernel,
        out_shape=shape((7, planes, tall, width), f32),
        in_specs=[VMEM] * 7,
        out_specs=VMEM,
        scratch_shapes=[wide_block] * 2,
        compiler_params=params(12),
        name="weigh",
    )(scalars, packed, source, even, odd, row_top, row_bottom)
    top = lax.ppermute(top, "tile", wheel(tiles, -1))
    bottom = lax.ppermute(bottom, "tile", wheel(tiles, 1))
    smooth = pl.pallas_call(
        smooth_kernel,
        out_shape=shape((rows, depth, width), f32),
        in_specs=[VMEM] * 4,
        out_specs=HBM,
        scratch_shapes=[wide_block] * 2 + [pltpu.VMEM(block, f32), pltpu.SemaphoreType.DMA((depth // 8,))],
        compiler_params=params(16),
        name="smooth",
    )(corrected, top, bottom, weights)
    return smooth, coarse_correction.reshape(cells)


def solution(mesh):
    placed = (
        P("tile", "slab", None),
        P("tile", "slab", None),
        P("tile", "slab", None),
        P(),
        P(),
        P("slab", "tile", None, None),
        P("slab", "tile", None),
        P("slab", "tile", None),
        P(("slab", "tile")),
        P(("slab", "tile"), None, None),
        P(("slab", "tile")),
        P(("slab", "tile"), None),
        P(("slab", "tile"), None),
    )
    return jax.shard_map(
        shards,
        mesh=mesh,
        in_specs=placed,
        out_specs=(P("tile", "slab", None), P(("slab", "tile"))),
        check_vma=False,
    )
```

```python
import functools

import jax
import jax.numpy as jnp
from jax import lax
from jax.experimental import pallas as pl
from jax.experimental.pallas import tpu as pltpu
from jax.sharding import PartitionSpec as P

COARSE_SWEEPS = 4
SMOOTH_SWEEPS = 2
OMEGA = 0.8

VMEM = pl.BlockSpec(memory_space=pltpu.VMEM)
SMEM = pl.BlockSpec(memory_space=pltpu.SMEM)
HBM = pl.BlockSpec(memory_space=pltpu.HBM)
MIB = 1024 * 1024
HALF, SECOND, COLS, DIAG, PLACE, SUMS = 64, 16, 32, 46, 47, 48
BASE = 4096


def place_of(index, count):
    row = index % 8
    return row // 4 * (count // 2) + index // 8 * 4 + row % 4


def params(mib=16):
    return pltpu.CompilerParams(vmem_limit_bytes=mib * MIB)


def wheel(count, step):
    return [(i, (i + step) % count) for i in range(count)]


def pairs(count, odd):
    start = 1 if odd else 0
    table = list(range(count))
    for i in range(start, count - 1, 2):
        table[i], table[i + 1] = i + 1, i
    return list(enumerate(table))


def fetch(pairs_of_refs, sems):
    copies = [
        pltpu.make_async_copy(source, target, sems.at[k])
        for k, (source, target) in enumerate(pairs_of_refs)
    ]
    for copy in copies:
        copy.start()
    return copies


def sort_kernel(slot_hbm, len_hbm, ids_hbm, basis_hbm, *refs, capacity, count):
    slot_ref, len_ref, ids_ref, basis_ref, sems = refs[-5:]
    outs = refs[:-5]
    entries, voxels = basis_ref.shape
    lines = entries // len(outs)
    cells = len_ref.shape[0]
    support = entries // cells
    wide = outs[0].shape[1]
    border = (wide - 128 - voxels) // 2
    chunk = voxels // 2
    pieces = [
        (basis_hbm.at[:, pl.ds(k * chunk, chunk)], basis_ref.at[:, pl.ds(k * chunk, chunk)]) for k in range(2)
    ]
    small = [(slot_hbm, slot_ref), (len_hbm, len_ref), (ids_hbm, ids_ref)]
    copies = fetch(small + pieces, sems)
    for copy in copies[:3]:
        copy.wait()
    lane = lax.broadcasted_iota(jnp.int32, (1, entries), 1)
    length = jnp.zeros((1, entries), jnp.int32)
    ident = jnp.zeros((1, entries), jnp.int32)
    for cell in range(cells):
        here = lane // support == cell
        length = jnp.where(here, len_ref[cell], length)
        ident = jnp.where(here, ids_ref[cell], ident)
    ident = place_of(ident, count)
    live = lane % support < length
    slot = jnp.where(live, slot_ref[...], -1)
    row = lax.broadcasted_iota(jnp.int32, (entries, entries), 0)
    if len(outs) > 1:
        row = row ^ (lax.axis_index("slab") * capacity)
    above = jnp.where(row >= entries - capacity, row + capacity - entries, row + capacity)
    below = jnp.where(row < capacity, row - capacity + entries, row - capacity)
    hits = [slot == row, slot == above, slot == below]
    picks = [jnp.where(hit, 1.0, 0.0).astype(jnp.bfloat16) for hit in hits]

    def put(block, start):
        for k, out in enumerate(outs):
            part = block[k * lines : (k + 1) * lines]
            out[:, start : start + block.shape[1]] = part.astype(jnp.bfloat16)

    def move(pick, start, size, target):
        block = basis_ref[:, start : start + size]
        put(jnp.dot(pick, block, preferred_element_type=jnp.float32), target)

    extra = lax.broadcasted_iota(jnp.int32, (entries, 128), 1)
    tail = jnp.zeros((entries, 128), jnp.float32)
    for k, hit in enumerate(hits):
        low = jnp.sum(jnp.where(hit, ident % 256, 0).astype(jnp.float32), axis=1, keepdims=True)
        high = jnp.sum(jnp.where(hit, ident // 256, 0).astype(jnp.float32), axis=1, keepdims=True)
        tail = jnp.where(extra == 2 * k, low, jnp.where(extra == 2 * k + 1, high, tail))
    cell = jnp.sum(jnp.where(hits[0], lane // support, 0).astype(jnp.float32), axis=1, keepdims=True)
    put(jnp.where(extra == 2 * len(hits), cell, tail), voxels + 2 * border)
    for k in range(2):
        copies[3 + k].wait()
        for start in range(k * chunk, (k + 1) * chunk, 512):
            move(picks[0], start, 512, start)
        if k == 0:
            move(picks[1], 0, border, voxels)
    move(picks[2], voxels - border, border, voxels + border)


def shuffle(table, slab, slots, capacity):
    lane = lax.broadcasted_iota(jnp.int32, table.shape, 1)
    size = table.shape[1]
    bit = 1
    while bit < slots:
        shift = bit * capacity
        other = jnp.where((lane // shift) % 2 == 1, pltpu.roll(table, shift, 1), pltpu.roll(table, size - shift, 1))
        table = jnp.where((slab // bit) % 2 == 1, other, table)
        bit *= 2
    return table


LOW, FAR, SOURCE, LABELS, CORNERS, TABLE = 32, 64, 96, 128, 144, 148
MESSAGE = 160


def border_kernel(
    sol_hbm, label_hbm, src_hbm, table_hbm, even_ref, odd_ref, top_ref, bottom_ref,
    sol_ref, label_ref, src_ref, table_ref, sems, *, direct,
):
    rows, depth, width = sol_ref.shape
    blocks = ((sol_hbm, sol_ref), (label_hbm, label_ref), (src_hbm, src_ref), (table_hbm, table_ref))
    for copy in fetch(blocks, sems):
        copy.wait()
    odd = lax.axis_index("slab") % 2 == 1

    def planes(start):
        parts = [ref[:, start : start + 2, :].astype(jnp.float32) for ref in (sol_ref, label_ref, src_ref, src_ref)]
        block = jnp.transpose(jnp.concatenate(parts, axis=1), (1, 0, 2))
        return [block[k] for k in range(6)]

    near, far, label, label_far, origin, unused = planes(0)
    down = near, far, origin, pack_labels(label, label_far, 16)
    far, near, label_far, label, unused, origin = planes(depth - 2)
    up = near, far, origin, pack_labels(label, label_far, 16)
    slots, capacity = table_ref.shape
    table = flat(table_ref[...]).astype(jnp.float32)
    table = jnp.concatenate([table, jnp.zeros((1, width - table.shape[1]), jnp.float32)], axis=1)
    tables = [table, table]
    if direct:
        slab, slabs = lax.axis_index("slab"), lax.axis_size("slab")
        tables = [shuffle(table, (slab + step) % slabs, slots, capacity) for step in (1, slabs - 1)]
    line = lax.broadcasted_iota(jnp.int32, (16, width), 0) + CORNERS
    up = up + (jnp.where(line == TABLE, tables[0], 0.0),)
    down = down + (jnp.where(line == TABLE, tables[1], 0.0),)
    for first, second, ref in ((up, down, even_ref), (down, up, odd_ref)):
        near, far, origin, labels, table = [jnp.where(odd, b, a) for a, b in zip(first, second)]
        high = near.astype(jnp.bfloat16)
        ref[:LOW] = high
        ref[LOW:FAR] = (near - high.astype(jnp.float32)).astype(jnp.bfloat16)
        ref[FAR:SOURCE] = far.astype(jnp.bfloat16)
        ref[SOURCE:LABELS] = origin.astype(jnp.bfloat16)
        ref[LABELS:CORNERS] = labels.astype(jnp.bfloat16)
        ref[CORNERS:] = table.astype(jnp.bfloat16)
    for ref, near, far in ((top_ref, 0, 1), (bottom_ref, rows - 1, rows - 2)):
        ref[0] = sol_ref[near]
        ref[1] = (label_ref[near] + 3 * label_ref[far]).astype(jnp.float32)
        ref[2] = src_ref[near]


def flat(table):
    return jnp.concatenate([table[at : at + 1] for at in range(table.shape[0])], axis=1)


def pack_labels(near, far, lines):
    pair = near + 3.0 * far
    packed = pair[0:lines]
    for k in range(1, pair.shape[0] // lines):
        packed = packed + float(9**k) * pair[lines * k : lines * (k + 1)]
    return packed


def unpack_labels(packed, rows):
    found = []
    for k in range(rows // packed.shape[0]):
        rest = jnp.floor((packed + 0.5) * (1.0 / 9.0))
        found.append(packed - 9.0 * rest)
        packed = rest
    return part_pair(jnp.concatenate(found, axis=0))


def part_pair(pair):
    far = jnp.floor((pair + 0.5) * (1.0 / 3.0))
    return pair - 3.0 * far, far


def from_slab(even_ref, odd_ref, start, stop):
    swap = lax.axis_index("slab") % 2 == 1
    even, odd = even_ref[start:stop].astype(jnp.float32), odd_ref[start:stop].astype(jnp.float32)
    return jnp.where(swap, odd, even), jnp.where(swap, even, odd)


def nearest_planes(even_ref, odd_ref):
    upper, lower = from_slab(even_ref, odd_ref, 0, LOW), from_slab(even_ref, odd_ref, LOW, FAR)
    return upper[0] + lower[0], upper[1] + lower[1]


def corner_kernel(even_in, odd_in, top_in, bottom_in, even_ref, odd_ref, top_ref, bottom_ref, sems):
    for copy in fetch([(even_in, even_ref), (odd_in, odd_ref), (top_in, top_ref), (bottom_in, bottom_ref)], sems):
        copy.wait()
    depth, width = top_ref.shape[1:]
    odd = lax.axis_index("slab") % 2 == 1
    line = lax.broadcasted_iota(jnp.int32, (16, width), 0)
    for ref, upward in ((even_ref, jnp.logical_not(odd)), (odd_ref, odd)):
        block = ref[CORNERS:].astype(jnp.float32)
        for k in range(4):
            edge_ref, low = (top_ref, bottom_ref)[k // 2], k % 2
            high = depth - 1 - low
            pair = jnp.where(upward, edge_ref[1, high : high + 1], edge_ref[1, low : low + 1])
            block = jnp.where(line == k, pair, block)
        ref[CORNERS:] = block.astype(jnp.bfloat16)


def beside(plane, lane):
    rows, width = plane.shape
    left = jnp.where(lane == 0, 0.0, pltpu.roll(plane, 1, 1))
    right = jnp.where(lane == width - 1, 0.0, pltpu.roll(plane, width - 1, 1))
    return left + right + pltpu.roll(plane, 1, 0) + pltpu.roll(plane, rows - 1, 0)


class Grid:
    def __init__(self, diffs, uptakes, labels, top_pairs, bottom_pairs, outside, conduct_ref, uptake_ref):
        self.conduct_ref, self.uptake_ref = conduct_ref, uptake_ref
        self.planes, rows, width = conduct_ref.shape
        own = labels[0].shape[0]
        row = lax.broadcasted_iota(jnp.int32, (rows, width), 0)
        self.lane = lax.broadcasted_iota(jnp.int32, (rows, width), 1)
        tile = lax.axis_index("tile")
        beyond = (row >= own + 2) & (row < rows - 2)
        beyond = beyond | ((row >= own) & (row < own + 4) & (tile == lax.axis_size("tile") - 1))
        beyond = beyond | ((row >= own + 4) & (tile == 0))
        blank = jnp.zeros((8, width), jnp.float32)
        for z, (label, top, bottom) in enumerate(zip(labels, top_pairs, bottom_pairs)):
            conduct_ref[z, :own] = label
            conduct_ref[z, own:] = blank
            near, far = part_pair(top)
            conduct_ref[z, own : own + 1] = near
            conduct_ref[z, own + 1 : own + 2] = far
            near, far = part_pair(bottom)
            conduct_ref[z, rows - 1 :] = near
            conduct_ref[z, rows - 2 : rows - 1] = far
            label = jnp.where(beyond | outside[z] if z in outside else beyond, -1.0, conduct_ref[z])
            conduct = jnp.zeros(label.shape, jnp.float32)
            uptake = jnp.zeros(label.shape, jnp.float32)
            for phase, (diff, upt) in enumerate(zip(diffs, uptakes)):
                conduct = jnp.where(label == float(phase), diff, conduct)
                uptake = jnp.where(label == float(phase), upt, uptake)
            conduct_ref[z] = conduct
            uptake_ref[z] = uptake

    def in_plane(self, z):
        rows, width = self.conduct_ref.shape[1:]
        plane = self.conduct_ref[z]
        return (
            jnp.where(self.lane == 0, 0.0, pltpu.roll(plane, 1, 1)),
            jnp.where(self.lane == width - 1, 0.0, pltpu.roll(plane, width - 1, 1)),
            pltpu.roll(plane, 1, 0),
            pltpu.roll(plane, rows - 1, 0),
        )


def ends():
    slab = lax.axis_index("slab")
    return slab == lax.axis_size("slab") - 1, slab == 0


def residual_kernel(*refs, direct, count):
    operands, outputs, scratch = refs[:12], refs[12:20], refs[20:]
    conduct_ref, uptake_ref, sol_ref = scratch[:3]
    local, sems = scratch[3:15], scratch[15]
    diff_ref, upt_ref, diag_ref, ids_ref = local[:4]
    off_ref, cols_ref, table_ref, sol_in, label_in, src_in, top_ref, bottom_ref = local[4:]
    res_ref, face_ref, plain_ref, packed_ref, tables_ref, column_ref, record_ref, scalar_ref = outputs
    for copy in fetch(list(zip(operands, local)), sems):
        copy.wait()
    own, depth, width = sol_in.shape
    rows = conduct_ref.shape[1]
    cells, nnz = off_ref.shape

    for phase in range(diff_ref.shape[0]):
        scalar_ref[0, phase] = jnp.full((8, 128), diff_ref[phase])
        scalar_ref[1, phase] = jnp.full((8, 128), upt_ref[phase])
    line = lax.broadcasted_iota(jnp.int32, record_ref.shape, 0)
    mine = jnp.zeros(record_ref.shape, jnp.int32)
    for cell in range(cells):
        mine = jnp.where(line == cell, ids_ref[cell], mine)
    mine = place_of(mine, count).astype(jnp.float32)
    scalar_ref[2, 0] = mine
    lane = lax.broadcasted_iota(jnp.int32, record_ref.shape, 1)
    record = jnp.where(lane == PLACE, mine, 0.0)
    for cell in range(cells):
        record = jnp.where((line == cell) & (lane == DIAG), diag_ref[cell], record)
    record_ref[...] = record
    group = nnz // 2
    cols = place_of(cols_ref[...], count).astype(jnp.float32)
    record_ref[:, :group] = off_ref[:, :group]
    record_ref[:, SECOND : SECOND + group] = off_ref[:, group:]
    record_ref[:, COLS : COLS + group] = cols[:, :group] + float(BASE) * cols[:, group:]
    record = record_ref[...]
    record_ref[:4] = jnp.concatenate([record[:4, :HALF], record[4:, :HALF]], axis=1)
    slots, capacity = table_ref.shape
    entries = slots * capacity
    table = flat(table_ref[...]).astype(jnp.float32)
    table = jnp.concatenate([table, jnp.zeros((1, 128 - entries), jnp.float32)], axis=1)
    if direct:
        table = shuffle(table, lax.axis_index("slab"), slots, capacity)
    table = jnp.broadcast_to(table, (8, 128))
    tables_ref[...] = table[:, :entries].astype(jnp.int32)
    column_ref[...] = jnp.transpose(table)[:entries].astype(jnp.int32)

    labels = []
    for start in range(0, depth, 8):
        block = jnp.transpose(label_in[:, start : start + 8, :].astype(jnp.float32), (1, 0, 2))
        labels = labels + [block[at] for at in range(8)]
    for k in range(depth // 2):
        packed_ref[k] = pack_labels(labels[2 * k], labels[2 * k + 1], 8)
    top_pairs = [top_ref[1, z : z + 1] for z in range(depth)]
    bottom_pairs = [bottom_ref[1, z : z + 1] for z in range(depth)]
    phases = range(diff_ref.shape[0])
    diffs, uptakes = [diff_ref[phase] for phase in phases], [upt_ref[phase] for phase in phases]
    grid = Grid(diffs, uptakes, labels, top_pairs, bottom_pairs, {}, conduct_ref, uptake_ref)
    blank = jnp.zeros((8, width), jnp.float32)
    for start in range(0, depth, 8):
        block = jnp.transpose(sol_in[:, start : start + 8, :], (1, 0, 2))
        for at in range(8):
            z = start + at
            plain_ref[z] = block[at]
            sol_ref[z, :own] = block[at]
            sol_ref[z, own:] = blank
            sol_ref[z, own : own + 1] = top_ref[0, z : z + 1]
            sol_ref[z, rows - 1 :] = bottom_ref[0, z : z + 1]
            sol_ref[z] = jnp.where(conduct_ref[z] > 0.0, sol_ref[z], 0.0)
    for start in range(0, depth, 8):
        block = jnp.transpose(src_in[:, start : start + 8, :], (1, 0, 2))
        for at in range(8):
            z = start + at
            conduct, value = conduct_ref[z], sol_ref[z]
            near = sum(grid.in_plane(z))
            diagonal = uptake_ref[z] + 2.0 * conduct + 0.5 * near
            flow = conduct * beside(value, grid.lane) + beside(conduct * value, grid.lane)
            applied = (diagonal * value - 0.5 * flow)[:own]
            conduct, value = conduct[:own], value[:own]
            for other in (z - 1, z + 1):
                if 0 <= other < depth:
                    applied = applied + 0.5 * (conduct + conduct_ref[other, :own]) * (value - sol_ref[other, :own])
            left = block[at] - applied
            res_ref[z] = left.astype(jnp.bfloat16)
            if z in (0, depth - 1):
                side = 0 if z == 0 else 3
                face_ref[side] = left
                face_ref[side + 1] = conduct
                face_ref[side + 2] = value


def phase_rows(scalar_ref, kind, width):
    found = []
    for phase in range(scalar_ref.shape[1]):
        row = scalar_ref[kind, phase, 0:1]
        found.append(jnp.concatenate([row] * (width // row.shape[1]), axis=1))
    return found


def weigh_kernel(
    scalar_ref, packed_ref, src_in, even_ref, odd_ref, top_ref, bottom_ref, weight_ref,
    conduct_ref, uptake_ref,
):
    own, depth, width = src_in.shape
    planes, rows = conduct_ref.shape[0:2]
    labels = []
    for k in range(depth // 2):
        labels = labels + list(unpack_labels(packed_ref[k], own))
    high, low = from_slab(even_ref, odd_ref, LABELS, CORNERS)
    (high_near, high_far), (low_near, low_far) = unpack_labels(high, own), unpack_labels(low, own)
    labels = labels + [high_near, high_far, low_far, low_near]
    high, low = from_slab(even_ref, odd_ref, CORNERS, MESSAGE)
    top_pairs = [top_ref[1, z : z + 1] for z in range(depth)] + [high[0:1], high[1:2], low[1:2], low[0:1]]
    bottom_pairs = [bottom_ref[1, z : z + 1] for z in range(depth)] + [high[2:3], high[3:4], low[3:4], low[2:3]]
    above, below = ends()
    outside = {depth: above, depth + 1: above, depth + 2: below, depth + 3: below}
    diffs, uptakes = phase_rows(scalar_ref, 0, width), phase_rows(scalar_ref, 1, width)
    grid = Grid(diffs, uptakes, labels, top_pairs, bottom_pairs, outside, conduct_ref, uptake_ref)
    blank = jnp.zeros((8, width), jnp.float32)
    outer = dict(zip((depth, planes - 1), from_slab(even_ref, odd_ref, SOURCE, LABELS)))
    for start in (0, 8, planes - 1, depth):
        if start < depth:
            block = jnp.transpose(src_in[:, start : start + 8, :], (1, 0, 2))
            sources = {start + at: block[at] for at in range(8)}
        else:
            sources = {start: outer[start]}
        for z, source in sources.items():
            conduct = conduct_ref[z]
            near = grid.in_plane(z) + (conduct_ref[(z - 1) % planes], conduct_ref[(z + 1) % planes])
            diagonal = uptake_ref[z] + 3.0 * conduct + 0.5 * sum(near[1:], near[0])
            inside = conduct > 0.0
            scale = jnp.where(inside, OMEGA / jnp.where(inside, diagonal, 1.0), 0.0)
            for k, other in enumerate(near):
                weight_ref[k, z] = jnp.where(other > 0.0, 0.5 * scale * (conduct + other), 0.0)
            weight_ref[6, z, :own] = scale[:own] * source
            weight_ref[6, z, own:] = blank
            if z < depth:
                weight_ref[6, z, own : own + 1] = scale[own : own + 1] * top_ref[2, z : z + 1]
                weight_ref[6, z, rows - 1 :] = scale[rows - 1 :] * bottom_ref[2, z : z + 1]


def rows_of(basis, start, size):
    parts = [ref[:, start : start + size].astype(jnp.float32) for ref in basis]
    return parts[0] if len(parts) == 1 else jnp.concatenate(parts, axis=0)


def owners_of(basis):
    tail = rows_of(basis, basis[0].shape[1] - 128, 128)
    cell = tail[:, 6:7].astype(jnp.int32)
    return cell, [
        (tail[:, 2 * k : 2 * k + 1] + 256.0 * tail[:, 2 * k + 1 : 2 * k + 2]).astype(jnp.int32)
        for k in range(3)
    ]


def restrict_kernel(scalar_ref, column_ref, record_ref, even_ref, odd_ref, face_ref, res_ref, *refs, capacity):
    basis, out_ref = refs[:-1], refs[-1]
    depth, own, width = res_ref.shape
    entries = column_ref.shape[0]
    pick = column_ref[:, 0:1] == lax.broadcasted_iota(jnp.int32, (entries, own), 1)
    pick = jnp.where(pick, 1.0, 0.0).astype(jnp.bfloat16)
    values = nearest_planes(even_ref, odd_ref)
    packed = from_slab(even_ref, odd_ref, LABELS, CORNERS)
    diffs = phase_rows(scalar_ref, 0, width)
    faces = {}
    for z, side, at in ((0, 0, 1), (depth - 1, 3, 0)):
        label = unpack_labels(packed[at], own)[0]
        beyond = jnp.zeros(label.shape, jnp.float32)
        for phase, diff in enumerate(diffs):
            beyond = jnp.where(label == float(phase), diff, beyond)
        beyond = jnp.where(ends()[at], 0.0, beyond)
        value = jnp.where(ends()[at], 0.0, values[at])
        applied = 0.5 * (face_ref[side + 1] + beyond) * (face_ref[side + 2] - value)
        faces[z] = (face_ref[side] - applied).astype(jnp.bfloat16)
    total = jnp.zeros((entries, width), jnp.float32)
    for z in range(depth):
        plane = faces[z] if z in faces else res_ref[z]
        piece = jnp.dot(pick, plane, preferred_element_type=jnp.float32)
        total = total + piece * rows_of(basis, z * width, width)
    product = jnp.sum(total, axis=1, keepdims=True)
    cell, unused = owners_of(basis)
    copies, lines, lanes = out_ref.shape
    peer = lax.broadcasted_iota(jnp.int32, (entries, 1), 0) // capacity
    target = (peer // 8 * 4 + peer % 4) * lanes + peer % 8 // 4 * HALF + SUMS + cell
    lane = lax.broadcasted_iota(jnp.int32, (entries, lanes), 1)
    rows = []
    for line in range(lines):
        share = jnp.sum(jnp.where(target == line * lanes + lane, product, 0.0), axis=0, keepdims=True)
        rows.append(share + record_ref[line : line + 1] if line < 4 else share)
    block = jnp.concatenate(rows, axis=0)

    def put(copy, carry):
        out_ref[copy] = block
        return carry

    lax.fori_loop(0, copies, put, 0, unroll=8)


def solve(got, tiles):
    extent, lanes = got[0].shape
    turned = jnp.transpose(got[0][...])
    chunks = range(0, extent, lanes)
    owners = 4 * tiles
    line = lax.broadcasted_iota(jnp.int32, (8, lanes), 0)
    lane = lax.broadcasted_iota(jnp.int32, (8, lanes), 1)

    def left(block, by):
        return pltpu.roll(block, lanes - by, 1) if by else block

    rhs = [jnp.zeros((8, lanes), jnp.float32) for at in range(2 * len(chunks))]
    place = [lane + at * lanes for at in range(2 * len(chunks))]
    for t, ref in enumerate(got):
        total = ref[:owners]
        for at in range(owners, extent, owners):
            total = total + ref[at : at + owners]
        block = jnp.transpose(jnp.concatenate([total] * (lanes // owners), axis=0))
        value = jnp.zeros((8, lanes), jnp.float32)
        ident = jnp.zeros((8, lanes), jnp.float32)
        for half in range(2):
            total = block[half * HALF + SUMS : half * HALF + SUMS + 8]
            row = half * HALF + PLACE
            places = jnp.broadcast_to(turned[row : row + 1, t * lanes : (t + 1) * lanes], (8, lanes))
            for i in range(4):
                value = jnp.where(lane // owners == 4 * half + i, left(total, i), value)
                ident = jnp.where(line == 4 * half + i, left(places, i), ident)
        ident = ident.astype(jnp.int32)
        for at in range(0, lanes, 4):
            here, amount = ident[:, at : at + 1], value[:, at : at + 1]
            rhs = [total + jnp.where(here == spot, amount, 0.0) for total, spot in zip(rhs, place)]
    rhs = [jnp.sum(total, axis=0, keepdims=True) for total in rhs]

    values, places, inverse = [], [], []
    for half in range(2):
        for at in chunks:
            block = turned[half * HALF : (half + 1) * HALF, at : at + lanes]
            values.append(block[:COLS])
            packed = block[COLS : COLS + SECOND]
            second = jnp.floor(packed * (1.0 / BASE))
            first = packed - float(BASE) * second
            places.append(jnp.concatenate([first, second], axis=0).astype(jnp.int32) % (2 * extent))
            inverse.append(1.0 / block[DIAG : DIAG + 1])
    state = [total * factor for total, factor in zip(rhs, inverse)]
    for repeat in range(COARSE_SWEEPS - 1):
        sources = [jnp.broadcast_to(part, (COLS, lanes)) for part in state]
        new = []
        for total, factor, value, spot in zip(rhs, inverse, values, places):
            found = jnp.zeros((COLS, lanes), jnp.float32)
            for k, source in enumerate(sources):
                taken = jnp.take_along_axis(source, spot % lanes, axis=1, mode="promise_in_bounds")
                found = jnp.where(spot // lanes == k, taken, found)
            new.append((total - jnp.sum(value * found, axis=0, keepdims=True)) * factor)
        state = new
    return jnp.concatenate(state, axis=1)


def prolong_kernel(scalar_ref, tables_ref, even_ref, odd_ref, plain_ref, *refs, groups):
    got, basis = refs[:groups], refs[groups:-4]
    cor_ref, top_ref, bottom_ref, correction_ref = refs[-4:]
    planes, own, width = cor_ref.shape
    depth = plain_ref.shape[0]
    entries = tables_ref.shape[1]
    cells = correction_ref.shape[1]
    count = 2 * got[0].shape[0]
    state = solve(got, lax.axis_size("tile"))
    line = lax.broadcasted_iota(jnp.int32, (cells, 1), 0)
    mine = scalar_ref[2, 0, :, 0:1].astype(jnp.int32)

    def look_up(ident):
        hit = ident == lax.broadcasted_iota(jnp.int32, (ident.shape[0], count), 1)
        return jnp.sum(jnp.where(hit, state, 0.0), axis=1, keepdims=True)

    diagonal = line == lax.broadcasted_iota(jnp.int32, (cells, cells), 1)
    correction_ref[...] = jnp.sum(jnp.where(diagonal, look_up(mine), 0.0), axis=0, keepdims=True)
    near_high, near_low = nearest_planes(even_ref, odd_ref)
    far_high, far_low = from_slab(even_ref, odd_ref, FAR, SOURCE)
    wide = {depth: near_high, depth + 1: far_high, depth + 2: far_low, depth + 3: near_low}
    high, low = from_slab(even_ref, odd_ref, CORNERS, MESSAGE)
    line = TABLE - CORNERS
    table_high, table_low = high[line : line + 1, :entries], low[line : line + 1, :entries]
    tables = (tables_ref[0:1], table_high.astype(jnp.int32), table_low.astype(jnp.int32))
    base = depth * width
    unused, owners = owners_of(basis)
    for group, owner in enumerate(owners):
        pick = tables[group] == lax.broadcasted_iota(jnp.int32, (own, entries), 0)
        pick = jnp.where(pick, 1.0, 0.0).astype(jnp.bfloat16)
        factor = look_up(owner)
        if group == 0:
            places = [(z, z * width) for z in range(depth)]
        else:
            at = depth + 2 * (group - 1)
            places = [(at + k, base + (at + k - depth) * width) for k in range(2)]
        for z, start in places:
            part = (rows_of(basis, start, width) * factor).astype(jnp.bfloat16)
            added = jnp.dot(pick, part, preferred_element_type=jnp.float32)
            value = (plain_ref[z] if z < depth else wide[z]) + added
            cor_ref[z] = value
            top_ref[z] = value[:2]
            bottom_ref[z] = value[own - 2 :]


def smooth_kernel(cor_ref, top_ref, bottom_ref, weight_ref, out_hbm, ext_ref, mid_ref, out_ref, sems):
    planes, rows, width = ext_ref.shape
    own, depth, unused = out_ref.shape
    blank = jnp.zeros((8, width), jnp.float32)
    for z in range(planes):
        ext_ref[z, :own] = cor_ref[z]
        ext_ref[z, own:] = blank
        ext_ref[z, own : own + 2] = top_ref[z]
        ext_ref[z, rows - 2 :] = bottom_ref[z]

    def sweep(ref, z, upto):
        value = ref[z]
        near = (
            pltpu.roll(value, 1, 1)[:upto],
            pltpu.roll(value, width - 1, 1)[:upto],
            pltpu.roll(value, 1, 0)[:upto],
            pltpu.roll(value, rows - 1, 0)[:upto],
            ref[(z - 1) % planes, :upto],
            ref[(z + 1) % planes, :upto],
        )
        total = (1.0 - OMEGA) * value[:upto] + weight_ref[6, z, :upto]
        for k in range(6):
            total = total + weight_ref[k, z, :upto] * near[k]
        return total

    for z in [planes - 1] + list(range(depth + 1)):
        mid_ref[z] = sweep(ext_ref, z, rows)
    copies = []
    for start in range(0, depth, 8):
        for z in range(start, start + 8):
            ext_ref[z, :own] = sweep(mid_ref, z, own)
        out_ref[:, start : start + 8, :] = jnp.transpose(ext_ref[start : start + 8, :own], (1, 0, 2))
        part = pl.ds(start, 8)
        copies.append(pltpu.make_async_copy(out_ref.at[:, part], out_hbm.at[:, part], sems.at[start // 8]))
        copies[-1].start()
    for copy in copies:
        copy.wait()


def shards(
    solution,
    source,
    phase_label,
    phase_diffusivity,
    phase_uptake,
    send_tiles,
    support_slot,
    support_len,
    coarse_ids,
    basis_values,
    coarse_diag,
    coarse_off,
    coarse_cols,
):
    f32, i32, bf16 = jnp.float32, jnp.int32, jnp.bfloat16
    rows, depth, width = solution.shape
    voxels = depth * width
    slabs, tiles = lax.axis_size("slab"), lax.axis_size("tile")
    devices = slabs * tiles
    capacity = send_tiles.shape[3]
    cells, support, unused = basis_values.shape
    entries = cells * support
    count = cells * devices
    nnz = coarse_off.shape[1]
    shape = jax.ShapeDtypeStruct
    planes, tall = depth + 4, rows + 8
    block = (rows, depth, width)
    table = send_tiles.reshape(slabs, capacity)
    wide = voxels + 4 * width + 128

    def pinned(*arrays):
        return [pltpu.with_memory_space_constraint(array, pltpu.HBM) for array in arrays]

    direct = False
    parts = slabs if direct else 1
    outgoing = pl.pallas_call(
        functools.partial(sort_kernel, capacity=capacity, count=count),
        out_shape=(shape((entries // parts, wide), bf16),) * parts,
        in_specs=[HBM] * 4,
        out_specs=(VMEM,) * parts,
        scratch_shapes=[
            pltpu.VMEM((1, entries), i32),
            pltpu.SMEM((cells,), i32),
            pltpu.SMEM((cells,), i32),
            pltpu.VMEM((entries, voxels), bf16),
            pltpu.SemaphoreType.DMA((7,)),
        ],
        compiler_params=params(12),
        name="sort_basis",
    )(
        *pinned(
            support_slot.reshape(1, entries),
            support_len.reshape(cells),
            coarse_ids,
            basis_values.reshape(entries, voxels),
        )
    )
    if direct:
        basis = [
            lax.ppermute(outgoing[s], "slab", [(i, i ^ s) for i in range(slabs)]) for s in range(slabs - 1, 0, -1)
        ] + [outgoing[0]]
    else:
        basis = lax.all_to_all(
            outgoing[0].reshape(slabs, capacity, wide), "slab", split_axis=0, concat_axis=0, tiled=True
        )
        basis = [basis.reshape(entries, wide)]
    outgoing, solution, phase_label, source, table = lax.optimization_barrier(
        (outgoing, solution, phase_label, source, table)
    )
    message = shape((MESSAGE, width), bf16)
    edge = shape((3, depth, width), f32)
    even, odd, top, bottom = pl.pallas_call(
        functools.partial(border_kernel, direct=direct),
        out_shape=(message, message, edge, edge),
        in_specs=[HBM] * 4,
        out_specs=(VMEM,) * 4,
        scratch_shapes=[
            pltpu.VMEM(block, f32),
            pltpu.VMEM(block, i32),
            pltpu.VMEM(block, f32),
            pltpu.VMEM((slabs, capacity), i32),
            pltpu.SemaphoreType.DMA((4,)),
        ],
        compiler_params=params(8),
        name="border",
    )(*pinned(solution, phase_label, source, table))
    top = lax.ppermute(top, "tile", wheel(tiles, -1))
    bottom = lax.ppermute(bottom, "tile", wheel(tiles, 1))
    even, odd = pl.pallas_call(
        corner_kernel,
        out_shape=(message, message),
        in_specs=[HBM] * 4,
        out_specs=(VMEM,) * 2,
        scratch_shapes=[pltpu.VMEM(edge.shape, f32)] * 2 + [pltpu.SemaphoreType.DMA((4,))],
        compiler_params=params(8),
        name="corner",
    )(even, odd, top, bottom)
    even = lax.ppermute(even, "slab", pairs(slabs, False))
    odd = lax.ppermute(odd, "slab", pairs(slabs, True))
    row_top, row_bottom = top, bottom

    wide_block = pltpu.VMEM((planes, tall, width), f32)
    operands = [
        phase_diffusivity, phase_uptake, coarse_diag, coarse_ids, coarse_off, coarse_cols, table,
        solution, phase_label, source, top, bottom,
    ]
    phases = phase_diffusivity.shape[0]
    residual, face, plain, packed, tables, column, record, scalars = pl.pallas_call(
        functools.partial(residual_kernel, direct=direct, count=count),
        out_shape=(
            shape((depth, rows, width), bf16),
            shape((6, rows, width), f32),
            shape((depth, rows, width), f32),
            shape((depth // 2, 8, width), f32),
            shape((8, entries), i32),
            shape((entries, 8), i32),
            shape((cells, 128), f32),
            shape((3, phases, 8, 128), f32),
        ),
        in_specs=[HBM] * 12,
        out_specs=(VMEM,) * 8,
        scratch_shapes=[pltpu.VMEM((depth, tall, width), f32)] * 3
        + [pltpu.SMEM(array.shape, array.dtype) for array in operands[:4]]
        + [pltpu.VMEM(array.shape, array.dtype) for array in operands[4:]]
        + [pltpu.SemaphoreType.DMA((12,))],
        compiler_params=params(12),
        name="residual",
    )(*pinned(*operands[:10]), *operands[10:])

    groups = max(1, slabs // 8)
    lines = 4 * groups
    payload = pl.pallas_call(
        functools.partial(restrict_kernel, capacity=capacity),
        out_shape=shape((devices, lines, 128), f32),
        in_specs=[VMEM] * (7 + parts),
        out_specs=VMEM,
        compiler_params=params(8),
        name="restrict",
    )(scalars, column, record, even, odd, face, residual, *basis)
    got = lax.all_to_all(payload, ("slab", "tile"), split_axis=0, concat_axis=0, tiled=True)
    got = [got[:, 4 * t : 4 * t + 4].reshape(4 * devices, 128) for t in range(groups)]

    edge = shape((planes, 2, width), f32)
    corrected, top, bottom, coarse_correction = pl.pallas_call(
        functools.partial(prolong_kernel, groups=groups),
        out_shape=(shape((planes, rows, width), f32), edge, edge, shape((1, cells), f32)),
        in_specs=[VMEM] * (5 + groups + parts),
        out_specs=(VMEM, VMEM, VMEM, VMEM),
        compiler_params=params(12 + count // 128),
        name="prolong",
    )(scalars, tables, even, odd, plain, *got, *basis)
    corrected, packed = lax.optimization_barrier((corrected, packed))
    weights = pl.pallas_call(
        weigh_kernel,
        out_shape=shape((7, planes, tall, width), f32),
        in_specs=[VMEM] * 7,
        out_specs=VMEM,
        scratch_shapes=[wide_block] * 2,
        compiler_params=params(12),
        name="weigh",
    )(scalars, packed, source, even, odd, row_top, row_bottom)
    top = lax.ppermute(top, "tile", wheel(tiles, -1))
    bottom = lax.ppermute(bottom, "tile", wheel(tiles, 1))
    smooth = pl.pallas_call(
        smooth_kernel,
        out_shape=shape((rows, depth, width), f32),
        in_specs=[VMEM] * 4,
        out_specs=HBM,
        scratch_shapes=[wide_block] * 2 + [pltpu.VMEM(block, f32), pltpu.SemaphoreType.DMA((depth // 8,))],
        compiler_params=params(16),
        name="smooth",
    )(corrected, top, bottom, weights)
    return smooth, coarse_correction.reshape(cells)


def solution(mesh):
    placed = (
        P("tile", "slab", None),
        P("tile", "slab", None),
        P("tile", "slab", None),
        P(),
        P(),
        P("slab", "tile", None, None),
        P("slab", "tile", None),
        P("slab", "tile", None),
        P(("slab", "tile")),
        P(("slab", "tile"), None, None),
        P(("slab", "tile")),
        P(("slab", "tile"), None),
        P(("slab", "tile"), None),
    )
    return jax.shard_map(
        shards,
        mesh=mesh,
        in_specs=placed,
        out_specs=(P("tile", "slab", None), P(("slab", "tile"))),
        check_vma=False,
    )
```

```python
import functools

import jax
import jax.numpy as jnp
from jax import lax
from jax.experimental import pallas as pl
from jax.experimental.pallas import tpu as pltpu
from jax.sharding import PartitionSpec as P

COARSE_SWEEPS = 4
SMOOTH_SWEEPS = 2
OMEGA = 0.8

VMEM = pl.BlockSpec(memory_space=pltpu.VMEM)
SMEM = pl.BlockSpec(memory_space=pltpu.SMEM)
HBM = pl.BlockSpec(memory_space=pltpu.HBM)
MIB = 1024 * 1024
HALF, SECOND, COLS, DIAG, PLACE, SUMS = 64, 16, 32, 46, 47, 48
BASE = 4096


def place_of(index, count):
    row = index % 8
    return row // 4 * (count // 2) + index // 8 * 4 + row % 4


def params(mib=16):
    return pltpu.CompilerParams(vmem_limit_bytes=mib * MIB)


def pairs(count, odd):
    shift = 1 if odd else 0
    return [(i, ((i - shift) ^ 1) + shift) if i - shift >= 0 else (i, count - 1) for i in range(count)]


def closed(table, count):
    return [(source, target % count) for source, target in table]


def along_tile(message, odd):
    tiles = lax.axis_size("tile")
    return lax.ppermute(message, "tile", closed(pairs(tiles, odd), tiles))


def along_slab(message, odd):
    slabs, tiles = lax.axis_size("slab"), lax.axis_size("tile")
    table = []
    for source, target in closed(pairs(slabs, odd), slabs):
        inside = abs(source - target) == 1
        for tile in range(tiles):
            to = target * tiles + tile if inside else source * tiles + (tile ^ 1)
            table.append((source * tiles + tile, to))
    return lax.ppermute(message, ("slab", "tile"), table)


class Either:
    def __init__(self, flag, yes, no):
        self.flag, self.yes, self.no = flag, yes, no
        self.shape = yes.shape

    def __getitem__(self, at):
        return jnp.where(self.flag, self.yes[at], self.no[at])


def from_tile(even_ref, odd_ref):
    odd = lax.axis_index("tile") % 2 == 1
    return Either(odd, odd_ref, even_ref), Either(odd, even_ref, odd_ref)


def fetch(pairs_of_refs, sems):
    copies = [
        pltpu.make_async_copy(source, target, sems.at[k])
        for k, (source, target) in enumerate(pairs_of_refs)
    ]
    for copy in copies:
        copy.start()
    return copies


def sort_kernel(slot_hbm, len_hbm, ids_hbm, basis_hbm, *refs, capacity, count):
    out_hbm, slot_ref, len_ref, ids_ref, basis_ref, out_ref, sems = refs
    entries, voxels = basis_ref.shape
    cells = len_ref.shape[0]
    support = entries // cells
    wide = out_ref.shape[1]
    border = (wide - 128 - voxels) // 2
    chunk = voxels // 2
    pieces = [
        (basis_hbm.at[:, pl.ds(k * chunk, chunk)], basis_ref.at[:, pl.ds(k * chunk, chunk)]) for k in range(2)
    ]
    small = [(slot_hbm, slot_ref), (len_hbm, len_ref), (ids_hbm, ids_ref)]
    copies = fetch(small + pieces, sems)
    for copy in copies[:3]:
        copy.wait()
    lane = lax.broadcasted_iota(jnp.int32, (1, entries), 1)
    length = jnp.zeros((1, entries), jnp.int32)
    ident = jnp.zeros((1, entries), jnp.int32)
    for cell in range(cells):
        here = lane // support == cell
        length = jnp.where(here, len_ref[cell], length)
        ident = jnp.where(here, ids_ref[cell], ident)
    ident = place_of(ident, count)
    live = lane % support < length
    slot = jnp.where(live, slot_ref[...], -1)
    row = lax.broadcasted_iota(jnp.int32, (entries, entries), 0)
    above = jnp.where(row >= entries - capacity, row + capacity - entries, row + capacity)
    below = jnp.where(row < capacity, row - capacity + entries, row - capacity)
    hits = [slot == row, slot == above, slot == below]
    picks = [jnp.where(hit, 1.0, 0.0).astype(jnp.bfloat16) for hit in hits]

    def put(block, start):
        out_ref[:, start : start + block.shape[1]] = block.astype(jnp.bfloat16)

    def send(k, start, size):
        part = pl.ds(start, size)
        copy = pltpu.make_async_copy(out_ref.at[:, part], out_hbm.at[:, part], sems.at[len(copies) + k])
        copy.start()
        return copy

    def move(pick, start, size, target):
        block = basis_ref[:, start : start + size]
        put(jnp.dot(pick, block, preferred_element_type=jnp.float32), target)

    extra = lax.broadcasted_iota(jnp.int32, (entries, 128), 1)
    tail = jnp.zeros((entries, 128), jnp.float32)
    for k, hit in enumerate(hits):
        low = jnp.sum(jnp.where(hit, ident % 256, 0).astype(jnp.float32), axis=1, keepdims=True)
        high = jnp.sum(jnp.where(hit, ident // 256, 0).astype(jnp.float32), axis=1, keepdims=True)
        tail = jnp.where(extra == 2 * k, low, jnp.where(extra == 2 * k + 1, high, tail))
    cell = jnp.sum(jnp.where(hits[0], lane // support, 0).astype(jnp.float32), axis=1, keepdims=True)
    put(jnp.where(extra == 2 * len(hits), cell, tail), voxels + 2 * border)
    for k in range(2):
        copies[3 + k].wait()
        for start in range(k * chunk, (k + 1) * chunk, 512):
            move(picks[0], start, 512, start)
        if k == 0:
            sent = send(0, 0, chunk)
            move(picks[1], 0, border, voxels)
    move(picks[2], voxels - border, border, voxels + border)
    send(1, chunk, wide - chunk).wait()
    sent.wait()


LOW, FAR, SOURCE, LABELS, CORNERS, TABLE = 32, 64, 96, 128, 144, 148
MESSAGE = 160


def border_kernel(
    sol_hbm, label_hbm, src_hbm, table_hbm, even_ref, odd_ref, row_even_ref, row_odd_ref,
    sol_ref, label_ref, src_ref, table_ref, sems,
):
    rows, depth, width = sol_ref.shape
    blocks = ((sol_hbm, sol_ref), (label_hbm, label_ref), (src_hbm, src_ref), (table_hbm, table_ref))
    for copy in fetch(blocks, sems):
        copy.wait()
    odd = lax.axis_index("slab") % 2 == 1

    def planes(start):
        parts = [ref[:, start : start + 2, :].astype(jnp.float32) for ref in (sol_ref, label_ref, src_ref, src_ref)]
        block = jnp.transpose(jnp.concatenate(parts, axis=1), (1, 0, 2))
        return [block[k] for k in range(6)]

    near, far, label, label_far, origin, unused = planes(0)
    down = near, far, origin, pack_labels(label, label_far, 16)
    far, near, label_far, label, unused, origin = planes(depth - 2)
    up = near, far, origin, pack_labels(label, label_far, 16)
    slots, capacity = table_ref.shape
    table = flat(table_ref[...]).astype(jnp.float32)
    table = jnp.concatenate([table, jnp.zeros((1, width - table.shape[1]), jnp.float32)], axis=1)
    line = lax.broadcasted_iota(jnp.int32, (16, width), 0) + CORNERS
    table = jnp.where(line == TABLE, table, 0.0)
    for first, second, ref in ((up, down, even_ref), (down, up, odd_ref)):
        near, far, origin, labels = [jnp.where(odd, b, a) for a, b in zip(first, second)]
        high = near.astype(jnp.bfloat16)
        ref[:LOW] = high
        ref[LOW:FAR] = (near - high.astype(jnp.float32)).astype(jnp.bfloat16)
        ref[FAR:SOURCE] = far.astype(jnp.bfloat16)
        ref[SOURCE:LABELS] = origin.astype(jnp.bfloat16)
        ref[LABELS:CORNERS] = labels.astype(jnp.bfloat16)
        ref[CORNERS:] = table.astype(jnp.bfloat16)
    first, last = [
        (sol_ref[near], (label_ref[near] + 3 * label_ref[far]).astype(jnp.float32), src_ref[near])
        for near, far in ((0, 1), (rows - 1, rows - 2))
    ]
    odd = lax.axis_index("tile") % 2 == 1
    for k in range(3):
        row_even_ref[k] = jnp.where(odd, first[k], last[k])
        row_odd_ref[k] = jnp.where(odd, last[k], first[k])


def flat(table):
    return jnp.concatenate([table[at : at + 1] for at in range(table.shape[0])], axis=1)


def pack_labels(near, far, lines):
    pair = near + 3.0 * far
    packed = pair[0:lines]
    for k in range(1, pair.shape[0] // lines):
        packed = packed + float(9**k) * pair[lines * k : lines * (k + 1)]
    return packed


def unpack_labels(packed, rows):
    found = []
    for k in range(rows // packed.shape[0]):
        rest = jnp.floor((packed + 0.5) * (1.0 / 9.0))
        found.append(packed - 9.0 * rest)
        packed = rest
    return part_pair(jnp.concatenate(found, axis=0))


def part_pair(pair):
    far = jnp.floor((pair + 0.5) * (1.0 / 3.0))
    return pair - 3.0 * far, far


def from_slab(even_ref, odd_ref, start, stop):
    swap = lax.axis_index("slab") % 2 == 1
    even, odd = even_ref[start:stop].astype(jnp.float32), odd_ref[start:stop].astype(jnp.float32)
    return jnp.where(swap, odd, even), jnp.where(swap, even, odd)


def nearest_planes(even_ref, odd_ref):
    upper, lower = from_slab(even_ref, odd_ref, 0, LOW), from_slab(even_ref, odd_ref, LOW, FAR)
    return upper[0] + lower[0], upper[1] + lower[1]


def corner_kernel(even_in, odd_in, row_even, row_odd, even_ref, odd_ref, row_even_ref, row_odd_ref, sems):
    moves = [(even_in, even_ref), (odd_in, odd_ref), (row_even, row_even_ref), (row_odd, row_odd_ref)]
    for copy in fetch(moves, sems):
        copy.wait()
    top_ref, bottom_ref = from_tile(row_even_ref, row_odd_ref)
    depth, width = top_ref.shape[1:]
    odd = lax.axis_index("slab") % 2 == 1
    line = lax.broadcasted_iota(jnp.int32, (16, width), 0)
    for ref, upward in ((even_ref, jnp.logical_not(odd)), (odd_ref, odd)):
        block = ref[CORNERS:].astype(jnp.float32)
        for k in range(4):
            edge_ref, low = (top_ref, bottom_ref)[k // 2], k % 2
            high = depth - 1 - low
            pair = jnp.where(upward, edge_ref[1, high : high + 1], edge_ref[1, low : low + 1])
            block = jnp.where(line == k, pair, block)
        ref[CORNERS:] = block.astype(jnp.bfloat16)


def beside(plane, lane):
    rows, width = plane.shape
    left = jnp.where(lane == 0, 0.0, pltpu.roll(plane, 1, 1))
    right = jnp.where(lane == width - 1, 0.0, pltpu.roll(plane, width - 1, 1))
    return left + right + pltpu.roll(plane, 1, 0) + pltpu.roll(plane, rows - 1, 0)


class Grid:
    def __init__(self, diffs, uptakes, labels, top_pairs, bottom_pairs, outside, conduct_ref, uptake_ref):
        self.conduct_ref, self.uptake_ref = conduct_ref, uptake_ref
        self.planes, rows, width = conduct_ref.shape
        own = labels[0].shape[0]
        row = lax.broadcasted_iota(jnp.int32, (rows, width), 0)
        self.lane = lax.broadcasted_iota(jnp.int32, (rows, width), 1)
        tile = lax.axis_index("tile")
        beyond = (row >= own + 2) & (row < rows - 2)
        beyond = beyond | ((row >= own) & (row < own + 4) & (tile == lax.axis_size("tile") - 1))
        beyond = beyond | ((row >= own + 4) & (tile == 0))
        blank = jnp.zeros((8, width), jnp.float32)
        for z, (label, top, bottom) in enumerate(zip(labels, top_pairs, bottom_pairs)):
            conduct_ref[z, :own] = label
            conduct_ref[z, own:] = blank
            near, far = part_pair(top)
            conduct_ref[z, own : own + 1] = near
            conduct_ref[z, own + 1 : own + 2] = far
            near, far = part_pair(bottom)
            conduct_ref[z, rows - 1 :] = near
            conduct_ref[z, rows - 2 : rows - 1] = far
            label = jnp.where(beyond | outside[z] if z in outside else beyond, -1.0, conduct_ref[z])
            conduct = jnp.zeros(label.shape, jnp.float32)
            uptake = jnp.zeros(label.shape, jnp.float32)
            for phase, (diff, upt) in enumerate(zip(diffs, uptakes)):
                conduct = jnp.where(label == float(phase), diff, conduct)
                uptake = jnp.where(label == float(phase), upt, uptake)
            conduct_ref[z] = conduct
            uptake_ref[z] = uptake

    def in_plane(self, z):
        rows, width = self.conduct_ref.shape[1:]
        plane = self.conduct_ref[z]
        return (
            jnp.where(self.lane == 0, 0.0, pltpu.roll(plane, 1, 1)),
            jnp.where(self.lane == width - 1, 0.0, pltpu.roll(plane, width - 1, 1)),
            pltpu.roll(plane, 1, 0),
            pltpu.roll(plane, rows - 1, 0),
        )


def ends():
    slab = lax.axis_index("slab")
    return slab == lax.axis_size("slab") - 1, slab == 0


def residual_kernel(*refs, count):
    operands, outputs, scratch = refs[:12], refs[12:20], refs[20:]
    conduct_ref, uptake_ref, sol_ref = scratch[:3]
    local, sems = scratch[3:15], scratch[15]
    diff_ref, upt_ref, diag_ref, ids_ref = local[:4]
    off_ref, cols_ref, table_ref, sol_in, label_in, src_in = local[4:10]
    top_ref, bottom_ref = from_tile(*local[10:])
    res_ref, face_ref, plain_ref, packed_ref, tables_ref, column_ref, record_ref, scalar_ref = outputs
    for copy in fetch(list(zip(operands, local)), sems):
        copy.wait()
    own, depth, width = sol_in.shape
    rows = conduct_ref.shape[1]
    cells, nnz = off_ref.shape

    for phase in range(diff_ref.shape[0]):
        scalar_ref[0, phase] = jnp.full((8, 128), diff_ref[phase])
        scalar_ref[1, phase] = jnp.full((8, 128), upt_ref[phase])
    line = lax.broadcasted_iota(jnp.int32, record_ref.shape, 0)
    mine = jnp.zeros(record_ref.shape, jnp.int32)
    for cell in range(cells):
        mine = jnp.where(line == cell, ids_ref[cell], mine)
    mine = place_of(mine, count).astype(jnp.float32)
    scalar_ref[2, 0] = mine
    lane = lax.broadcasted_iota(jnp.int32, record_ref.shape, 1)
    record = jnp.where(lane == PLACE, mine, 0.0)
    for cell in range(cells):
        record = jnp.where((line == cell) & (lane == DIAG), diag_ref[cell], record)
    record_ref[...] = record
    group = nnz // 2
    cols = place_of(cols_ref[...], count).astype(jnp.float32)
    record_ref[:, :group] = off_ref[:, :group]
    record_ref[:, SECOND : SECOND + group] = off_ref[:, group:]
    record_ref[:, COLS : COLS + group] = cols[:, :group] + float(BASE) * cols[:, group:]
    record = record_ref[...]
    record_ref[:4] = jnp.concatenate([record[:4, :HALF], record[4:, :HALF]], axis=1)
    slots, capacity = table_ref.shape
    entries = slots * capacity
    table = flat(table_ref[...]).astype(jnp.float32)
    table = jnp.concatenate([table, jnp.zeros((1, 128 - entries), jnp.float32)], axis=1)
    table = jnp.broadcast_to(table, (8, 128))
    tables_ref[...] = table[:, :entries].astype(jnp.int32)
    column_ref[...] = jnp.transpose(table)[:entries].astype(jnp.int32)

    labels = []
    for start in range(0, depth, 8):
        block = jnp.transpose(label_in[:, start : start + 8, :].astype(jnp.float32), (1, 0, 2))
        labels = labels + [block[at] for at in range(8)]
    for k in range(depth // 2):
        packed_ref[k] = pack_labels(labels[2 * k], labels[2 * k + 1], 8)
    top_pairs = [top_ref[1, z : z + 1] for z in range(depth)]
    bottom_pairs = [bottom_ref[1, z : z + 1] for z in range(depth)]
    phases = range(diff_ref.shape[0])
    diffs, uptakes = [diff_ref[phase] for phase in phases], [upt_ref[phase] for phase in phases]
    grid = Grid(diffs, uptakes, labels, top_pairs, bottom_pairs, {}, conduct_ref, uptake_ref)
    blank = jnp.zeros((8, width), jnp.float32)
    for start in range(0, depth, 8):
        block = jnp.transpose(sol_in[:, start : start + 8, :], (1, 0, 2))
        for at in range(8):
            z = start + at
            plain_ref[z] = block[at]
            sol_ref[z, :own] = block[at]
            sol_ref[z, own:] = blank
            sol_ref[z, own : own + 1] = top_ref[0, z : z + 1]
            sol_ref[z, rows - 1 :] = bottom_ref[0, z : z + 1]
            sol_ref[z] = jnp.where(conduct_ref[z] > 0.0, sol_ref[z], 0.0)
    for start in range(0, depth, 8):
        block = jnp.transpose(src_in[:, start : start + 8, :], (1, 0, 2))
        for at in range(8):
            z = start + at
            conduct, value = conduct_ref[z], sol_ref[z]
            near = sum(grid.in_plane(z))
            diagonal = uptake_ref[z] + 2.0 * conduct + 0.5 * near
            flow = conduct * beside(value, grid.lane) + beside(conduct * value, grid.lane)
            applied = (diagonal * value - 0.5 * flow)[:own]
            conduct, value = conduct[:own], value[:own]
            for other in (z - 1, z + 1):
                if 0 <= other < depth:
                    applied = applied + 0.5 * (conduct + conduct_ref[other, :own]) * (value - sol_ref[other, :own])
            left = block[at] - applied
            res_ref[z] = left.astype(jnp.bfloat16)
            if z in (0, depth - 1):
                side = 0 if z == 0 else 3
                face_ref[side] = left
                face_ref[side + 1] = conduct
                face_ref[side + 2] = value


def phase_rows(scalar_ref, kind, width):
    found = []
    for phase in range(scalar_ref.shape[1]):
        row = scalar_ref[kind, phase, 0:1]
        found.append(jnp.concatenate([row] * (width // row.shape[1]), axis=1))
    return found


def weigh_kernel(
    scalar_ref, packed_ref, src_in, even_ref, odd_ref, row_even_ref, row_odd_ref, weight_ref,
    conduct_ref, uptake_ref,
):
    own, depth, width = src_in.shape
    planes, rows = conduct_ref.shape[0:2]
    top_ref, bottom_ref = from_tile(row_even_ref, row_odd_ref)
    labels = []
    for k in range(depth // 2):
        labels = labels + list(unpack_labels(packed_ref[k], own))
    high, low = from_slab(even_ref, odd_ref, LABELS, CORNERS)
    (high_near, high_far), (low_near, low_far) = unpack_labels(high, own), unpack_labels(low, own)
    labels = labels + [high_near, high_far, low_far, low_near]
    high, low = from_slab(even_ref, odd_ref, CORNERS, MESSAGE)
    top_pairs = [top_ref[1, z : z + 1] for z in range(depth)] + [high[0:1], high[1:2], low[1:2], low[0:1]]
    bottom_pairs = [bottom_ref[1, z : z + 1] for z in range(depth)] + [high[2:3], high[3:4], low[3:4], low[2:3]]
    above, below = ends()
    outside = {depth: above, depth + 1: above, depth + 2: below, depth + 3: below}
    diffs, uptakes = phase_rows(scalar_ref, 0, width), phase_rows(scalar_ref, 1, width)
    grid = Grid(diffs, uptakes, labels, top_pairs, bottom_pairs, outside, conduct_ref, uptake_ref)
    blank = jnp.zeros((8, width), jnp.float32)
    outer = dict(zip((depth, planes - 1), from_slab(even_ref, odd_ref, SOURCE, LABELS)))
    for start in (0, 8, planes - 1, depth):
        if start < depth:
            block = jnp.transpose(src_in[:, start : start + 8, :], (1, 0, 2))
            sources = {start + at: block[at] for at in range(8)}
        else:
            sources = {start: outer[start]}
        for z, source in sources.items():
            conduct = conduct_ref[z]
            near = grid.in_plane(z) + (conduct_ref[(z - 1) % planes], conduct_ref[(z + 1) % planes])
            diagonal = uptake_ref[z] + 3.0 * conduct + 0.5 * sum(near[1:], near[0])
            inside = conduct > 0.0
            scale = jnp.where(inside, OMEGA / jnp.where(inside, diagonal, 1.0), 0.0)
            for k, other in enumerate(near):
                weight_ref[k, z] = jnp.where(other > 0.0, 0.5 * scale * (conduct + other), 0.0)
            weight_ref[6, z, :own] = scale[:own] * source
            weight_ref[6, z, own:] = blank
            if z < depth:
                weight_ref[6, z, own : own + 1] = scale[own : own + 1] * top_ref[2, z : z + 1]
                weight_ref[6, z, rows - 1 :] = scale[rows - 1 :] * bottom_ref[2, z : z + 1]


def rows_of(basis, start, size):
    return basis[:, start : start + size].astype(jnp.float32)


def owners_of(basis):
    tail = rows_of(basis, basis.shape[1] - 128, 128)
    cell = tail[:, 6:7].astype(jnp.int32)
    return cell, [
        (tail[:, 2 * k : 2 * k + 1] + 256.0 * tail[:, 2 * k + 1 : 2 * k + 2]).astype(jnp.int32)
        for k in range(3)
    ]


def restrict_kernel(scalar_ref, column_ref, record_ref, even_ref, odd_ref, face_ref, res_ref, *refs, capacity):
    basis, out_ref = refs
    depth, own, width = res_ref.shape
    entries = column_ref.shape[0]
    pick = column_ref[:, 0:1] == lax.broadcasted_iota(jnp.int32, (entries, own), 1)
    pick = jnp.where(pick, 1.0, 0.0).astype(jnp.bfloat16)
    values = nearest_planes(even_ref, odd_ref)
    packed = from_slab(even_ref, odd_ref, LABELS, CORNERS)
    diffs = phase_rows(scalar_ref, 0, width)
    faces = {}
    for z, side, at in ((0, 0, 1), (depth - 1, 3, 0)):
        label = unpack_labels(packed[at], own)[0]
        beyond = jnp.zeros(label.shape, jnp.float32)
        for phase, diff in enumerate(diffs):
            beyond = jnp.where(label == float(phase), diff, beyond)
        beyond = jnp.where(ends()[at], 0.0, beyond)
        value = jnp.where(ends()[at], 0.0, values[at])
        applied = 0.5 * (face_ref[side + 1] + beyond) * (face_ref[side + 2] - value)
        faces[z] = (face_ref[side] - applied).astype(jnp.bfloat16)
    total = jnp.zeros((entries, width), jnp.float32)
    for z in range(depth):
        plane = faces[z] if z in faces else res_ref[z]
        piece = jnp.dot(pick, plane, preferred_element_type=jnp.float32)
        total = total + piece * rows_of(basis, z * width, width)
    product = jnp.sum(total, axis=1, keepdims=True)
    cell, unused = owners_of(basis)
    copies, lines, lanes = out_ref.shape
    peer = lax.broadcasted_iota(jnp.int32, (entries, 1), 0) // capacity
    target = (peer // 8 * 4 + peer % 4) * lanes + peer % 8 // 4 * HALF + SUMS + cell
    lane = lax.broadcasted_iota(jnp.int32, (entries, lanes), 1)
    rows = []
    for line in range(lines):
        share = jnp.sum(jnp.where(target == line * lanes + lane, product, 0.0), axis=0, keepdims=True)
        rows.append(share + record_ref[line : line + 1] if line < 4 else share)
    block = jnp.concatenate(rows, axis=0)

    def put(copy, carry):
        out_ref[copy] = block
        return carry

    lax.fori_loop(0, copies, put, 0, unroll=8)


def solve(got, tiles):
    extent, lanes = got[0].shape
    turned = jnp.transpose(got[0][...])
    chunks = range(0, extent, lanes)
    owners = 4 * tiles
    line = lax.broadcasted_iota(jnp.int32, (8, lanes), 0)
    lane = lax.broadcasted_iota(jnp.int32, (8, lanes), 1)

    def left(block, by):
        return pltpu.roll(block, lanes - by, 1) if by else block

    rhs = [jnp.zeros((8, lanes), jnp.float32) for at in range(2 * len(chunks))]
    place = [lane + at * lanes for at in range(2 * len(chunks))]
    for t, ref in enumerate(got):
        total = ref[:owners]
        for at in range(owners, extent, owners):
            total = total + ref[at : at + owners]
        block = jnp.transpose(jnp.concatenate([total] * (lanes // owners), axis=0))
        value = jnp.zeros((8, lanes), jnp.float32)
        ident = jnp.zeros((8, lanes), jnp.float32)
        for half in range(2):
            total = block[half * HALF + SUMS : half * HALF + SUMS + 8]
            row = half * HALF + PLACE
            places = jnp.broadcast_to(turned[row : row + 1, t * lanes : (t + 1) * lanes], (8, lanes))
            for i in range(4):
                value = jnp.where(lane // owners == 4 * half + i, left(total, i), value)
                ident = jnp.where(line == 4 * half + i, left(places, i), ident)
        ident = ident.astype(jnp.int32)
        for at in range(0, lanes, 4):
            here, amount = ident[:, at : at + 1], value[:, at : at + 1]
            rhs = [total + jnp.where(here == spot, amount, 0.0) for total, spot in zip(rhs, place)]
    rhs = [jnp.sum(total, axis=0, keepdims=True) for total in rhs]

    values, places, inverse = [], [], []
    for half in range(2):
        for at in chunks:
            block = turned[half * HALF : (half + 1) * HALF, at : at + lanes]
            values.append(block[:COLS])
            packed = block[COLS : COLS + SECOND]
            second = jnp.floor(packed * (1.0 / BASE))
            first = packed - float(BASE) * second
            places.append(jnp.concatenate([first, second], axis=0).astype(jnp.int32) % (2 * extent))
            inverse.append(1.0 / block[DIAG : DIAG + 1])
    state = [total * factor for total, factor in zip(rhs, inverse)]
    for repeat in range(COARSE_SWEEPS - 1):
        sources = [jnp.broadcast_to(part, (COLS, lanes)) for part in state]
        new = []
        for total, factor, value, spot in zip(rhs, inverse, values, places):
            found = jnp.zeros((COLS, lanes), jnp.float32)
            for k, source in enumerate(sources):
                taken = jnp.take_along_axis(source, spot % lanes, axis=1, mode="promise_in_bounds")
                found = jnp.where(spot // lanes == k, taken, found)
            new.append((total - jnp.sum(value * found, axis=0, keepdims=True)) * factor)
        state = new
    return jnp.concatenate(state, axis=1)


def prolong_kernel(scalar_ref, tables_ref, even_ref, odd_ref, plain_ref, *refs, groups):
    got, basis = refs[:groups], refs[groups]
    cor_ref, row_even_ref, row_odd_ref, correction_ref = refs[-4:]
    odd = lax.axis_index("tile") % 2 == 1
    planes, own, width = cor_ref.shape
    depth = plain_ref.shape[0]
    entries = tables_ref.shape[1]
    cells = correction_ref.shape[1]
    count = 2 * got[0].shape[0]
    state = solve(got, lax.axis_size("tile"))
    line = lax.broadcasted_iota(jnp.int32, (cells, 1), 0)
    mine = scalar_ref[2, 0, :, 0:1].astype(jnp.int32)

    def look_up(ident):
        hit = ident == lax.broadcasted_iota(jnp.int32, (ident.shape[0], count), 1)
        return jnp.sum(jnp.where(hit, state, 0.0), axis=1, keepdims=True)

    diagonal = line == lax.broadcasted_iota(jnp.int32, (cells, cells), 1)
    correction_ref[...] = jnp.sum(jnp.where(diagonal, look_up(mine), 0.0), axis=0, keepdims=True)
    near_high, near_low = nearest_planes(even_ref, odd_ref)
    far_high, far_low = from_slab(even_ref, odd_ref, FAR, SOURCE)
    wide = {depth: near_high, depth + 1: far_high, depth + 2: far_low, depth + 3: near_low}
    high, low = from_slab(even_ref, odd_ref, CORNERS, MESSAGE)
    line = TABLE - CORNERS
    table_high, table_low = high[line : line + 1, :entries], low[line : line + 1, :entries]
    tables = (tables_ref[0:1], table_high.astype(jnp.int32), table_low.astype(jnp.int32))
    base = depth * width
    unused, owners = owners_of(basis)
    for group, owner in enumerate(owners):
        pick = tables[group] == lax.broadcasted_iota(jnp.int32, (own, entries), 0)
        pick = jnp.where(pick, 1.0, 0.0).astype(jnp.bfloat16)
        factor = look_up(owner)
        if group == 0:
            places = [(z, z * width) for z in range(depth)]
        else:
            at = depth + 2 * (group - 1)
            places = [(at + k, base + (at + k - depth) * width) for k in range(2)]
        for z, start in places:
            part = (rows_of(basis, start, width) * factor).astype(jnp.bfloat16)
            added = jnp.dot(pick, part, preferred_element_type=jnp.float32)
            value = (plain_ref[z] if z < depth else wide[z]) + added
            cor_ref[z] = value
            first, last = value[:2], value[own - 2 :]
            row_even_ref[z] = jnp.where(odd, first, last)
            row_odd_ref[z] = jnp.where(odd, last, first)


def smooth_kernel(cor_ref, row_even_ref, row_odd_ref, weight_ref, out_hbm, new_ref, mid_ref, out_ref, sems):
    planes, rows, width = mid_ref.shape
    own, depth, unused = out_ref.shape
    top_ref, bottom_ref = from_tile(row_even_ref, row_odd_ref)
    gap = jnp.zeros((rows - own - 4, width), jnp.float32)

    def corrected(z):
        return jnp.concatenate([cor_ref[z], top_ref[z], gap, bottom_ref[z]], axis=0)

    def middle(z):
        return mid_ref[z]

    def sweep(plane, z, upto):
        value = plane(z)
        near = (
            pltpu.roll(value, 1, 1)[:upto],
            pltpu.roll(value, width - 1, 1)[:upto],
            pltpu.roll(value, 1, 0)[:upto],
            pltpu.roll(value, rows - 1, 0)[:upto],
            plane((z - 1) % planes)[:upto],
            plane((z + 1) % planes)[:upto],
        )
        total = (1.0 - OMEGA) * value[:upto] + weight_ref[6, z, :upto]
        for k in range(6):
            total = total + weight_ref[k, z, :upto] * near[k]
        return total

    for z in [planes - 1] + list(range(depth + 1)):
        mid_ref[z] = sweep(corrected, z, rows)
    copies = []
    for start in range(0, depth, 8):
        for z in range(start, start + 8):
            new_ref[z] = sweep(middle, z, own)
        out_ref[:, start : start + 8, :] = jnp.transpose(new_ref[start : start + 8], (1, 0, 2))
        part = pl.ds(start, 8)
        copies.append(pltpu.make_async_copy(out_ref.at[:, part], out_hbm.at[:, part], sems.at[start // 8]))
        copies[-1].start()
    for copy in copies:
        copy.wait()


def shards(
    solution,
    source,
    phase_label,
    phase_diffusivity,
    phase_uptake,
    send_tiles,
    support_slot,
    support_len,
    coarse_ids,
    basis_values,
    coarse_diag,
    coarse_off,
    coarse_cols,
):
    f32, i32, bf16 = jnp.float32, jnp.int32, jnp.bfloat16
    rows, depth, width = solution.shape
    voxels = depth * width
    slabs, tiles = lax.axis_size("slab"), lax.axis_size("tile")
    devices = slabs * tiles
    capacity = send_tiles.shape[3]
    cells, support, unused = basis_values.shape
    entries = cells * support
    count = cells * devices
    nnz = coarse_off.shape[1]
    shape = jax.ShapeDtypeStruct
    planes, tall = depth + 4, rows + 8
    block = (rows, depth, width)
    table = send_tiles.reshape(slabs, capacity)
    wide = voxels + 4 * width + 128

    def pinned(*arrays):
        return [pltpu.with_memory_space_constraint(array, pltpu.HBM) for array in arrays]

    outgoing = pl.pallas_call(
        functools.partial(sort_kernel, capacity=capacity, count=count),
        out_shape=shape((entries, wide), bf16),
        in_specs=[HBM] * 4,
        out_specs=HBM,
        scratch_shapes=[
            pltpu.VMEM((1, entries), i32),
            pltpu.SMEM((cells,), i32),
            pltpu.SMEM((cells,), i32),
            pltpu.VMEM((entries, voxels), bf16),
            pltpu.VMEM((entries, wide), bf16),
            pltpu.SemaphoreType.DMA((7,)),
        ],
        compiler_params=params(60),
        name="sort_basis",
    )(
        *pinned(
            support_slot.reshape(1, entries),
            support_len.reshape(cells),
            coarse_ids,
            basis_values.reshape(entries, voxels),
        )
    )
    basis = lax.all_to_all(
        outgoing.reshape(slabs, capacity, wide), "slab", split_axis=0, concat_axis=0, tiled=True
    ).reshape(entries, wide)
    outgoing, solution, phase_label, source, table = lax.optimization_barrier(
        (outgoing, solution, phase_label, source, table)
    )
    message = shape((MESSAGE, width), bf16)
    edge = shape((3, depth, width), f32)
    even, odd, row_even, row_odd = pl.pallas_call(
        border_kernel,
        out_shape=(message, message, edge, edge),
        in_specs=[HBM] * 4,
        out_specs=(VMEM,) * 4,
        scratch_shapes=[
            pltpu.VMEM(block, f32),
            pltpu.VMEM(block, i32),
            pltpu.VMEM(block, f32),
            pltpu.VMEM((slabs, capacity), i32),
            pltpu.SemaphoreType.DMA((4,)),
        ],
        compiler_params=params(8),
        name="border",
    )(*pinned(solution, phase_label, source, table))
    row_even = along_tile(row_even, False)
    row_odd = along_tile(row_odd, True)
    even, odd = pl.pallas_call(
        corner_kernel,
        out_shape=(message, message),
        in_specs=[HBM] * 4,
        out_specs=(VMEM,) * 2,
        scratch_shapes=[pltpu.VMEM(edge.shape, f32)] * 2 + [pltpu.SemaphoreType.DMA((4,))],
        compiler_params=params(8),
        name="corner",
    )(even, odd, row_even, row_odd)
    even = along_slab(even, False)
    odd = along_slab(odd, True)
    first_even, first_odd = row_even, row_odd

    wide_block = pltpu.VMEM((planes, tall, width), f32)
    operands = [
        phase_diffusivity, phase_uptake, coarse_diag, coarse_ids, coarse_off, coarse_cols, table,
        solution, phase_label, source, row_even, row_odd,
    ]
    phases = phase_diffusivity.shape[0]
    residual, face, plain, packed, tables, column, record, scalars = pl.pallas_call(
        functools.partial(residual_kernel, count=count),
        out_shape=(
            shape((depth, rows, width), bf16),
            shape((6, rows, width), f32),
            shape((depth, rows, width), f32),
            shape((depth // 2, 8, width), f32),
            shape((8, entries), i32),
            shape((entries, 8), i32),
            shape((cells, 128), f32),
            shape((3, phases, 8, 128), f32),
        ),
        in_specs=[HBM] * 12,
        out_specs=(VMEM,) * 8,
        scratch_shapes=[pltpu.VMEM((depth, tall, width), f32)] * 3
        + [pltpu.SMEM(array.shape, array.dtype) for array in operands[:4]]
        + [pltpu.VMEM(array.shape, array.dtype) for array in operands[4:]]
        + [pltpu.SemaphoreType.DMA((12,))],
        compiler_params=params(12),
        name="residual",
    )(*pinned(*operands[:10]), *operands[10:])

    groups = max(1, slabs // 8)
    lines = 4 * groups
    payload = pl.pallas_call(
        functools.partial(restrict_kernel, capacity=capacity),
        out_shape=shape((devices, lines, 128), f32),
        in_specs=[VMEM] * 8,
        out_specs=VMEM,
        compiler_params=params(8),
        name="restrict",
    )(scalars, column, record, even, odd, face, residual, basis)
    got = lax.all_to_all(payload, ("slab", "tile"), split_axis=0, concat_axis=0, tiled=True)
    got = [got[:, 4 * t : 4 * t + 4].reshape(4 * devices, 128) for t in range(groups)]

    edge = shape((planes, 2, width), f32)
    corrected, row_even, row_odd, coarse_correction = pl.pallas_call(
        functools.partial(prolong_kernel, groups=groups),
        out_shape=(shape((planes, rows, width), f32), edge, edge, shape((1, cells), f32)),
        in_specs=[VMEM] * (6 + groups),
        out_specs=(VMEM, VMEM, VMEM, VMEM),
        compiler_params=params(12 + count // 128),
        name="prolong",
    )(scalars, tables, even, odd, plain, *got, basis)
    corrected, packed = lax.optimization_barrier((corrected, packed))
    weights = pl.pallas_call(
        weigh_kernel,
        out_shape=shape((7, planes, tall, width), f32),
        in_specs=[VMEM] * 7,
        out_specs=VMEM,
        scratch_shapes=[wide_block] * 2,
        compiler_params=params(12),
        name="weigh",
    )(scalars, packed, source, even, odd, first_even, first_odd)
    row_even = along_tile(row_even, False)
    row_odd = along_tile(row_odd, True)
    smooth = pl.pallas_call(
        smooth_kernel,
        out_shape=shape((rows, depth, width), f32),
        in_specs=[VMEM] * 4,
        out_specs=HBM,
        scratch_shapes=[pltpu.VMEM((depth, rows, width), f32), wide_block, pltpu.VMEM(block, f32)]
        + [pltpu.SemaphoreType.DMA((depth // 8,))],
        compiler_params=params(16),
        name="smooth",
    )(corrected, row_even, row_odd, weights)
    return smooth, coarse_correction.reshape(cells)


def solution(mesh):
    placed = (
        P("tile", "slab", None),
        P("tile", "slab", None),
        P("tile", "slab", None),
        P(),
        P(),
        P("slab", "tile", None, None),
        P("slab", "tile", None),
        P("slab", "tile", None),
        P(("slab", "tile")),
        P(("slab", "tile"), None, None),
        P(("slab", "tile")),
        P(("slab", "tile"), None),
        P(("slab", "tile"), None),
    )
    return jax.shard_map(
        shards,
        mesh=mesh,
        in_specs=placed,
        out_specs=(P("tile", "slab", None), P(("slab", "tile"))),
        check_vma=False,
    )
```

```python
import functools

import jax
import jax.numpy as jnp
from jax import lax
from jax.experimental import pallas as pl
from jax.experimental.pallas import tpu as pltpu
from jax.sharding import PartitionSpec as P

COARSE_SWEEPS = 4
SMOOTH_SWEEPS = 2
OMEGA = 0.8

VMEM = pl.BlockSpec(memory_space=pltpu.VMEM)
SMEM = pl.BlockSpec(memory_space=pltpu.SMEM)
HBM = pl.BlockSpec(memory_space=pltpu.HBM)
MIB = 1024 * 1024
HALF, SECOND, COLS, DIAG, PLACE, SUMS = 64, 16, 32, 46, 47, 48
BASE = 4096


def place_of(index, count):
    row = index % 8
    return row // 4 * (count // 2) + index // 8 * 4 + row % 4


def params(mib=16):
    return pltpu.CompilerParams(vmem_limit_bytes=mib * MIB)


def pairs(count, odd):
    shift = 1 if odd else 0
    return [(i, ((i - shift) ^ 1) + shift) if i - shift >= 0 else (i, count - 1) for i in range(count)]


def closed(table, count):
    return [(source, target % count) for source, target in table]


def along_tile(message, odd):
    tiles = lax.axis_size("tile")
    return lax.ppermute(message, "tile", closed(pairs(tiles, odd), tiles))


def along_slab(message, odd):
    slabs, tiles = lax.axis_size("slab"), lax.axis_size("tile")
    table = []
    for source, target in closed(pairs(slabs, odd), slabs):
        inside = abs(source - target) == 1
        for tile in range(tiles):
            to = target * tiles + tile if inside else source * tiles + (tile ^ 1)
            table.append((source * tiles + tile, to))
    return lax.ppermute(message, ("slab", "tile"), table)


class Either:
    def __init__(self, flag, yes, no):
        self.flag, self.yes, self.no = flag, yes, no
        self.shape = yes.shape

    def __getitem__(self, at):
        return jnp.where(self.flag, self.yes[at], self.no[at])


def from_tile(even_ref, odd_ref):
    odd = lax.axis_index("tile") % 2 == 1
    return Either(odd, odd_ref, even_ref), Either(odd, even_ref, odd_ref)


def fetch(pairs_of_refs, sems):
    copies = [
        pltpu.make_async_copy(source, target, sems.at[k])
        for k, (source, target) in enumerate(pairs_of_refs)
    ]
    for copy in copies:
        copy.start()
    return copies


def sort_kernel(slot_hbm, len_hbm, ids_hbm, basis_hbm, *refs, capacity, count):
    out_hbm, slot_ref, len_ref, ids_ref, basis_ref, out_ref, sems = refs
    entries, voxels = basis_ref.shape
    cells = len_ref.shape[0]
    support = entries // cells
    wide = out_ref.shape[1]
    border = (wide - 128 - voxels) // 2
    chunk = voxels // 2
    pieces = [
        (basis_hbm.at[:, pl.ds(k * chunk, chunk)], basis_ref.at[:, pl.ds(k * chunk, chunk)]) for k in range(2)
    ]
    small = [(slot_hbm, slot_ref), (len_hbm, len_ref), (ids_hbm, ids_ref)]
    copies = fetch(small + pieces, sems)
    for copy in copies[:3]:
        copy.wait()
    lane = lax.broadcasted_iota(jnp.int32, (1, entries), 1)
    length = jnp.zeros((1, entries), jnp.int32)
    ident = jnp.zeros((1, entries), jnp.int32)
    for cell in range(cells):
        here = lane // support == cell
        length = jnp.where(here, len_ref[cell], length)
        ident = jnp.where(here, ids_ref[cell], ident)
    ident = place_of(ident, count)
    live = lane % support < length
    slot = jnp.where(live, slot_ref[...], -1)
    row = lax.broadcasted_iota(jnp.int32, (entries, entries), 0)
    above = jnp.where(row >= entries - capacity, row + capacity - entries, row + capacity)
    below = jnp.where(row < capacity, row - capacity + entries, row - capacity)
    hits = [slot == row, slot == above, slot == below]
    picks = [jnp.where(hit, 1.0, 0.0).astype(jnp.bfloat16) for hit in hits]

    def put(block, start):
        out_ref[:, start : start + block.shape[1]] = block.astype(jnp.bfloat16)

    def send(k, start, size):
        part = pl.ds(start, size)
        copy = pltpu.make_async_copy(out_ref.at[:, part], out_hbm.at[:, part], sems.at[len(copies) + k])
        copy.start()
        return copy

    def move(pick, start, size, target):
        block = basis_ref[:, start : start + size]
        put(jnp.dot(pick, block, preferred_element_type=jnp.float32), target)

    extra = lax.broadcasted_iota(jnp.int32, (entries, 128), 1)
    tail = jnp.zeros((entries, 128), jnp.float32)
    for k, hit in enumerate(hits):
        low = jnp.sum(jnp.where(hit, ident % 256, 0).astype(jnp.float32), axis=1, keepdims=True)
        high = jnp.sum(jnp.where(hit, ident // 256, 0).astype(jnp.float32), axis=1, keepdims=True)
        tail = jnp.where(extra == 2 * k, low, jnp.where(extra == 2 * k + 1, high, tail))
    cell = jnp.sum(jnp.where(hits[0], lane // support, 0).astype(jnp.float32), axis=1, keepdims=True)
    put(jnp.where(extra == 2 * len(hits), cell, tail), voxels + 2 * border)
    for k in range(2):
        copies[3 + k].wait()
        for start in range(k * chunk, (k + 1) * chunk, 512):
            move(picks[0], start, 512, start)
        if k == 0:
            sent = send(0, 0, chunk)
            move(picks[1], 0, border, voxels)
    move(picks[2], voxels - border, border, voxels + border)
    send(1, chunk, wide - chunk).wait()
    sent.wait()


LOW, FAR, SOURCE, LABELS, CORNERS, TABLE = 32, 64, 96, 128, 144, 148
MESSAGE = 160


def border_kernel(
    sol_hbm, label_hbm, src_hbm, table_hbm, even_ref, odd_ref, row_even_ref, row_odd_ref,
    sol_ref, label_ref, src_ref, table_ref, sems,
):
    rows, depth, width = sol_ref.shape
    blocks = ((sol_hbm, sol_ref), (label_hbm, label_ref), (src_hbm, src_ref), (table_hbm, table_ref))
    for copy in fetch(blocks, sems):
        copy.wait()
    odd = lax.axis_index("slab") % 2 == 1

    def planes(start):
        parts = [ref[:, start : start + 2, :].astype(jnp.float32) for ref in (sol_ref, label_ref, src_ref, src_ref)]
        block = jnp.transpose(jnp.concatenate(parts, axis=1), (1, 0, 2))
        return [block[k] for k in range(6)]

    near, far, label, label_far, origin, unused = planes(0)
    down = near, far, origin, pack_labels(label, label_far, 16)
    far, near, label_far, label, unused, origin = planes(depth - 2)
    up = near, far, origin, pack_labels(label, label_far, 16)
    slots, capacity = table_ref.shape
    table = flat(table_ref[...]).astype(jnp.float32)
    table = jnp.concatenate([table, jnp.zeros((1, width - table.shape[1]), jnp.float32)], axis=1)
    line = lax.broadcasted_iota(jnp.int32, (16, width), 0) + CORNERS
    table = jnp.where(line == TABLE, table, 0.0)
    for first, second, ref in ((up, down, even_ref), (down, up, odd_ref)):
        near, far, origin, labels = [jnp.where(odd, b, a) for a, b in zip(first, second)]
        high = near.astype(jnp.bfloat16)
        ref[:LOW] = high
        ref[LOW:FAR] = (near - high.astype(jnp.float32)).astype(jnp.bfloat16)
        ref[FAR:SOURCE] = far.astype(jnp.bfloat16)
        ref[SOURCE:LABELS] = origin.astype(jnp.bfloat16)
        ref[LABELS:CORNERS] = labels.astype(jnp.bfloat16)
        ref[CORNERS:] = table.astype(jnp.bfloat16)
    first, last = [
        (sol_ref[near], (label_ref[near] + 3 * label_ref[far]).astype(jnp.float32), src_ref[near])
        for near, far in ((0, 1), (rows - 1, rows - 2))
    ]
    odd = lax.axis_index("tile") % 2 == 1
    for k in range(3):
        row_even_ref[k] = jnp.where(odd, first[k], last[k])
        row_odd_ref[k] = jnp.where(odd, last[k], first[k])


def flat(table):
    return jnp.concatenate([table[at : at + 1] for at in range(table.shape[0])], axis=1)


def pack_labels(near, far, lines):
    pair = near + 3.0 * far
    packed = pair[0:lines]
    for k in range(1, pair.shape[0] // lines):
        packed = packed + float(9**k) * pair[lines * k : lines * (k + 1)]
    return packed


def unpack_labels(packed, rows):
    found = []
    for k in range(rows // packed.shape[0]):
        rest = jnp.floor((packed + 0.5) * (1.0 / 9.0))
        found.append(packed - 9.0 * rest)
        packed = rest
    return part_pair(jnp.concatenate(found, axis=0))


def part_pair(pair):
    far = jnp.floor((pair + 0.5) * (1.0 / 3.0))
    return pair - 3.0 * far, far


def from_slab(even_ref, odd_ref, start, stop):
    swap = lax.axis_index("slab") % 2 == 1
    even, odd = even_ref[start:stop].astype(jnp.float32), odd_ref[start:stop].astype(jnp.float32)
    return jnp.where(swap, odd, even), jnp.where(swap, even, odd)


def nearest_planes(even_ref, odd_ref):
    upper, lower = from_slab(even_ref, odd_ref, 0, LOW), from_slab(even_ref, odd_ref, LOW, FAR)
    return upper[0] + lower[0], upper[1] + lower[1]


def corner_kernel(even_in, odd_in, row_even, row_odd, even_ref, odd_ref, row_even_ref, row_odd_ref, sems):
    moves = [(even_in, even_ref), (odd_in, odd_ref), (row_even, row_even_ref), (row_odd, row_odd_ref)]
    for copy in fetch(moves, sems):
        copy.wait()
    top_ref, bottom_ref = from_tile(row_even_ref, row_odd_ref)
    depth, width = top_ref.shape[1:]
    odd = lax.axis_index("slab") % 2 == 1
    line = lax.broadcasted_iota(jnp.int32, (16, width), 0)
    for ref, upward in ((even_ref, jnp.logical_not(odd)), (odd_ref, odd)):
        block = ref[CORNERS:].astype(jnp.float32)
        for k in range(4):
            edge_ref, low = (top_ref, bottom_ref)[k // 2], k % 2
            high = depth - 1 - low
            pair = jnp.where(upward, edge_ref[1, high : high + 1], edge_ref[1, low : low + 1])
            block = jnp.where(line == k, pair, block)
        ref[CORNERS:] = block.astype(jnp.bfloat16)


def beside(plane, lane):
    rows, width = plane.shape
    left = jnp.where(lane == 0, 0.0, pltpu.roll(plane, 1, 1))
    right = jnp.where(lane == width - 1, 0.0, pltpu.roll(plane, width - 1, 1))
    return left + right + pltpu.roll(plane, 1, 0) + pltpu.roll(plane, rows - 1, 0)


class Grid:
    def __init__(self, diffs, uptakes, labels, top_pairs, bottom_pairs, outside, conduct_ref, uptake_ref):
        self.conduct_ref, self.uptake_ref = conduct_ref, uptake_ref
        self.planes, rows, width = conduct_ref.shape
        own = labels[0].shape[0]
        row = lax.broadcasted_iota(jnp.int32, (rows, width), 0)
        self.lane = lax.broadcasted_iota(jnp.int32, (rows, width), 1)
        tile = lax.axis_index("tile")
        beyond = (row >= own + 2) & (row < rows - 2)
        beyond = beyond | ((row >= own) & (row < own + 4) & (tile == lax.axis_size("tile") - 1))
        beyond = beyond | ((row >= own + 4) & (tile == 0))
        blank = jnp.zeros((8, width), jnp.float32)
        for z, (label, top, bottom) in enumerate(zip(labels, top_pairs, bottom_pairs)):
            conduct_ref[z, :own] = label
            conduct_ref[z, own:] = blank
            near, far = part_pair(top)
            conduct_ref[z, own : own + 1] = near
            conduct_ref[z, own + 1 : own + 2] = far
            near, far = part_pair(bottom)
            conduct_ref[z, rows - 1 :] = near
            conduct_ref[z, rows - 2 : rows - 1] = far
            label = jnp.where(beyond | outside[z] if z in outside else beyond, -1.0, conduct_ref[z])
            conduct = jnp.zeros(label.shape, jnp.float32)
            uptake = jnp.zeros(label.shape, jnp.float32)
            for phase, (diff, upt) in enumerate(zip(diffs, uptakes)):
                conduct = jnp.where(label == float(phase), diff, conduct)
                uptake = jnp.where(label == float(phase), upt, uptake)
            conduct_ref[z] = conduct
            uptake_ref[z] = uptake

    def in_plane(self, z):
        rows, width = self.conduct_ref.shape[1:]
        plane = self.conduct_ref[z]
        return (
            jnp.where(self.lane == 0, 0.0, pltpu.roll(plane, 1, 1)),
            jnp.where(self.lane == width - 1, 0.0, pltpu.roll(plane, width - 1, 1)),
            pltpu.roll(plane, 1, 0),
            pltpu.roll(plane, rows - 1, 0),
        )


def ends():
    slab = lax.axis_index("slab")
    return slab == lax.axis_size("slab") - 1, slab == 0


def residual_kernel(*refs, count):
    operands, outputs, scratch = refs[:12], refs[12:20], refs[20:]
    conduct_ref, uptake_ref, sol_ref = scratch[:3]
    local, sems = scratch[3:15], scratch[15]
    diff_ref, upt_ref, diag_ref, ids_ref = local[:4]
    off_ref, cols_ref, table_ref, sol_in, label_in, src_in = local[4:10]
    top_ref, bottom_ref = from_tile(*local[10:])
    res_ref, face_ref, plain_ref, packed_ref, tables_ref, column_ref, record_ref, scalar_ref = outputs
    for copy in fetch(list(zip(operands, local)), sems):
        copy.wait()
    own, depth, width = sol_in.shape
    rows = conduct_ref.shape[1]
    cells, nnz = off_ref.shape

    for phase in range(diff_ref.shape[0]):
        scalar_ref[0, phase] = jnp.full((8, 128), diff_ref[phase])
        scalar_ref[1, phase] = jnp.full((8, 128), upt_ref[phase])
    line = lax.broadcasted_iota(jnp.int32, record_ref.shape, 0)
    mine = jnp.zeros(record_ref.shape, jnp.int32)
    for cell in range(cells):
        mine = jnp.where(line == cell, ids_ref[cell], mine)
    mine = place_of(mine, count).astype(jnp.float32)
    scalar_ref[2, 0] = mine
    lane = lax.broadcasted_iota(jnp.int32, record_ref.shape, 1)
    record = jnp.where(lane == PLACE, mine, 0.0)
    for cell in range(cells):
        record = jnp.where((line == cell) & (lane == DIAG), diag_ref[cell], record)
    record_ref[...] = record
    group = nnz // 2
    cols = place_of(cols_ref[...], count).astype(jnp.float32)
    record_ref[:, :group] = off_ref[:, :group]
    record_ref[:, SECOND : SECOND + group] = off_ref[:, group:]
    record_ref[:, COLS : COLS + group] = cols[:, :group] + float(BASE) * cols[:, group:]
    record = record_ref[...]
    record_ref[:4] = jnp.concatenate([record[:4, :HALF], record[4:, :HALF]], axis=1)
    slots, capacity = table_ref.shape
    entries = slots * capacity
    table = flat(table_ref[...]).astype(jnp.float32)
    table = jnp.concatenate([table, jnp.zeros((1, 128 - entries), jnp.float32)], axis=1)
    table = jnp.broadcast_to(table, (8, 128))
    tables_ref[...] = table[:, :entries].astype(jnp.int32)
    column_ref[...] = jnp.transpose(table)[:entries].astype(jnp.int32)

    labels = []
    for start in range(0, depth, 8):
        block = jnp.transpose(label_in[:, start : start + 8, :].astype(jnp.float32), (1, 0, 2))
        labels = labels + [block[at] for at in range(8)]
    for k in range(depth // 2):
        packed_ref[k] = pack_labels(labels[2 * k], labels[2 * k + 1], 8)
    top_pairs = [top_ref[1, z : z + 1] for z in range(depth)]
    bottom_pairs = [bottom_ref[1, z : z + 1] for z in range(depth)]
    phases = range(diff_ref.shape[0])
    diffs, uptakes = [diff_ref[phase] for phase in phases], [upt_ref[phase] for phase in phases]
    grid = Grid(diffs, uptakes, labels, top_pairs, bottom_pairs, {}, conduct_ref, uptake_ref)
    blank = jnp.zeros((8, width), jnp.float32)
    for start in range(0, depth, 8):
        block = jnp.transpose(sol_in[:, start : start + 8, :], (1, 0, 2))
        for at in range(8):
            z = start + at
            plain_ref[z] = block[at]
            sol_ref[z, :own] = block[at]
            sol_ref[z, own:] = blank
            sol_ref[z, own : own + 1] = top_ref[0, z : z + 1]
            sol_ref[z, rows - 1 :] = bottom_ref[0, z : z + 1]
            sol_ref[z] = jnp.where(conduct_ref[z] > 0.0, sol_ref[z], 0.0)
    for start in range(0, depth, 8):
        block = jnp.transpose(src_in[:, start : start + 8, :], (1, 0, 2))
        for at in range(8):
            z = start + at
            conduct, value = conduct_ref[z], sol_ref[z]
            near = sum(grid.in_plane(z))
            diagonal = uptake_ref[z] + 2.0 * conduct + 0.5 * near
            flow = conduct * beside(value, grid.lane) + beside(conduct * value, grid.lane)
            applied = (diagonal * value - 0.5 * flow)[:own]
            conduct, value = conduct[:own], value[:own]
            for other in (z - 1, z + 1):
                if 0 <= other < depth:
                    applied = applied + 0.5 * (conduct + conduct_ref[other, :own]) * (value - sol_ref[other, :own])
            left = block[at] - applied
            res_ref[z] = left.astype(jnp.bfloat16)
            if z in (0, depth - 1):
                side = 0 if z == 0 else 3
                face_ref[side] = left
                face_ref[side + 1] = conduct
                face_ref[side + 2] = value


def phase_rows(scalar_ref, kind, width):
    found = []
    for phase in range(scalar_ref.shape[1]):
        row = scalar_ref[kind, phase, 0:1]
        found.append(jnp.concatenate([row] * (width // row.shape[1]), axis=1))
    return found


def weigh_kernel(
    scalar_ref, packed_ref, src_in, even_ref, odd_ref, row_even_ref, row_odd_ref, cor_ref, weight_ref, inner_ref,
    conduct_ref, uptake_ref,
):
    own, depth, width = src_in.shape
    planes, rows = conduct_ref.shape[0:2]
    top_ref, bottom_ref = from_tile(row_even_ref, row_odd_ref)
    labels = []
    for k in range(depth // 2):
        labels = labels + list(unpack_labels(packed_ref[k], own))
    high, low = from_slab(even_ref, odd_ref, LABELS, CORNERS)
    (high_near, high_far), (low_near, low_far) = unpack_labels(high, own), unpack_labels(low, own)
    labels = labels + [high_near, high_far, low_far, low_near]
    high, low = from_slab(even_ref, odd_ref, CORNERS, MESSAGE)
    top_pairs = [top_ref[1, z : z + 1] for z in range(depth)] + [high[0:1], high[1:2], low[1:2], low[0:1]]
    bottom_pairs = [bottom_ref[1, z : z + 1] for z in range(depth)] + [high[2:3], high[3:4], low[3:4], low[2:3]]
    above, below = ends()
    outside = {depth: above, depth + 1: above, depth + 2: below, depth + 3: below}
    diffs, uptakes = phase_rows(scalar_ref, 0, width), phase_rows(scalar_ref, 1, width)
    grid = Grid(diffs, uptakes, labels, top_pairs, bottom_pairs, outside, conduct_ref, uptake_ref)
    blank = jnp.zeros((8, width), jnp.float32)
    outer = dict(zip((depth, planes - 1), from_slab(even_ref, odd_ref, SOURCE, LABELS)))
    for start in (0, 8, planes - 1, depth):
        if start < depth:
            block = jnp.transpose(src_in[:, start : start + 8, :], (1, 0, 2))
            sources = {start + at: block[at] for at in range(8)}
        else:
            sources = {start: outer[start]}
        for z, source in sources.items():
            conduct = conduct_ref[z]
            near = grid.in_plane(z) + (conduct_ref[(z - 1) % planes], conduct_ref[(z + 1) % planes])
            diagonal = uptake_ref[z] + 3.0 * conduct + 0.5 * sum(near[1:], near[0])
            inside = conduct > 0.0
            scale = jnp.where(inside, OMEGA / jnp.where(inside, diagonal, 1.0), 0.0)
            for k, other in enumerate(near):
                weight_ref[k, z] = jnp.where(other > 0.0, 0.5 * scale * (conduct + other), 0.0)
            weight_ref[6, z, :own] = scale[:own] * source
            weight_ref[6, z, own:] = blank
            if z < depth:
                weight_ref[6, z, own : own + 1] = scale[own : own + 1] * top_ref[2, z : z + 1]
                weight_ref[6, z, rows - 1 :] = scale[rows - 1 :] * bottom_ref[2, z : z + 1]
            value, inner = cor_ref[z], slice(8, own - 8)
            beside_all = (
                pltpu.roll(value, 1, 1)[inner],
                pltpu.roll(value, width - 1, 1)[inner],
                pltpu.roll(value, 1, 0)[inner],
                pltpu.roll(value, own - 1, 0)[inner],
                cor_ref[(z - 1) % planes, inner],
                cor_ref[(z + 1) % planes, inner],
            )
            total = (1.0 - OMEGA) * value[inner] + weight_ref[6, z, inner]
            for k, other in enumerate(beside_all):
                total = total + weight_ref[k, z, inner] * other
            inner_ref[z] = total


def rows_of(basis, start, size):
    return basis[:, start : start + size].astype(jnp.float32)


def owners_of(basis):
    tail = rows_of(basis, basis.shape[1] - 128, 128)
    cell = tail[:, 6:7].astype(jnp.int32)
    return cell, [
        (tail[:, 2 * k : 2 * k + 1] + 256.0 * tail[:, 2 * k + 1 : 2 * k + 2]).astype(jnp.int32)
        for k in range(3)
    ]


def restrict_kernel(scalar_ref, column_ref, record_ref, even_ref, odd_ref, face_ref, res_ref, *refs, capacity):
    basis, out_ref = refs
    depth, own, width = res_ref.shape
    entries = column_ref.shape[0]
    pick = column_ref[:, 0:1] == lax.broadcasted_iota(jnp.int32, (entries, own), 1)
    pick = jnp.where(pick, 1.0, 0.0).astype(jnp.bfloat16)
    values = nearest_planes(even_ref, odd_ref)
    packed = from_slab(even_ref, odd_ref, LABELS, CORNERS)
    diffs = phase_rows(scalar_ref, 0, width)
    faces = {}
    for z, side, at in ((0, 0, 1), (depth - 1, 3, 0)):
        label = unpack_labels(packed[at], own)[0]
        beyond = jnp.zeros(label.shape, jnp.float32)
        for phase, diff in enumerate(diffs):
            beyond = jnp.where(label == float(phase), diff, beyond)
        beyond = jnp.where(ends()[at], 0.0, beyond)
        value = jnp.where(ends()[at], 0.0, values[at])
        applied = 0.5 * (face_ref[side + 1] + beyond) * (face_ref[side + 2] - value)
        faces[z] = (face_ref[side] - applied).astype(jnp.bfloat16)
    total = jnp.zeros((entries, width), jnp.float32)
    for z in range(depth):
        plane = faces[z] if z in faces else res_ref[z]
        piece = jnp.dot(pick, plane, preferred_element_type=jnp.float32)
        total = total + piece * rows_of(basis, z * width, width)
    product = jnp.sum(total, axis=1, keepdims=True)
    cell, unused = owners_of(basis)
    copies, lines, lanes = out_ref.shape
    peer = lax.broadcasted_iota(jnp.int32, (entries, 1), 0) // capacity
    target = (peer // 8 * 4 + peer % 4) * lanes + peer % 8 // 4 * HALF + SUMS + cell
    lane = lax.broadcasted_iota(jnp.int32, (entries, lanes), 1)
    rows = []
    for line in range(lines):
        share = jnp.sum(jnp.where(target == line * lanes + lane, product, 0.0), axis=0, keepdims=True)
        rows.append(share + record_ref[line : line + 1] if line < 4 else share)
    block = jnp.concatenate(rows, axis=0)

    def put(copy, carry):
        out_ref[copy] = block
        return carry

    lax.fori_loop(0, copies, put, 0, unroll=8)


def solve(got, tiles):
    extent, lanes = got[0].shape
    turned = jnp.transpose(got[0][...])
    chunks = range(0, extent, lanes)
    owners = 4 * tiles
    line = lax.broadcasted_iota(jnp.int32, (8, lanes), 0)
    lane = lax.broadcasted_iota(jnp.int32, (8, lanes), 1)

    def left(block, by):
        return pltpu.roll(block, lanes - by, 1) if by else block

    rhs = [jnp.zeros((8, lanes), jnp.float32) for at in range(2 * len(chunks))]
    place = [lane + at * lanes for at in range(2 * len(chunks))]
    for t, ref in enumerate(got):
        total = ref[:owners]
        for at in range(owners, extent, owners):
            total = total + ref[at : at + owners]
        block = jnp.transpose(jnp.concatenate([total] * (lanes // owners), axis=0))
        value = jnp.zeros((8, lanes), jnp.float32)
        ident = jnp.zeros((8, lanes), jnp.float32)
        for half in range(2):
            total = block[half * HALF + SUMS : half * HALF + SUMS + 8]
            row = half * HALF + PLACE
            places = jnp.broadcast_to(turned[row : row + 1, t * lanes : (t + 1) * lanes], (8, lanes))
            for i in range(4):
                value = jnp.where(lane // owners == 4 * half + i, left(total, i), value)
                ident = jnp.where(line == 4 * half + i, left(places, i), ident)
        ident = ident.astype(jnp.int32)
        for at in range(0, lanes, 4):
            here, amount = ident[:, at : at + 1], value[:, at : at + 1]
            rhs = [total + jnp.where(here == spot, amount, 0.0) for total, spot in zip(rhs, place)]
    rhs = [jnp.sum(total, axis=0, keepdims=True) for total in rhs]

    values, places, inverse = [], [], []
    for half in range(2):
        for at in chunks:
            block = turned[half * HALF : (half + 1) * HALF, at : at + lanes]
            values.append(block[:COLS])
            packed = block[COLS : COLS + SECOND]
            second = jnp.floor(packed * (1.0 / BASE))
            first = packed - float(BASE) * second
            places.append(jnp.concatenate([first, second], axis=0).astype(jnp.int32) % (2 * extent))
            inverse.append(1.0 / block[DIAG : DIAG + 1])
    state = [total * factor for total, factor in zip(rhs, inverse)]
    for repeat in range(COARSE_SWEEPS - 1):
        sources = [jnp.broadcast_to(part, (COLS, lanes)) for part in state]
        new = []
        for total, factor, value, spot in zip(rhs, inverse, values, places):
            found = jnp.zeros((COLS, lanes), jnp.float32)
            for k, source in enumerate(sources):
                taken = jnp.take_along_axis(source, spot % lanes, axis=1, mode="promise_in_bounds")
                found = jnp.where(spot // lanes == k, taken, found)
            new.append((total - jnp.sum(value * found, axis=0, keepdims=True)) * factor)
        state = new
    return jnp.concatenate(state, axis=1)


def prolong_kernel(scalar_ref, tables_ref, even_ref, odd_ref, plain_ref, *refs, groups):
    got, basis = refs[:groups], refs[groups]
    cor_ref, row_even_ref, row_odd_ref, correction_ref = refs[-4:]
    odd = lax.axis_index("tile") % 2 == 1
    planes, own, width = cor_ref.shape
    depth = plain_ref.shape[0]
    entries = tables_ref.shape[1]
    cells = correction_ref.shape[1]
    count = 2 * got[0].shape[0]
    state = solve(got, lax.axis_size("tile"))
    line = lax.broadcasted_iota(jnp.int32, (cells, 1), 0)
    mine = scalar_ref[2, 0, :, 0:1].astype(jnp.int32)

    def look_up(ident):
        hit = ident == lax.broadcasted_iota(jnp.int32, (ident.shape[0], count), 1)
        return jnp.sum(jnp.where(hit, state, 0.0), axis=1, keepdims=True)

    diagonal = line == lax.broadcasted_iota(jnp.int32, (cells, cells), 1)
    correction_ref[...] = jnp.sum(jnp.where(diagonal, look_up(mine), 0.0), axis=0, keepdims=True)
    near_high, near_low = nearest_planes(even_ref, odd_ref)
    far_high, far_low = from_slab(even_ref, odd_ref, FAR, SOURCE)
    wide = {depth: near_high, depth + 1: far_high, depth + 2: far_low, depth + 3: near_low}
    high, low = from_slab(even_ref, odd_ref, CORNERS, MESSAGE)
    line = TABLE - CORNERS
    table_high, table_low = high[line : line + 1, :entries], low[line : line + 1, :entries]
    tables = (tables_ref[0:1], table_high.astype(jnp.int32), table_low.astype(jnp.int32))
    base = depth * width
    unused, owners = owners_of(basis)
    for group, owner in enumerate(owners):
        pick = tables[group] == lax.broadcasted_iota(jnp.int32, (own, entries), 0)
        pick = jnp.where(pick, 1.0, 0.0).astype(jnp.bfloat16)
        factor = look_up(owner)
        if group == 0:
            places = [(z, z * width) for z in range(depth)]
        else:
            at = depth + 2 * (group - 1)
            places = [(at + k, base + (at + k - depth) * width) for k in range(2)]
        for z, start in places:
            part = (rows_of(basis, start, width) * factor).astype(jnp.bfloat16)
            added = jnp.dot(pick, part, preferred_element_type=jnp.float32)
            value = (plain_ref[z] if z < depth else wide[z]) + added
            cor_ref[z] = value
            first, last = value[:2], value[own - 2 :]
            row_even_ref[z] = jnp.where(odd, first, last)
            row_odd_ref[z] = jnp.where(odd, last, first)


def smooth_kernel(cor_ref, row_even_ref, row_odd_ref, weight_ref, inner_ref, out_hbm, new_ref, mid_ref, out_ref, sems):
    planes, rows, width = mid_ref.shape
    own, depth, unused = out_ref.shape
    top_ref, bottom_ref = from_tile(row_even_ref, row_odd_ref)
    gap = jnp.zeros((rows - own - 4, width), jnp.float32)

    def corrected(z):
        return jnp.concatenate([cor_ref[z], top_ref[z], gap, bottom_ref[z]], axis=0)

    def middle(z):
        return jnp.concatenate([mid_ref[z, :8], inner_ref[z], mid_ref[z, own - 8 :]], axis=0)

    def sweep(plane, z, part):
        value = plane(z)
        near = (
            pltpu.roll(value, 1, 1)[part],
            pltpu.roll(value, width - 1, 1)[part],
            pltpu.roll(value, 1, 0)[part],
            pltpu.roll(value, rows - 1, 0)[part],
            plane((z - 1) % planes)[part],
            plane((z + 1) % planes)[part],
        )
        total = (1.0 - OMEGA) * value[part] + weight_ref[6, z, part]
        for k in range(6):
            total = total + weight_ref[k, z, part] * near[k]
        return total

    for z in [planes - 1] + list(range(depth + 1)):
        for part in (slice(0, 8), slice(own - 8, rows)):
            mid_ref[z, part] = sweep(corrected, z, part)
    copies = []
    for start in range(0, depth, 8):
        for z in range(start, start + 8):
            new_ref[z] = sweep(middle, z, slice(0, own))
        out_ref[:, start : start + 8, :] = jnp.transpose(new_ref[start : start + 8], (1, 0, 2))
        part = pl.ds(start, 8)
        copies.append(pltpu.make_async_copy(out_ref.at[:, part], out_hbm.at[:, part], sems.at[start // 8]))
        copies[-1].start()
    for copy in copies:
        copy.wait()


def shards(
    solution,
    source,
    phase_label,
    phase_diffusivity,
    phase_uptake,
    send_tiles,
    support_slot,
    support_len,
    coarse_ids,
    basis_values,
    coarse_diag,
    coarse_off,
    coarse_cols,
):
    f32, i32, bf16 = jnp.float32, jnp.int32, jnp.bfloat16
    rows, depth, width = solution.shape
    voxels = depth * width
    slabs, tiles = lax.axis_size("slab"), lax.axis_size("tile")
    devices = slabs * tiles
    capacity = send_tiles.shape[3]
    cells, support, unused = basis_values.shape
    entries = cells * support
    count = cells * devices
    nnz = coarse_off.shape[1]
    shape = jax.ShapeDtypeStruct
    planes, tall = depth + 4, rows + 8
    block = (rows, depth, width)
    table = send_tiles.reshape(slabs, capacity)
    wide = voxels + 4 * width + 128

    def pinned(*arrays):
        return [pltpu.with_memory_space_constraint(array, pltpu.HBM) for array in arrays]

    outgoing = pl.pallas_call(
        functools.partial(sort_kernel, capacity=capacity, count=count),
        out_shape=shape((entries, wide), bf16),
        in_specs=[HBM] * 4,
        out_specs=HBM,
        scratch_shapes=[
            pltpu.VMEM((1, entries), i32),
            pltpu.SMEM((cells,), i32),
            pltpu.SMEM((cells,), i32),
            pltpu.VMEM((entries, voxels), bf16),
            pltpu.VMEM((entries, wide), bf16),
            pltpu.SemaphoreType.DMA((7,)),
        ],
        compiler_params=params(60),
        name="sort_basis",
    )(
        *pinned(
            support_slot.reshape(1, entries),
            support_len.reshape(cells),
            coarse_ids,
            basis_values.reshape(entries, voxels),
        )
    )
    basis = lax.all_to_all(
        outgoing.reshape(slabs, capacity, wide), "slab", split_axis=0, concat_axis=0, tiled=True
    ).reshape(entries, wide)
    outgoing, solution, phase_label, source, table = lax.optimization_barrier(
        (outgoing, solution, phase_label, source, table)
    )
    message = shape((MESSAGE, width), bf16)
    edge = shape((3, depth, width), f32)
    even, odd, row_even, row_odd = pl.pallas_call(
        border_kernel,
        out_shape=(message, message, edge, edge),
        in_specs=[HBM] * 4,
        out_specs=(VMEM,) * 4,
        scratch_shapes=[
            pltpu.VMEM(block, f32),
            pltpu.VMEM(block, i32),
            pltpu.VMEM(block, f32),
            pltpu.VMEM((slabs, capacity), i32),
            pltpu.SemaphoreType.DMA((4,)),
        ],
        compiler_params=params(8),
        name="border",
    )(*pinned(solution, phase_label, source, table))
    row_even = along_tile(row_even, False)
    row_odd = along_tile(row_odd, True)
    even, odd = pl.pallas_call(
        corner_kernel,
        out_shape=(message, message),
        in_specs=[HBM] * 4,
        out_specs=(VMEM,) * 2,
        scratch_shapes=[pltpu.VMEM(edge.shape, f32)] * 2 + [pltpu.SemaphoreType.DMA((4,))],
        compiler_params=params(8),
        name="corner",
    )(even, odd, row_even, row_odd)
    even = along_slab(even, False)
    odd = along_slab(odd, True)
    first_even, first_odd = row_even, row_odd

    wide_block = pltpu.VMEM((planes, tall, width), f32)
    operands = [
        phase_diffusivity, phase_uptake, coarse_diag, coarse_ids, coarse_off, coarse_cols, table,
        solution, phase_label, source, row_even, row_odd,
    ]
    phases = phase_diffusivity.shape[0]
    residual, face, plain, packed, tables, column, record, scalars = pl.pallas_call(
        functools.partial(residual_kernel, count=count),
        out_shape=(
            shape((depth, rows, width), bf16),
            shape((6, rows, width), f32),
            shape((depth, rows, width), f32),
            shape((depth // 2, 8, width), f32),
            shape((8, entries), i32),
            shape((entries, 8), i32),
            shape((cells, 128), f32),
            shape((3, phases, 8, 128), f32),
        ),
        in_specs=[HBM] * 12,
        out_specs=(VMEM,) * 8,
        scratch_shapes=[pltpu.VMEM((depth, tall, width), f32)] * 3
        + [pltpu.SMEM(array.shape, array.dtype) for array in operands[:4]]
        + [pltpu.VMEM(array.shape, array.dtype) for array in operands[4:]]
        + [pltpu.SemaphoreType.DMA((12,))],
        compiler_params=params(12),
        name="residual",
    )(*pinned(*operands[:10]), *operands[10:])

    groups = max(1, slabs // 8)
    lines = 4 * groups
    payload = pl.pallas_call(
        functools.partial(restrict_kernel, capacity=capacity),
        out_shape=shape((devices, lines, 128), f32),
        in_specs=[VMEM] * 8,
        out_specs=VMEM,
        compiler_params=params(8),
        name="restrict",
    )(scalars, column, record, even, odd, face, residual, basis)
    got = lax.all_to_all(payload, ("slab", "tile"), split_axis=0, concat_axis=0, tiled=True)
    got = [got[:, 4 * t : 4 * t + 4].reshape(4 * devices, 128) for t in range(groups)]

    edge = shape((planes, 2, width), f32)
    corrected, row_even, row_odd, coarse_correction = pl.pallas_call(
        functools.partial(prolong_kernel, groups=groups),
        out_shape=(shape((planes, rows, width), f32), edge, edge, shape((1, cells), f32)),
        in_specs=[VMEM] * (6 + groups),
        out_specs=(VMEM, VMEM, VMEM, VMEM),
        compiler_params=params(12 + count // 128),
        name="prolong",
    )(scalars, tables, even, odd, plain, *got, basis)
    corrected, packed = lax.optimization_barrier((corrected, packed))
    weights, inner = pl.pallas_call(
        weigh_kernel,
        out_shape=(shape((7, planes, tall, width), f32), shape((planes, rows - 16, width), f32)),
        in_specs=[VMEM] * 8,
        out_specs=(VMEM, VMEM),
        scratch_shapes=[wide_block] * 2,
        compiler_params=params(12),
        name="weigh",
    )(scalars, packed, source, even, odd, first_even, first_odd, corrected)
    row_even = along_tile(row_even, False)
    row_odd = along_tile(row_odd, True)
    smooth = pl.pallas_call(
        smooth_kernel,
        out_shape=shape((rows, depth, width), f32),
        in_specs=[VMEM] * 5,
        out_specs=HBM,
        scratch_shapes=[pltpu.VMEM((depth, rows, width), f32), wide_block, pltpu.VMEM(block, f32)]
        + [pltpu.SemaphoreType.DMA((depth // 8,))],
        compiler_params=params(16),
        name="smooth",
    )(corrected, row_even, row_odd, weights, inner)
    return smooth, coarse_correction.reshape(cells)


def solution(mesh):
    placed = (
        P("tile", "slab", None),
        P("tile", "slab", None),
        P("tile", "slab", None),
        P(),
        P(),
        P("slab", "tile", None, None),
        P("slab", "tile", None),
        P("slab", "tile", None),
        P(("slab", "tile")),
        P(("slab", "tile"), None, None),
        P(("slab", "tile")),
        P(("slab", "tile"), None),
        P(("slab", "tile"), None),
    )
    return jax.shard_map(
        shards,
        mesh=mesh,
        in_specs=placed,
        out_specs=(P("tile", "slab", None), P(("slab", "tile"))),
        check_vma=False,
    )
```

```python
import functools

import jax
import jax.numpy as jnp
from jax import lax
from jax.experimental import pallas as pl
from jax.experimental.pallas import tpu as pltpu
from jax.sharding import PartitionSpec as P

COARSE_SWEEPS = 4
SMOOTH_SWEEPS = 2
OMEGA = 0.8

VMEM = pl.BlockSpec(memory_space=pltpu.VMEM)
SMEM = pl.BlockSpec(memory_space=pltpu.SMEM)
HBM = pl.BlockSpec(memory_space=pltpu.HBM)
MIB = 1024 * 1024
HALF, SECOND, COLS, DIAG, PLACE, SUMS = 64, 16, 32, 46, 47, 48
BASE = 4096


def place_of(index, count):
    row = index % 8
    return row // 4 * (count // 2) + index // 8 * 4 + row % 4


def params(mib=16):
    return pltpu.CompilerParams(vmem_limit_bytes=mib * MIB)


def pairs(count, odd):
    shift = 1 if odd else 0
    return [(i, ((i - shift) ^ 1) + shift) if i - shift >= 0 else (i, count - 1) for i in range(count)]


def closed(table, count):
    return [(source, target % count) for source, target in table]


def along_tile(message, odd):
    tiles = lax.axis_size("tile")
    return lax.ppermute(message, "tile", closed(pairs(tiles, odd), tiles))


def along_slab(message, odd):
    slabs, tiles = lax.axis_size("slab"), lax.axis_size("tile")
    table = []
    for source, target in closed(pairs(slabs, odd), slabs):
        inside = abs(source - target) == 1
        for tile in range(tiles):
            to = target * tiles + tile if inside else source * tiles + (tile ^ 1)
            table.append((source * tiles + tile, to))
    return lax.ppermute(message, ("slab", "tile"), table)


class Either:
    def __init__(self, flag, yes, no):
        self.flag, self.yes, self.no = flag, yes, no
        self.shape = yes.shape

    def __getitem__(self, at):
        return jnp.where(self.flag, self.yes[at], self.no[at])


def from_tile(even_ref, odd_ref):
    odd = lax.axis_index("tile") % 2 == 1
    return Either(odd, odd_ref, even_ref), Either(odd, even_ref, odd_ref)


def fetch(pairs_of_refs, sems):
    copies = [
        pltpu.make_async_copy(source, target, sems.at[k])
        for k, (source, target) in enumerate(pairs_of_refs)
    ]
    for copy in copies:
        copy.start()
    return copies


def sort_kernel(slot_hbm, len_hbm, ids_hbm, basis_hbm, *refs, capacity, count):
    out_hbm, slot_ref, len_ref, ids_ref, basis_ref, out_ref, sems = refs
    entries, voxels = basis_ref.shape
    cells = len_ref.shape[0]
    support = entries // cells
    wide = out_ref.shape[1]
    border = (wide - 128 - voxels) // 2
    chunk = voxels // 2
    pieces = [
        (basis_hbm.at[:, pl.ds(k * chunk, chunk)], basis_ref.at[:, pl.ds(k * chunk, chunk)]) for k in range(2)
    ]
    small = [(slot_hbm, slot_ref), (len_hbm, len_ref), (ids_hbm, ids_ref)]
    copies = fetch(small + pieces, sems)
    for copy in copies[:3]:
        copy.wait()
    lane = lax.broadcasted_iota(jnp.int32, (1, entries), 1)
    length = jnp.zeros((1, entries), jnp.int32)
    ident = jnp.zeros((1, entries), jnp.int32)
    for cell in range(cells):
        here = lane // support == cell
        length = jnp.where(here, len_ref[cell], length)
        ident = jnp.where(here, ids_ref[cell], ident)
    ident = place_of(ident, count)
    live = lane % support < length
    slot = jnp.where(live, slot_ref[...], -1)
    row = lax.broadcasted_iota(jnp.int32, (entries, entries), 0)
    above = jnp.where(row >= entries - capacity, row + capacity - entries, row + capacity)
    below = jnp.where(row < capacity, row - capacity + entries, row - capacity)
    hits = [slot == row, slot == above, slot == below]
    picks = [jnp.where(hit, 1.0, 0.0).astype(jnp.bfloat16) for hit in hits]

    def put(block, start):
        out_ref[:, start : start + block.shape[1]] = block.astype(jnp.bfloat16)

    def send(k, start, size):
        part = pl.ds(start, size)
        copy = pltpu.make_async_copy(out_ref.at[:, part], out_hbm.at[:, part], sems.at[len(copies) + k])
        copy.start()
        return copy

    def move(pick, start, size, target):
        block = basis_ref[:, start : start + size]
        put(jnp.dot(pick, block, preferred_element_type=jnp.float32), target)

    extra = lax.broadcasted_iota(jnp.int32, (entries, 128), 1)
    tail = jnp.zeros((entries, 128), jnp.float32)
    for k, hit in enumerate(hits):
        low = jnp.sum(jnp.where(hit, ident % 256, 0).astype(jnp.float32), axis=1, keepdims=True)
        high = jnp.sum(jnp.where(hit, ident // 256, 0).astype(jnp.float32), axis=1, keepdims=True)
        tail = jnp.where(extra == 2 * k, low, jnp.where(extra == 2 * k + 1, high, tail))
    cell = jnp.sum(jnp.where(hits[0], lane // support, 0).astype(jnp.float32), axis=1, keepdims=True)
    put(jnp.where(extra == 2 * len(hits), cell, tail), voxels + 2 * border)
    for k in range(2):
        copies[3 + k].wait()
        for start in range(k * chunk, (k + 1) * chunk, 512):
            move(picks[0], start, 512, start)
        if k == 0:
            sent = send(0, 0, chunk)
            move(picks[1], 0, border, voxels)
    move(picks[2], voxels - border, border, voxels + border)
    send(1, chunk, wide - chunk).wait()
    sent.wait()


LOW, FAR, SOURCE, LABELS, CORNERS, TABLE = 32, 64, 96, 128, 144, 148
MESSAGE = 160


def border_kernel(
    sol_hbm, label_hbm, src_hbm, table_hbm, even_ref, odd_ref, row_even_ref, row_odd_ref,
    sol_ref, label_ref, src_ref, table_ref, sems,
):
    rows, depth, width = sol_ref.shape
    blocks = ((sol_hbm, sol_ref), (label_hbm, label_ref), (src_hbm, src_ref), (table_hbm, table_ref))
    for copy in fetch(blocks, sems):
        copy.wait()
    odd = lax.axis_index("slab") % 2 == 1

    def planes(start):
        parts = [ref[:, start : start + 2, :].astype(jnp.float32) for ref in (sol_ref, label_ref, src_ref, src_ref)]
        block = jnp.transpose(jnp.concatenate(parts, axis=1), (1, 0, 2))
        return [block[k] for k in range(6)]

    near, far, label, label_far, origin, unused = planes(0)
    down = near, far, origin, pack_labels(label, label_far, 16)
    far, near, label_far, label, unused, origin = planes(depth - 2)
    up = near, far, origin, pack_labels(label, label_far, 16)
    slots, capacity = table_ref.shape
    table = flat(table_ref[...]).astype(jnp.float32)
    table = jnp.concatenate([table, jnp.zeros((1, width - table.shape[1]), jnp.float32)], axis=1)
    line = lax.broadcasted_iota(jnp.int32, (16, width), 0) + CORNERS
    table = jnp.where(line == TABLE, table, 0.0)
    for first, second, ref in ((up, down, even_ref), (down, up, odd_ref)):
        near, far, origin, labels = [jnp.where(odd, b, a) for a, b in zip(first, second)]
        high = near.astype(jnp.bfloat16)
        ref[:LOW] = high
        ref[LOW:FAR] = (near - high.astype(jnp.float32)).astype(jnp.bfloat16)
        ref[FAR:SOURCE] = far.astype(jnp.bfloat16)
        ref[SOURCE:LABELS] = origin.astype(jnp.bfloat16)
        ref[LABELS:CORNERS] = labels.astype(jnp.bfloat16)
        ref[CORNERS:] = table.astype(jnp.bfloat16)
    first, last = [
        (sol_ref[near], (label_ref[near] + 3 * label_ref[far]).astype(jnp.float32), src_ref[near])
        for near, far in ((0, 1), (rows - 1, rows - 2))
    ]
    odd = lax.axis_index("tile") % 2 == 1
    for k in range(3):
        row_even_ref[k] = jnp.where(odd, first[k], last[k])
        row_odd_ref[k] = jnp.where(odd, last[k], first[k])


def flat(table):
    return jnp.concatenate([table[at : at + 1] for at in range(table.shape[0])], axis=1)


def pack_labels(near, far, lines):
    pair = near + 3.0 * far
    packed = pair[0:lines]
    for k in range(1, pair.shape[0] // lines):
        packed = packed + float(9**k) * pair[lines * k : lines * (k + 1)]
    return packed


def unpack_labels(packed, rows):
    found = []
    for k in range(rows // packed.shape[0]):
        rest = jnp.floor((packed + 0.5) * (1.0 / 9.0))
        found.append(packed - 9.0 * rest)
        packed = rest
    return part_pair(jnp.concatenate(found, axis=0))


def part_pair(pair):
    far = jnp.floor((pair + 0.5) * (1.0 / 3.0))
    return pair - 3.0 * far, far


def from_slab(even_ref, odd_ref, start, stop):
    swap = lax.axis_index("slab") % 2 == 1
    even, odd = even_ref[start:stop].astype(jnp.float32), odd_ref[start:stop].astype(jnp.float32)
    return jnp.where(swap, odd, even), jnp.where(swap, even, odd)


def nearest_planes(even_ref, odd_ref):
    upper, lower = from_slab(even_ref, odd_ref, 0, LOW), from_slab(even_ref, odd_ref, LOW, FAR)
    return upper[0] + lower[0], upper[1] + lower[1]


def corner_kernel(even_in, odd_in, row_even, row_odd, even_ref, odd_ref, row_even_ref, row_odd_ref, sems):
    moves = [(even_in, even_ref), (odd_in, odd_ref), (row_even, row_even_ref), (row_odd, row_odd_ref)]
    for copy in fetch(moves, sems):
        copy.wait()
    top_ref, bottom_ref = from_tile(row_even_ref, row_odd_ref)
    depth, width = top_ref.shape[1:]
    odd = lax.axis_index("slab") % 2 == 1
    line = lax.broadcasted_iota(jnp.int32, (16, width), 0)
    for ref, upward in ((even_ref, jnp.logical_not(odd)), (odd_ref, odd)):
        block = ref[CORNERS:].astype(jnp.float32)
        for k in range(4):
            edge_ref, low = (top_ref, bottom_ref)[k // 2], k % 2
            high = depth - 1 - low
            pair = jnp.where(upward, edge_ref[1, high : high + 1], edge_ref[1, low : low + 1])
            block = jnp.where(line == k, pair, block)
        ref[CORNERS:] = block.astype(jnp.bfloat16)


def beside(plane, lane):
    rows, width = plane.shape
    left = jnp.where(lane == 0, 0.0, pltpu.roll(plane, 1, 1))
    right = jnp.where(lane == width - 1, 0.0, pltpu.roll(plane, width - 1, 1))
    return left + right + pltpu.roll(plane, 1, 0) + pltpu.roll(plane, rows - 1, 0)


class Grid:
    def __init__(self, diffs, uptakes, labels, top_pairs, bottom_pairs, outside, conduct_ref, uptake_ref):
        self.conduct_ref, self.uptake_ref = conduct_ref, uptake_ref
        self.planes, rows, width = conduct_ref.shape
        own = labels[0].shape[0]
        row = lax.broadcasted_iota(jnp.int32, (rows, width), 0)
        self.lane = lax.broadcasted_iota(jnp.int32, (rows, width), 1)
        tile = lax.axis_index("tile")
        beyond = (row >= own + 2) & (row < rows - 2)
        beyond = beyond | ((row >= own) & (row < own + 4) & (tile == lax.axis_size("tile") - 1))
        beyond = beyond | ((row >= own + 4) & (tile == 0))
        blank = jnp.zeros((8, width), jnp.float32)
        for z, (label, top, bottom) in enumerate(zip(labels, top_pairs, bottom_pairs)):
            conduct_ref[z, :own] = label
            conduct_ref[z, own:] = blank
            near, far = part_pair(top)
            conduct_ref[z, own : own + 1] = near
            conduct_ref[z, own + 1 : own + 2] = far
            near, far = part_pair(bottom)
            conduct_ref[z, rows - 1 :] = near
            conduct_ref[z, rows - 2 : rows - 1] = far
            label = jnp.where(beyond | outside[z] if z in outside else beyond, -1.0, conduct_ref[z])
            conduct = jnp.zeros(label.shape, jnp.float32)
            uptake = jnp.zeros(label.shape, jnp.float32)
            for phase, (diff, upt) in enumerate(zip(diffs, uptakes)):
                conduct = jnp.where(label == float(phase), diff, conduct)
                uptake = jnp.where(label == float(phase), upt, uptake)
            conduct_ref[z] = conduct
            uptake_ref[z] = uptake

    def in_plane(self, plane):
        rows, width = plane.shape
        return (
            jnp.where(self.lane == 0, 0.0, pltpu.roll(plane, 1, 1)),
            jnp.where(self.lane == width - 1, 0.0, pltpu.roll(plane, width - 1, 1)),
            pltpu.roll(plane, 1, 0),
            pltpu.roll(plane, rows - 1, 0),
        )


def ends():
    slab = lax.axis_index("slab")
    return slab == lax.axis_size("slab") - 1, slab == 0


def residual_kernel(*refs, count):
    operands, outputs, scratch = refs[:12], refs[12:21], refs[21:]
    sol_ref, uptake_ref, local, sems = scratch[0], scratch[1], scratch[2:14], scratch[14]
    diff_ref, upt_ref, diag_ref, ids_ref = local[:4]
    off_ref, cols_ref, table_ref, sol_in, label_in, src_in = local[4:10]
    top_ref, bottom_ref = from_tile(*local[10:])
    res_ref, face_ref, plain_ref, conduct_ref, code_ref, tables_ref, column_ref, record_ref, scalar_ref = outputs
    for copy in fetch(list(zip(operands, local)), sems):
        copy.wait()
    own, depth, width = sol_in.shape
    rows = conduct_ref.shape[1]
    cells, nnz = off_ref.shape

    for phase in range(diff_ref.shape[0]):
        scalar_ref[0, phase] = jnp.full((8, 128), diff_ref[phase])
        scalar_ref[1, phase] = jnp.full((8, 128), upt_ref[phase])
    line = lax.broadcasted_iota(jnp.int32, record_ref.shape, 0)
    mine = jnp.zeros(record_ref.shape, jnp.int32)
    for cell in range(cells):
        mine = jnp.where(line == cell, ids_ref[cell], mine)
    mine = place_of(mine, count).astype(jnp.float32)
    scalar_ref[2, 0] = mine
    lane = lax.broadcasted_iota(jnp.int32, record_ref.shape, 1)
    record = jnp.where(lane == PLACE, mine, 0.0)
    for cell in range(cells):
        record = jnp.where((line == cell) & (lane == DIAG), diag_ref[cell], record)
    record_ref[...] = record
    group = nnz // 2
    cols = place_of(cols_ref[...], count).astype(jnp.float32)
    record_ref[:, :group] = off_ref[:, :group]
    record_ref[:, SECOND : SECOND + group] = off_ref[:, group:]
    record_ref[:, COLS : COLS + group] = cols[:, :group] + float(BASE) * cols[:, group:]
    record = record_ref[...]
    record_ref[:4] = jnp.concatenate([record[:4, :HALF], record[4:, :HALF]], axis=1)
    slots, capacity = table_ref.shape
    entries = slots * capacity
    table = flat(table_ref[...]).astype(jnp.float32)
    table = jnp.concatenate([table, jnp.zeros((1, 128 - entries), jnp.float32)], axis=1)
    table = jnp.broadcast_to(table, (8, 128))
    tables_ref[...] = table[:, :entries].astype(jnp.int32)
    column_ref[...] = jnp.transpose(table)[:entries].astype(jnp.int32)

    labels = []
    for start in range(0, depth, 8):
        block = jnp.transpose(label_in[:, start : start + 8, :].astype(jnp.float32), (1, 0, 2))
        labels = labels + [block[at] for at in range(8)]
    top_pairs = [top_ref[1, z : z + 1] for z in range(depth)]
    bottom_pairs = [bottom_ref[1, z : z + 1] for z in range(depth)]
    phases = range(diff_ref.shape[0])
    diffs, uptakes = [diff_ref[phase] for phase in phases], [upt_ref[phase] for phase in phases]
    grid = Grid(diffs, uptakes, labels, top_pairs, bottom_pairs, {}, conduct_ref, uptake_ref)
    gap = jnp.zeros((4, width), jnp.float32)
    for z in range(depth):
        (top, far), (bottom, farther) = part_pair(top_pairs[z]), part_pair(bottom_pairs[z])
        rim = jnp.concatenate([top, far, gap, farther, bottom], axis=0)
        code_ref[z] = jnp.concatenate([labels[z], rim, rim], axis=0).astype(jnp.bfloat16)
    blank = jnp.zeros((8, width), jnp.float32)
    for start in range(0, depth, 8):
        block = jnp.transpose(sol_in[:, start : start + 8, :], (1, 0, 2))
        for at in range(8):
            z = start + at
            plain_ref[z] = block[at]
            sol_ref[z, :own] = block[at]
            sol_ref[z, own:] = blank
            sol_ref[z, own : own + 1] = top_ref[0, z : z + 1]
            sol_ref[z, rows - 1 :] = bottom_ref[0, z : z + 1]
            sol_ref[z] = jnp.where(conduct_ref[z] > 0.0, sol_ref[z], 0.0)
    for start in range(0, depth, 8):
        block = jnp.transpose(src_in[:, start : start + 8, :], (1, 0, 2))
        for at in range(8):
            z = start + at
            conduct, value = conduct_ref[z], sol_ref[z]
            near = sum(grid.in_plane(conduct_ref[z]))
            diagonal = uptake_ref[z] + 2.0 * conduct + 0.5 * near
            flow = conduct * beside(value, grid.lane) + beside(conduct * value, grid.lane)
            applied = (diagonal * value - 0.5 * flow)[:own]
            conduct, value = conduct[:own], value[:own]
            for other in (z - 1, z + 1):
                if 0 <= other < depth:
                    applied = applied + 0.5 * (conduct + conduct_ref[other, :own]) * (value - sol_ref[other, :own])
            left = block[at] - applied
            res_ref[z] = left.astype(jnp.bfloat16)
            if z in (0, depth - 1):
                face_ref[0 if z == 0 else 1] = left


def phase_rows(scalar_ref, kind, width):
    found = []
    for phase in range(scalar_ref.shape[1]):
        row = scalar_ref[kind, phase, 0:1]
        found.append(jnp.concatenate([row] * (width // row.shape[1]), axis=1))
    return found


def weigh_kernel(
    scalar_ref, own_conduct_ref, code_ref, src_in, even_ref, odd_ref, row_even_ref, row_odd_ref, cor_ref,
    weight_ref, inner_ref, done_ref,
    conduct_ref, uptake_ref,
):
    own, depth, width = src_in.shape
    planes, rows = weight_ref.shape[1:3]
    top_ref, bottom_ref = from_tile(row_even_ref, row_odd_ref)
    high, low = from_slab(even_ref, odd_ref, LABELS, CORNERS)
    (high_near, high_far), (low_near, low_far) = unpack_labels(high, own), unpack_labels(low, own)
    labels = [high_near, high_far, low_far, low_near]
    high, low = from_slab(even_ref, odd_ref, CORNERS, MESSAGE)
    top_pairs = [high[0:1], high[1:2], low[1:2], low[0:1]]
    bottom_pairs = [high[2:3], high[3:4], low[3:4], low[2:3]]
    above, below = ends()
    outside = {0: above, 1: above, 2: below, 3: below}
    diffs, uptakes = phase_rows(scalar_ref, 0, width), phase_rows(scalar_ref, 1, width)
    grid = Grid(diffs, uptakes, labels, top_pairs, bottom_pairs, outside, conduct_ref, uptake_ref)

    def conduct_of(z):
        return own_conduct_ref[z] if z < depth else conduct_ref[z - depth]

    def uptake_of(z):
        if z >= depth:
            return uptake_ref[z - depth]
        code = code_ref[z].astype(jnp.float32)[:rows]
        found = jnp.zeros((rows, width), jnp.float32)
        for phase, value in enumerate(uptakes):
            found = jnp.where(code == float(phase), value, found)
        return found

    blank = jnp.zeros((8, width), jnp.float32)
    outer = dict(zip((depth, planes - 1), from_slab(even_ref, odd_ref, SOURCE, LABELS)))
    for start in (0, 8, planes - 1, depth):
        if start < depth:
            block = jnp.transpose(src_in[:, start : start + 8, :], (1, 0, 2))
            sources = {start + at: block[at] for at in range(8)}
        else:
            sources = {start: outer[start]}
        for z, source in sources.items():
            conduct = conduct_of(z)
            near = grid.in_plane(conduct) + (conduct_of((z - 1) % planes), conduct_of((z + 1) % planes))
            diagonal = uptake_of(z) + 3.0 * conduct + 0.5 * sum(near[1:], near[0])
            inside = conduct > 0.0
            scale = jnp.where(inside, OMEGA / jnp.where(inside, diagonal, 1.0), 0.0)
            for k, other in enumerate(near):
                weight_ref[k, z] = jnp.where(other > 0.0, 0.5 * scale * (conduct + other), 0.0)
            weight_ref[6, z, :own] = scale[:own] * source
            weight_ref[6, z, own:] = blank
            if z < depth:
                weight_ref[6, z, own : own + 1] = scale[own : own + 1] * top_ref[2, z : z + 1]
                weight_ref[6, z, rows - 1 :] = scale[rows - 1 :] * bottom_ref[2, z : z + 1]
            inner_ref[z] = inner_sweep(cor_ref, weight_ref, z, slice(0, own))
    for z in range(depth):
        done_ref[z] = inner_sweep(inner_ref, weight_ref, z, slice(8, own - 8))


def inner_sweep(ref, weight_ref, z, part):
    planes, own, width = ref.shape
    value = ref[z]
    near = (
        pltpu.roll(value, 1, 1)[part],
        pltpu.roll(value, width - 1, 1)[part],
        pltpu.roll(value, 1, 0)[part],
        pltpu.roll(value, own - 1, 0)[part],
        ref[(z - 1) % planes, part],
        ref[(z + 1) % planes, part],
    )
    total = (1.0 - OMEGA) * value[part] + weight_ref[6, z, part]
    for k, other in enumerate(near):
        total = total + weight_ref[k, z, part] * other
    return total


def rows_of(basis, start, size):
    return basis[:, start : start + size].astype(jnp.float32)


def owners_of(basis):
    tail = rows_of(basis, basis.shape[1] - 128, 128)
    cell = tail[:, 6:7].astype(jnp.int32)
    return cell, [
        (tail[:, 2 * k : 2 * k + 1] + 256.0 * tail[:, 2 * k + 1 : 2 * k + 2]).astype(jnp.int32)
        for k in range(3)
    ]


def restrict_kernel(scalar_ref, column_ref, record_ref, even_ref, odd_ref, face_ref, conduct_ref, plain_ref, res_ref, *refs, capacity):
    basis, out_ref = refs
    depth, own, width = res_ref.shape
    entries = column_ref.shape[0]
    pick = column_ref[:, 0:1] == lax.broadcasted_iota(jnp.int32, (entries, own), 1)
    pick = jnp.where(pick, 1.0, 0.0).astype(jnp.bfloat16)
    values = nearest_planes(even_ref, odd_ref)
    packed = from_slab(even_ref, odd_ref, LABELS, CORNERS)
    diffs = phase_rows(scalar_ref, 0, width)
    faces = {}
    for z, side, at in ((0, 0, 1), (depth - 1, 1, 0)):
        label = unpack_labels(packed[at], own)[0]
        beyond = jnp.zeros(label.shape, jnp.float32)
        for phase, diff in enumerate(diffs):
            beyond = jnp.where(label == float(phase), diff, beyond)
        beyond = jnp.where(ends()[at], 0.0, beyond)
        value = jnp.where(ends()[at], 0.0, values[at])
        applied = 0.5 * (conduct_ref[z, :own] + beyond) * (plain_ref[z] - value)
        faces[z] = (face_ref[side] - applied).astype(jnp.bfloat16)
    total = jnp.zeros((entries, width), jnp.float32)
    for z in range(depth):
        plane = faces[z] if z in faces else res_ref[z]
        piece = jnp.dot(pick, plane, preferred_element_type=jnp.float32)
        total = total + piece * rows_of(basis, z * width, width)
    product = jnp.sum(total, axis=1, keepdims=True)
    cell, unused = owners_of(basis)
    copies, lines, lanes = out_ref.shape
    peer = lax.broadcasted_iota(jnp.int32, (entries, 1), 0) // capacity
    target = (peer // 8 * 4 + peer % 4) * lanes + peer % 8 // 4 * HALF + SUMS + cell
    lane = lax.broadcasted_iota(jnp.int32, (entries, lanes), 1)
    rows = []
    for line in range(lines):
        share = jnp.sum(jnp.where(target == line * lanes + lane, product, 0.0), axis=0, keepdims=True)
        rows.append(share + record_ref[line : line + 1] if line < 4 else share)
    block = jnp.concatenate(rows, axis=0)

    def put(copy, carry):
        out_ref[copy] = block
        return carry

    lax.fori_loop(0, copies, put, 0, unroll=8)


def solve(got, tiles):
    extent, lanes = got[0].shape
    turned = jnp.transpose(got[0][...])
    chunks = range(0, extent, lanes)
    owners = 4 * tiles
    line = lax.broadcasted_iota(jnp.int32, (8, lanes), 0)
    lane = lax.broadcasted_iota(jnp.int32, (8, lanes), 1)

    def left(block, by):
        return pltpu.roll(block, lanes - by, 1) if by else block

    rhs = [jnp.zeros((8, lanes), jnp.float32) for at in range(2 * len(chunks))]
    place = [lane + at * lanes for at in range(2 * len(chunks))]
    for t, ref in enumerate(got):
        total = ref[:owners]
        for at in range(owners, extent, owners):
            total = total + ref[at : at + owners]
        block = jnp.transpose(jnp.concatenate([total] * (lanes // owners), axis=0))
        value = jnp.zeros((8, lanes), jnp.float32)
        ident = jnp.zeros((8, lanes), jnp.float32)
        for half in range(2):
            total = block[half * HALF + SUMS : half * HALF + SUMS + 8]
            row = half * HALF + PLACE
            places = jnp.broadcast_to(turned[row : row + 1, t * lanes : (t + 1) * lanes], (8, lanes))
            for i in range(4):
                value = jnp.where(lane // owners == 4 * half + i, left(total, i), value)
                ident = jnp.where(line == 4 * half + i, left(places, i), ident)
        ident = ident.astype(jnp.int32)
        for at in range(0, lanes, 4):
            here, amount = ident[:, at : at + 1], value[:, at : at + 1]
            rhs = [total + jnp.where(here == spot, amount, 0.0) for total, spot in zip(rhs, place)]
    rhs = [jnp.sum(total, axis=0, keepdims=True) for total in rhs]

    values, places, inverse = [], [], []
    for half in range(2):
        for at in chunks:
            block = turned[half * HALF : (half + 1) * HALF, at : at + lanes]
            values.append(block[:COLS])
            packed = block[COLS : COLS + SECOND]
            second = jnp.floor(packed * (1.0 / BASE))
            first = packed - float(BASE) * second
            places.append(jnp.concatenate([first, second], axis=0).astype(jnp.int32) % (2 * extent))
            inverse.append(1.0 / block[DIAG : DIAG + 1])
    state = [total * factor for total, factor in zip(rhs, inverse)]
    for repeat in range(COARSE_SWEEPS - 1):
        sources = [jnp.broadcast_to(part, (COLS, lanes)) for part in state]
        new = []
        for total, factor, value, spot in zip(rhs, inverse, values, places):
            found = jnp.zeros((COLS, lanes), jnp.float32)
            for k, source in enumerate(sources):
                taken = jnp.take_along_axis(source, spot % lanes, axis=1, mode="promise_in_bounds")
                found = jnp.where(spot // lanes == k, taken, found)
            new.append((total - jnp.sum(value * found, axis=0, keepdims=True)) * factor)
        state = new
    return jnp.concatenate(state, axis=1)


def prolong_kernel(scalar_ref, tables_ref, even_ref, odd_ref, plain_ref, *refs, groups):
    got, basis = refs[:groups], refs[groups]
    cor_ref, row_even_ref, row_odd_ref, correction_ref = refs[-4:]
    odd = lax.axis_index("tile") % 2 == 1
    planes, own, width = cor_ref.shape
    depth = plain_ref.shape[0]
    entries = tables_ref.shape[1]
    cells = correction_ref.shape[1]
    count = 2 * got[0].shape[0]
    state = solve(got, lax.axis_size("tile"))
    line = lax.broadcasted_iota(jnp.int32, (cells, 1), 0)
    mine = scalar_ref[2, 0, :, 0:1].astype(jnp.int32)

    def look_up(ident):
        hit = ident == lax.broadcasted_iota(jnp.int32, (ident.shape[0], count), 1)
        return jnp.sum(jnp.where(hit, state, 0.0), axis=1, keepdims=True)

    diagonal = line == lax.broadcasted_iota(jnp.int32, (cells, cells), 1)
    correction_ref[...] = jnp.sum(jnp.where(diagonal, look_up(mine), 0.0), axis=0, keepdims=True)
    near_high, near_low = nearest_planes(even_ref, odd_ref)
    far_high, far_low = from_slab(even_ref, odd_ref, FAR, SOURCE)
    wide = {depth: near_high, depth + 1: far_high, depth + 2: far_low, depth + 3: near_low}
    high, low = from_slab(even_ref, odd_ref, CORNERS, MESSAGE)
    line = TABLE - CORNERS
    table_high, table_low = high[line : line + 1, :entries], low[line : line + 1, :entries]
    tables = (tables_ref[0:1], table_high.astype(jnp.int32), table_low.astype(jnp.int32))
    base = depth * width
    unused, owners = owners_of(basis)
    for group, owner in enumerate(owners):
        pick = tables[group] == lax.broadcasted_iota(jnp.int32, (own, entries), 0)
        pick = jnp.where(pick, 1.0, 0.0).astype(jnp.bfloat16)
        factor = look_up(owner)
        if group == 0:
            places = [(z, z * width) for z in range(depth)]
        else:
            at = depth + 2 * (group - 1)
            places = [(at + k, base + (at + k - depth) * width) for k in range(2)]
        for z, start in places:
            part = (rows_of(basis, start, width) * factor).astype(jnp.bfloat16)
            added = jnp.dot(pick, part, preferred_element_type=jnp.float32)
            value = (plain_ref[z] if z < depth else wide[z]) + added
            cor_ref[z] = value
            first, last = value[:2], value[own - 2 :]
            row_even_ref[z] = jnp.where(odd, first, last)
            row_odd_ref[z] = jnp.where(odd, last, first)


def smooth_kernel(cor_ref, row_even_ref, row_odd_ref, weight_ref, inner_ref, done_ref, out_hbm, new_ref, mid_ref, out_ref, sems):
    planes, rows, width = mid_ref.shape
    own, depth, unused = out_ref.shape
    top_ref, bottom_ref = from_tile(row_even_ref, row_odd_ref)
    gap = jnp.zeros((rows - own - 4, width), jnp.float32)

    def corrected(z):
        return jnp.concatenate([cor_ref[z], top_ref[z], gap, bottom_ref[z]], axis=0)

    def middle(z):
        return jnp.concatenate([mid_ref[z, :8], inner_ref[z, 8 : own - 8], mid_ref[z, own - 8 :]], axis=0)

    def sweep(plane, z, part):
        value = plane(z)
        near = (
            pltpu.roll(value, 1, 1)[part],
            pltpu.roll(value, width - 1, 1)[part],
            pltpu.roll(value, 1, 0)[part],
            pltpu.roll(value, rows - 1, 0)[part],
            plane((z - 1) % planes)[part],
            plane((z + 1) % planes)[part],
        )
        total = (1.0 - OMEGA) * value[part] + weight_ref[6, z, part]
        for k in range(6):
            total = total + weight_ref[k, z, part] * near[k]
        return total

    for z in [planes - 1] + list(range(depth + 1)):
        for part in (slice(0, 8), slice(own - 8, rows)):
            mid_ref[z, part] = sweep(corrected, z, part)
    copies = []
    for start in range(0, depth, 8):
        for z in range(start, start + 8):
            for part in (slice(0, 8), slice(own - 8, own)):
                new_ref[z, part] = sweep(middle, z, part)
            new_ref[z, 8 : own - 8] = done_ref[z]
        out_ref[:, start : start + 8, :] = jnp.transpose(new_ref[start : start + 8], (1, 0, 2))
        part = pl.ds(start, 8)
        copies.append(pltpu.make_async_copy(out_ref.at[:, part], out_hbm.at[:, part], sems.at[start // 8]))
        copies[-1].start()
    for copy in copies:
        copy.wait()


def shards(
    solution,
    source,
    phase_label,
    phase_diffusivity,
    phase_uptake,
    send_tiles,
    support_slot,
    support_len,
    coarse_ids,
    basis_values,
    coarse_diag,
    coarse_off,
    coarse_cols,
):
    f32, i32, bf16 = jnp.float32, jnp.int32, jnp.bfloat16
    rows, depth, width = solution.shape
    voxels = depth * width
    slabs, tiles = lax.axis_size("slab"), lax.axis_size("tile")
    devices = slabs * tiles
    capacity = send_tiles.shape[3]
    cells, support, unused = basis_values.shape
    entries = cells * support
    count = cells * devices
    nnz = coarse_off.shape[1]
    shape = jax.ShapeDtypeStruct
    planes, tall = depth + 4, rows + 8
    block = (rows, depth, width)
    table = send_tiles.reshape(slabs, capacity)
    wide = voxels + 4 * width + 128

    def pinned(*arrays):
        return [pltpu.with_memory_space_constraint(array, pltpu.HBM) for array in arrays]

    outgoing = pl.pallas_call(
        functools.partial(sort_kernel, capacity=capacity, count=count),
        out_shape=shape((entries, wide), bf16),
        in_specs=[HBM] * 4,
        out_specs=HBM,
        scratch_shapes=[
            pltpu.VMEM((1, entries), i32),
            pltpu.SMEM((cells,), i32),
            pltpu.SMEM((cells,), i32),
            pltpu.VMEM((entries, voxels), bf16),
            pltpu.VMEM((entries, wide), bf16),
            pltpu.SemaphoreType.DMA((7,)),
        ],
        compiler_params=params(60),
        name="sort_basis",
    )(
        *pinned(
            support_slot.reshape(1, entries),
            support_len.reshape(cells),
            coarse_ids,
            basis_values.reshape(entries, voxels),
        )
    )
    basis = lax.all_to_all(
        outgoing.reshape(slabs, capacity, wide), "slab", split_axis=0, concat_axis=0, tiled=True
    ).reshape(entries, wide)
    outgoing, solution, phase_label, source, table = lax.optimization_barrier(
        (outgoing, solution, phase_label, source, table)
    )
    message = shape((MESSAGE, width), bf16)
    edge = shape((3, depth, width), f32)
    even, odd, row_even, row_odd = pl.pallas_call(
        border_kernel,
        out_shape=(message, message, edge, edge),
        in_specs=[HBM] * 4,
        out_specs=(VMEM,) * 4,
        scratch_shapes=[
            pltpu.VMEM(block, f32),
            pltpu.VMEM(block, i32),
            pltpu.VMEM(block, f32),
            pltpu.VMEM((slabs, capacity), i32),
            pltpu.SemaphoreType.DMA((4,)),
        ],
        compiler_params=params(8),
        name="border",
    )(*pinned(solution, phase_label, source, table))
    row_even = along_tile(row_even, False)
    row_odd = along_tile(row_odd, True)
    even, odd = pl.pallas_call(
        corner_kernel,
        out_shape=(message, message),
        in_specs=[HBM] * 4,
        out_specs=(VMEM,) * 2,
        scratch_shapes=[pltpu.VMEM(edge.shape, f32)] * 2 + [pltpu.SemaphoreType.DMA((4,))],
        compiler_params=params(8),
        name="corner",
    )(even, odd, row_even, row_odd)
    even = along_slab(even, False)
    odd = along_slab(odd, True)
    first_even, first_odd = row_even, row_odd

    wide_block = pltpu.VMEM((planes, tall, width), f32)
    operands = [
        phase_diffusivity, phase_uptake, coarse_diag, coarse_ids, coarse_off, coarse_cols, table,
        solution, phase_label, source, row_even, row_odd,
    ]
    phases = phase_diffusivity.shape[0]
    residual, face, plain, conduct, uptake, tables, column, record, scalars = pl.pallas_call(
        functools.partial(residual_kernel, count=count),
        out_shape=(
            shape((depth, rows, width), bf16),
            shape((2, rows, width), f32),
            shape((depth, rows, width), f32),
            shape((depth, tall, width), f32),
            shape((depth, tall + 8, width), bf16),
            shape((8, entries), i32),
            shape((entries, 8), i32),
            shape((cells, 128), f32),
            shape((3, phases, 8, 128), f32),
        ),
        in_specs=[HBM] * 12,
        out_specs=(VMEM,) * 9,
        scratch_shapes=[pltpu.VMEM((depth, tall, width), f32)] * 2
        + [pltpu.SMEM(array.shape, array.dtype) for array in operands[:4]]
        + [pltpu.VMEM(array.shape, array.dtype) for array in operands[4:]]
        + [pltpu.SemaphoreType.DMA((12,))],
        compiler_params=params(12),
        name="residual",
    )(*pinned(*operands[:10]), *operands[10:])

    groups = max(1, slabs // 8)
    lines = 4 * groups
    payload = pl.pallas_call(
        functools.partial(restrict_kernel, capacity=capacity),
        out_shape=shape((devices, lines, 128), f32),
        in_specs=[VMEM] * 10,
        out_specs=VMEM,
        compiler_params=params(8),
        name="restrict",
    )(scalars, column, record, even, odd, face, conduct, plain, residual, basis)
    got = lax.all_to_all(payload, ("slab", "tile"), split_axis=0, concat_axis=0, tiled=True)
    got = [got[:, 4 * t : 4 * t + 4].reshape(4 * devices, 128) for t in range(groups)]

    edge = shape((planes, 2, width), f32)
    corrected, row_even, row_odd, coarse_correction = pl.pallas_call(
        functools.partial(prolong_kernel, groups=groups),
        out_shape=(shape((planes, rows, width), f32), edge, edge, shape((1, cells), f32)),
        in_specs=[VMEM] * (6 + groups),
        out_specs=(VMEM, VMEM, VMEM, VMEM),
        compiler_params=params(12 + count // 128),
        name="prolong",
    )(scalars, tables, even, odd, plain, *got, basis)
    corrected, conduct = lax.optimization_barrier((corrected, conduct))
    weights, inner, done = pl.pallas_call(
        weigh_kernel,
        out_shape=(shape((7, planes, tall, width), f32), shape((planes, rows, width), f32), shape((depth, rows - 16, width), f32)),
        in_specs=[VMEM] * 9,
        out_specs=(VMEM, VMEM, VMEM),
        scratch_shapes=[pltpu.VMEM((4, tall, width), f32)] * 2,
        compiler_params=params(12),
        name="weigh",
    )(scalars, conduct, uptake, source, even, odd, first_even, first_odd, corrected)
    row_even = along_tile(row_even, False)
    row_odd = along_tile(row_odd, True)
    smooth = pl.pallas_call(
        smooth_kernel,
        out_shape=shape((rows, depth, width), f32),
        in_specs=[VMEM] * 6,
        out_specs=HBM,
        scratch_shapes=[pltpu.VMEM((depth, rows, width), f32), wide_block, pltpu.VMEM(block, f32)]
        + [pltpu.SemaphoreType.DMA((depth // 8,))],
        compiler_params=params(16),
        name="smooth",
    )(corrected, row_even, row_odd, weights, inner, done)
    return smooth, coarse_correction.reshape(cells)


def solution(mesh):
    placed = (
        P("tile", "slab", None),
        P("tile", "slab", None),
        P("tile", "slab", None),
        P(),
        P(),
        P("slab", "tile", None, None),
        P("slab", "tile", None),
        P("slab", "tile", None),
        P(("slab", "tile")),
        P(("slab", "tile"), None, None),
        P(("slab", "tile")),
        P(("slab", "tile"), None),
        P(("slab", "tile"), None),
    )
    return jax.shard_map(
        shards,
        mesh=mesh,
        in_specs=placed,
        out_specs=(P("tile", "slab", None), P(("slab", "tile"))),
        check_vma=False,
    )
```
